32 devices in a mesh: replica: 4 (over y, x), fsdp: 8 (over z, core).
Axes of the slice: x: 2, y: 2, z: 4, core: 2. Of those that a mesh axis runs over, the one named last changes fastest.
Arguments:
- tokens: bfloat16 [8192, 2048], P(('replica', 'fsdp')), may hold values from -6 to 6
- cotangent: bfloat16 [8192, 2048], P(('replica', 'fsdp')), may hold values from -6 to 6
- segment_ids: int32 [32, 256], P(('replica', 'fsdp')), may hold values from 0 to 7, never falling along the last dimension, each value on 1 to 128 neighbouring positions
- expert_index: int32 [8192, 8], P(('replica', 'fsdp')), may hold values from 0 to 15, all different within a row; in each aligned block of 256 rows (0 to 255, 256 to 511, ...) at most 144 rows name the same one
- clip_threshold: int32 [16], replicated, may hold values from 2 to 11
- attn_norm_gain: bfloat16 [2048], replicated, may hold values from 0.5 to 1.5
- w_query: bfloat16 [2048, 2048], P('fsdp'), may hold values from -0.125 to 0.125
- w_key: bfloat16 [2048, 2048], P('fsdp'), may hold values from -0.125 to 0.125
- w_value: bfloat16 [2048, 2048], P('fsdp'), may hold values from -0.125 to 0.125
- w_output: bfloat16 [2048, 2048], P('fsdp'), may hold values from -0.5 to 0.5
- query_gain: bfloat16 [128], replicated, may hold values from 0.5 to 1.5
- key_gain: bfloat16 [128], replicated, may hold values from 0.5 to 1.5
- ffn_norm_gain: bfloat16 [2048], replicated, may hold values from 0.5 to 1.5
- router: bfloat16 [2048, 16], P('fsdp'), may hold values from -0.0625 to 0.0625
- expert_in: bfloat16 [16, 2048, 2048], P('fsdp'), may hold values from -0.125 to 0.125
- expert_out: bfloat16 [16, 1024, 2048], P('fsdp'), may hold values from -0.75 to 0.75
Outputs:
- output: bfloat16 [8192, 2048], P(('replica', 'fsdp'))
- input_grad: bfloat16 [8192, 2048], P(('replica', 'fsdp'))
- attn_norm_gain_grad: float32 [2048], replicated
- w_query_grad: float32 [2048, 2048], P('fsdp')
- w_key_grad: float32 [2048, 2048], P('fsdp')
- w_value_grad: float32 [2048, 2048], P('fsdp')
- w_output_grad: float32 [2048, 2048], P('fsdp')
- query_gain_grad: float32 [128], replicated
- key_gain_grad: float32 [128], replicated
- ffn_norm_gain_grad: float32 [2048], replicated
- router_grad: float32 [2048, 16], P('fsdp')
- expert_in_grad: float32 [16, 2048, 2048], P('fsdp', 'replica')
- expert_out_grad: float32 [16, 1024, 2048], P('fsdp', 'replica')
- head_max: float32 [16], replicated
- clipped_query: bfloat16 [2048, 2048], P('fsdp')
- clipped_key: bfloat16 [2048, 2048], P('fsdp')
The draws below stay inside these ranges and needn't reach their ends.
Inputs may be any that keep to these rules, and one draw needn't show every extreme that they name: `segment_ids`: within each row the ids never fall; each id covers 1 to 128 positions, one exactly that many. `expert_index`: each row names 8 different experts; among the 256 rows of one sequence no expert is named more than 144 times, a bound that some block reaches.
All inputs are finite; a program needn't handle non-finite values.
Results may differ from the reference program's by a relative error of at most 0.023.
Values may be sent and summed in bfloat16 or wider, within the bound.
No kernel may reach another device: no remote copies, remote signals or barrier semaphores. Data moves between devices by JAX's collectives and lax.ppermute only.
A program may use at most 320 MiB of HBM per device.

```python
import math
import jax
import jax.numpy as jnp
import numpy as np
from jax import lax

D = 2048
H = 16
HD = 128
FF = 1024
TOPK = 8
EXPERTS = 16
TOK_DEV = 256
DOCS = 8
CAP = 144
SEQS = 32
TOKENS = 8192


def place_ends(array, stream_key, smallest, top_value):
    longest = array.shape.index(max(array.shape))
    spots = []
    for shift in (0, 1):
        where = [jax.random.randint(jax.random.fold_in(stream_key, axis), (), 0, length) for axis, length in enumerate(array.shape)]
        where[longest] = (where[longest] + shift) % array.shape[longest]
        spots.append(tuple(where))
    return array.at[spots[0]].set(smallest).at[spots[1]].set(top_value)


def block_scale(rng, dims, split, smallest, high):
    def one(position, blocks):
        heights = jax.random.uniform(jax.random.fold_in(jax.random.fold_in(rng, 6), position), (blocks,), jnp.float32, smallest / len(split), high / len(split))
        return jnp.repeat(jnp.exp(heights), dims[position] // blocks).reshape((-1,) + (1,) * (len(dims) - position - 1))

    level = one(*split[0])
    for cut in split[1:]:
        level = level * one(*cut)
    return level


def split_up(number_of, total, limit, skew):
    loads = [(1 << 20) // math.isqrt(standing ** skew) + 1 for standing in range(2, number_of + 1)]
    spare, holding = total - limit - (number_of - 1), [1] * (number_of - 1)
    while spare > 0:
        free = [i for i in range(number_of - 1) if holding[i] < limit]
        mass, left = sum([loads[i] for i in free]), spare
        for i in free:
            addition = min(limit - holding[i], max(1, left * loads[i] // mass), spare)
            holding[i] = holding[i] + addition
            spare = spare - addition
    return np.array([limit] + holding)


def ragged(stream_key, amount, total, bound, skew):
    if amount == 2:
        one = jax.random.randint(stream_key, (), max(1, total - bound), min(bound, total - 1) + 1)
        return jnp.stack([one, total - one])
    tallies = jnp.asarray(split_up(amount, total, bound, skew), jnp.int32)
    couples = (amount - 1) // 2
    source_of, taker = tallies[1:1 + 2 * couples:2], tallies[2:2 + 2 * couples:2]
    slack = jnp.minimum(source_of - 1, bound - taker)
    shifted = jax.random.randint(jax.random.fold_in(stream_key, 1), (couples,), 0, 1 << 20) % (slack + 1)
    tallies = tallies.at[1:1 + 2 * couples:2].set(source_of - shifted).at[2:2 + 2 * couples:2].set(taker + shifted)
    return tallies[jax.random.permutation(jax.random.fold_in(stream_key, 2), amount)]


def deal_out(key, own, number, rows, amount, top, reach, slope):
    ranking = jax.random.permutation(key, amount)
    crowded, usual = shares(amount, rows * top, reach, slope, True), shares(amount, rows * top, reach, slope, False)
    places = jnp.arange(amount)

    def named(sizes, offset_by):
        used = int((sizes > 0).sum())
        fixed = max(1, used // 4)
        moved = fixed + (places - fixed + offset_by * (used - fixed)) % max(1, amount - fixed)
        return jnp.zeros((amount,), jnp.int32).at[ranking[jnp.where(places < fixed, places, moved)]].set(jnp.asarray(sizes, jnp.int32))

    sizes = jnp.where(number % 4 == 0, named(crowded, number // 4), named(usual, number - number // 4 - 1))
    mixed = jax.random.permutation(jax.random.fold_in(own, 3), amount)
    donor, taker = mixed[0:amount // 2 * 2:2], mixed[1:amount // 2 * 2:2]
    margin = jnp.minimum(sizes[donor] - 1, reach - sizes[taker]) // 2
    margin = jnp.where((donor == ranking[0]) | (taker == ranking[0]) | (sizes[taker] == 0), 0, jnp.maximum(margin, 0))
    moved = jax.random.randint(jax.random.fold_in(own, 4), (amount // 2,), 0, 1 << 20) % (margin + 1)
    sizes = sizes.at[donor].add(-moved).at[taker].add(moved)
    items = jnp.searchsorted(jnp.cumsum(sizes), jnp.arange(rows * top), side="right").astype(jnp.int32)
    grid = items.reshape(top, rows).T
    grid = grid[jax.random.permutation(jax.random.fold_in(own, 1), rows)]
    offset_by = jax.random.randint(jax.random.fold_in(own, 2), (rows, 1), 0, top)
    return jnp.take_along_axis(grid, (jnp.arange(top)[None, :] + offset_by) % top, axis=1)


def shares(amount, total, bound, slope, full):
    loads = [(1 << 20) // math.isqrt(standing ** slope) + 1 for standing in range(1, amount + 1)]
    largest = bound if full else min(bound, max(-(-total // amount), total * loads[0] // sum(loads)))
    least = 1 if total - largest >= amount - 1 else 0
    counts, surplus = [largest] + [least] * (amount - 1), total - largest - least * (amount - 1)
    while surplus > 0:
        movable = [i for i in range(1, amount) if counts[i] < largest] or [i for i in range(1, amount) if counts[i] < bound]
        mass, left = sum([loads[i] for i in movable]), surplus
        for i in movable:
            more = min(bound - counts[i], max(1, left * loads[i] // mass), surplus)
            counts[i] = counts[i] + more
            surplus = surplus - more
    return np.array(counts)


def scatter_about(stream_key, extent, deviation, limit, cuts=(), kind=jnp.bfloat16):
    loudness = block_scale(stream_key, extent, cuts, -0.22, 0.18) if cuts else 1.0
    values = jax.random.normal(stream_key, extent, jnp.float32) * deviation * loudness
    return jnp.minimum(jnp.maximum(values, -limit), limit).astype(kind)


def setup_inputs(seed: int = 0) -> dict:
    arg_keys = jax.random.split(jax.random.key(seed), 17)
    tokens = scatter_about(arg_keys[0], (TOKENS, D), 1.0, 6.0, ((0, 32),))
    cotangent = scatter_about(arg_keys[1], (TOKENS, D), 1.0, 6.0, ((0, 32),))
    segment_ids = jax.vmap(lambda own: jnp.searchsorted(jnp.cumsum(ragged(own, DOCS, TOK_DEV, TOK_DEV // 2, 2)), jnp.arange(TOK_DEV), side="right"))(jax.random.split(arg_keys[2], SEQS)).reshape((SEQS, TOK_DEV)).astype(jnp.int32)
    expert_index_keys = jax.random.split(jax.random.fold_in(arg_keys[3], 1), TOKENS // TOK_DEV)
    expert_index_turns = jax.random.permutation(jax.random.fold_in(arg_keys[3], 3), TOKENS // TOK_DEV)
    expert_index = jax.vmap(lambda own, number: deal_out(jax.random.fold_in(arg_keys[3], 2), own, number, TOK_DEV, EXPERTS, TOPK, CAP, 1))(expert_index_keys, expert_index_turns).reshape((TOKENS, TOPK))
    clip_threshold = place_ends(jax.random.randint(arg_keys[4], (H,), 2, 12), jax.random.fold_in(arg_keys[4], 1), 2, 11).astype(jnp.int32)
    attn_norm_gain = jnp.clip(1.0 + 0.1 * jax.random.normal(arg_keys[5], (D,), jnp.float32), 0.5, 1.5).astype(jnp.bfloat16)
    w_query = scatter_about(arg_keys[6], (D, D), D ** -0.5, 0.125, ((0, 8),))
    w_key = scatter_about(arg_keys[7], (D, D), D ** -0.5, 0.125, ((0, 8),))
    w_value = scatter_about(arg_keys[8], (D, D), D ** -0.5, 0.125, ((0, 8),))
    w_output = scatter_about(arg_keys[9], (D, D), (D // 16) ** -0.5, 0.5, ((0, 8),))
    query_gain = jnp.clip(1.0 + 0.1 * jax.random.normal(arg_keys[10], (HD,), jnp.float32), 0.5, 1.5).astype(jnp.bfloat16)
    key_gain = jnp.clip(1.0 + 0.1 * jax.random.normal(arg_keys[11], (HD,), jnp.float32), 0.5, 1.5).astype(jnp.bfloat16)
    ffn_norm_gain = jnp.clip(1.0 + 0.1 * jax.random.normal(arg_keys[12], (D,), jnp.float32), 0.5, 1.5).astype(jnp.bfloat16)
    router = scatter_about(arg_keys[13], (D, EXPERTS), (4 * D) ** -0.5, 0.0625, ((0, 8),))
    expert_in = scatter_about(arg_keys[14], (EXPERTS, D, 2 * FF), D ** -0.5, 0.125, ((0, 8),))
    expert_out = scatter_about(arg_keys[15], (EXPERTS, FF, D), (FF // 16) ** -0.5, 0.75, ((0, 8),))
    return {"tokens": tokens, "cotangent": cotangent, "segment_ids": segment_ids, "expert_index": expert_index, "clip_threshold": clip_threshold, "attn_norm_gain": attn_norm_gain, "w_query": w_query, "w_key": w_key, "w_value": w_value, "w_output": w_output, "query_gain": query_gain, "key_gain": key_gain, "ffn_norm_gain": ffn_norm_gain, "router": router, "expert_in": expert_in, "expert_out": expert_out}


@jax.custom_vjp
def low(v):
    return lax.optimization_barrier(v.astype(jnp.bfloat16)).astype(jnp.float32)

@jax.custom_vjp
def low_back(v):
    return v

def low_keep(v):
    return (low(v), None)

def low_pass(kept, grad):
    return (grad,)

def back_keep(v):
    return (v, None)

def back_low(kept, grad):
    return (low(grad),)
low.defvjp(low_keep, low_pass)
low_back.defvjp(back_keep, back_low)
epsilon = 1e-06
rope_base = 10000.0

def matmul(left, right):
    return jnp.dot(left, right, precision=lax.Precision.HIGHEST)

def rms_norm(values, gain):
    return values * lax.rsqrt(lax.optimization_barrier(jnp.mean(values * values, axis=-1, keepdims=True)) + epsilon) * gain

def rope_tables(length, width):
    places = jnp.arange(length, dtype=jnp.float32)
    rates = rope_base ** (-jnp.arange(width // 2, dtype=jnp.float32) * 2.0 / width)
    angle = places[:, None] * rates[None, :]
    return (jnp.cos(angle)[:, None, :], jnp.sin(angle)[:, None, :])

def rotate(values, cosine, sine):
    half = values.shape[-1] // 2
    first = values[..., :half]
    second = values[..., half:]
    return jnp.concatenate([first * cosine - second * sine, second * cosine + first * sine], axis=-1)

def reference(tokens, cotangent, segment_ids, expert_index, clip_threshold, attn_norm_gain, w_query, w_key, w_value, w_output, query_gain, key_gain, ffn_norm_gain, router, expert_in, expert_out):
    blocks = TOKENS // TOK_DEV
    scale = HD ** (-0.5)
    cosine, sine = rope_tables(TOK_DEV, HD)
    same_doc = segment_ids[:, :, None] == segment_ids[:, None, :]
    flat_expert = expert_index.reshape(blocks, TOK_DEV * TOPK)
    expert_ids = jnp.arange(EXPERTS, dtype=jnp.int32)
    hot = (flat_expert[:, :, None] == expert_ids[None, None, :]).astype(jnp.int32)
    rank = lax.optimization_barrier(jnp.sum((jnp.cumsum(hot, axis=1) - 1) * hot, axis=2)).astype(jnp.int32)
    slot_row = (jnp.arange(blocks, dtype=jnp.int32)[:, None] * CAP + rank).astype(jnp.int32)
    assign_id = jnp.arange(TOKENS * TOPK, dtype=jnp.int32).reshape(blocks, TOK_DEV * TOPK)
    slot_token = jnp.full((EXPERTS, blocks * CAP), TOKENS, jnp.int32).at[flat_expert, slot_row].set((assign_id // TOPK).astype(jnp.int32))
    slot_assign = jnp.full((EXPERTS, blocks * CAP), TOKENS * TOPK, jnp.int32).at[flat_expert, slot_row].set(assign_id)

    def attend(item):
        query, key, value, allowed = item
        scores = low_back(jnp.einsum('shd,thd->hst', query, key, precision=lax.Precision.HIGHEST) * scale)
        masked = jnp.where(allowed[None], scores, -jnp.inf)
        peak = lax.optimization_barrier(jnp.max(masked, axis=-1, keepdims=True))
        log_total = peak + jnp.log(lax.optimization_barrier(jnp.sum(jnp.exp(masked - peak), axis=-1, keepdims=True)))
        weights = low(jnp.exp(masked - log_total))
        mixed = jnp.einsum('hst,thd->shd', weights, value, precision=lax.Precision.HIGHEST)
        return (mixed, lax.optimization_barrier(jnp.max(peak[:, :, 0], axis=1)))

    def forward(params, inputs):
        attn_gain, query_w, key_w, value_w, output_w, gain_query, gain_key, ffn_gain, router_w, weight_in_all, weight_out_all = params
        normed = low(rms_norm(inputs, attn_gain))
        query = low_back(matmul(normed, query_w)).reshape(blocks, TOK_DEV, H, HD)
        key = low_back(matmul(normed, key_w)).reshape(blocks, TOK_DEV, H, HD)
        value = low_back(low(matmul(normed, value_w))).reshape(blocks, TOK_DEV, H, HD)
        query = low(rotate(rms_norm(query, gain_query), cosine, sine))
        key = low(rotate(rms_norm(key, gain_key), cosine, sine))
        mixed, peaks = lax.map(jax.checkpoint(attend), (query, key, value, same_doc))
        mixed = low_back(low(mixed.reshape(TOKENS, D)))
        hidden = inputs + low_back(matmul(mixed, output_w))
        normed_ffn = low(rms_norm(hidden, ffn_gain))
        logits = low_back(matmul(normed_ffn, router_w))
        gates = jax.nn.softmax(jnp.take_along_axis(logits, expert_index, axis=1), axis=1)
        padded_rows = jnp.concatenate([normed_ffn, jnp.zeros((1, D), jnp.float32)], axis=0)
        padded_gates = jnp.concatenate([gates.reshape(-1), jnp.zeros((1,), jnp.float32)], axis=0)

        def expert_step(total, item):
            tokens_of, assigns_of, weight_in, weight_out = item
            rows = low_back(padded_rows[tokens_of])
            projected = low_back(matmul(rows, weight_in))
            active = low(jax.nn.silu(projected[:, :FF]) * projected[:, FF:])
            result = low_back(low(matmul(active, weight_out)))
            return (total.at[tokens_of].add(padded_gates[assigns_of][:, None] * result), None)
        moe, unused = lax.scan(jax.checkpoint(expert_step), jnp.zeros((TOKENS + 1, D), jnp.float32), (slot_token, slot_assign, weight_in_all, weight_out_all))
        return (hidden + moe[:TOKENS], lax.optimization_barrier(jnp.max(peaks, axis=0)))
    params = (attn_norm_gain.astype(jnp.float32), w_query.astype(jnp.float32), w_key.astype(jnp.float32), w_value.astype(jnp.float32), w_output.astype(jnp.float32), query_gain.astype(jnp.float32), key_gain.astype(jnp.float32), ffn_norm_gain.astype(jnp.float32), router.astype(jnp.float32), expert_in.astype(jnp.float32), expert_out.astype(jnp.float32))
    inputs = tokens.astype(jnp.float32)
    output, pullback, head_max = jax.vjp(forward, params, inputs, has_aux=True)
    param_grads, input_grad = pullback(cotangent.astype(jnp.float32))
    threshold = clip_threshold.astype(jnp.float32)
    factor = threshold / jnp.maximum(head_max, threshold)
    column_scale = jnp.repeat(jnp.sqrt(factor), HD)
    clipped_query = (params[1] * column_scale[None, :]).astype(jnp.bfloat16)
    clipped_key = (params[2] * column_scale[None, :]).astype(jnp.bfloat16)
    return (output.astype(jnp.bfloat16), input_grad.astype(jnp.bfloat16), param_grads[0], param_grads[1], param_grads[2], param_grads[3], param_grads[4], param_grads[5], param_grads[6], param_grads[7], param_grads[8], param_grads[9], param_grads[10], head_max, clipped_query, clipped_key)
```

```python
import jax
import jax.numpy as jnp
from jax import lax
from jax.sharding import PartitionSpec as P

HD = 128
EXPERTS = 16
CAP = 144

epsilon = 1e-06
rope_base = 10000.0
BF = jnp.bfloat16
F32 = jnp.float32


def rms_norm(values, gain):
    return values * lax.rsqrt(jnp.mean(values * values, axis=-1, keepdims=True) + epsilon) * gain


def rope_tables(length, width):
    places = jnp.arange(length, dtype=F32)
    rates = rope_base ** (-jnp.arange(width // 2, dtype=F32) * 2.0 / width)
    angle = places[:, None] * rates[None, :]
    return jnp.cos(angle), jnp.sin(angle)


def rotate(values, cosine, sine):
    half = values.shape[-1] // 2
    first = values[..., :half]
    second = values[..., half:]
    return jnp.concatenate(
        [first * cosine - second * sine, second * cosine + first * sine], axis=-1
    )


def dot(left, right):
    return jnp.dot(left, right, preferred_element_type=F32)


def dot_tn(left, right):
    return lax.dot_general(left, right, (((0,), (0,)), ((), ())), preferred_element_type=F32)


def dot_nt(left, right):
    return lax.dot_general(left, right, (((1,), (1,)), ((), ())), preferred_element_type=F32)


def local(
    tokens,
    cotangent,
    segment_ids,
    expert_index,
    clip_threshold,
    attn_norm_gain,
    w_query,
    w_key,
    w_value,
    w_output,
    query_gain,
    key_gain,
    ffn_norm_gain,
    router,
    expert_in,
    expert_out,
):
    replicas = lax.axis_size("replica")
    groups = lax.axis_size("fsdp")
    me_r = lax.axis_index("replica")
    me_f = lax.axis_index("fsdp")
    length, width = tokens.shape
    part = width // replicas
    heads = part // HD
    ff = expert_out.shape[1]
    local_experts = expert_in.shape[0]
    scale = HD ** (-0.5)
    attn_gain = attn_norm_gain.astype(F32)
    ffn_gain = ffn_norm_gain.astype(F32)
    gain_query = query_gain.astype(F32)
    gain_key = key_gain.astype(F32)

    def swap(value, k):
        return lax.ppermute(value, "replica", [(r, r ^ k) for r in range(replicas)])

    def columns(value, k, axis=1):
        return lax.dynamic_slice_in_dim(value, (me_r ^ k) * part, part, axis)

    def spread(value):
        return [value] + [swap(value, k) for k in range(1, replicas)]

    def trade_columns(value):
        return [columns(value, 0)] + [swap(columns(value, k), k) for k in range(1, replicas)]

    def join_columns(blocks):
        out = jnp.zeros((blocks[0].shape[0], part * replicas), blocks[0].dtype)
        for k, block in enumerate(blocks):
            out = lax.dynamic_update_slice_in_dim(out, block, (me_r ^ k) * part, 1)
        return out

    def gather(value):
        return lax.all_gather(value, "fsdp", axis=0, tiled=True)

    def reduce(value):
        return lax.psum_scatter(value, "fsdp", scatter_dimension=0, tiled=True)

    w_qkv = gather(jnp.concatenate([columns(w, 0) for w in (w_query, w_key, w_value)], axis=1))
    tokens_all = jnp.concatenate(spread(tokens), axis=0)
    segments = jnp.concatenate(spread(segment_ids), axis=0)
    full_index = gather(expert_index)
    w_or = gather(jnp.concatenate([w_output, router], axis=1))
    full_output, full_router = w_or[:, :width], w_or[:, width:]
    cot_all = gather(cotangent)

    inputs_all = tokens_all.astype(F32)
    normed = rms_norm(inputs_all, attn_gain).astype(BF)
    raw = dot(normed, w_qkv)
    by_head = raw.reshape(replicas, length, 3, heads, HD)
    query_raw = by_head[:, :, 0].transpose(0, 2, 1, 3)
    key_raw = by_head[:, :, 1].transpose(0, 2, 1, 3)
    value = by_head[:, :, 2].transpose(0, 2, 1, 3).astype(BF)
    cosine, sine = rope_tables(length, HD)

    def head_prep(values, gain):
        return rotate(rms_norm(values, gain), cosine, sine)

    query_rot = head_prep(query_raw, gain_query).astype(BF)
    key_rot = head_prep(key_raw, gain_key).astype(BF)
    allowed = (segments[:, :, None] == segments[:, None, :])[:, None]
    scores = jnp.einsum("nhsd,nhtd->nhst", query_rot, key_rot, preferred_element_type=F32) * scale
    masked = jnp.where(allowed, scores, -jnp.inf)
    peak = jnp.max(masked, axis=-1, keepdims=True)
    log_total = peak + jnp.log(jnp.sum(jnp.exp(masked - peak), axis=-1, keepdims=True))
    probs = jnp.exp(masked - log_total)
    weights = probs.astype(BF)
    mixed_heads = jnp.einsum("nhst,nhtd->nshd", weights, value, preferred_element_type=F32).astype(
        BF
    )
    mixed_heads = mixed_heads.reshape(replicas, length, part)
    my_max = jnp.max(peak, axis=(0, 2, 3))
    mixed = join_columns(
        [mixed_heads[0]] + [swap(mixed_heads[k], k) for k in range(1, replicas)]
    )
    inputs = tokens.astype(F32)
    hidden = inputs + dot(mixed, full_output)
    normed_ffn = rms_norm(hidden, ffn_gain).astype(BF)
    mixed_all = jnp.concatenate(spread(mixed), axis=0)

    nf_all = gather(normed_ffn)
    ids = jnp.arange(EXPERTS, dtype=jnp.int32)
    mask = jnp.any(full_index[:, :, None] == ids, axis=1)
    logits = dot(nf_all, full_router)
    logits = jnp.where(mask, logits, -jnp.inf)
    top = jnp.max(logits, axis=1, keepdims=True)
    powers = jnp.exp(logits - top)
    gates = powers / jnp.sum(powers, axis=1, keepdims=True)
    first = me_f * local_experts
    hot = lax.dynamic_slice_in_dim(mask, first, local_experts, 1).reshape(
        groups, length, local_experts
    )
    own_gates = lax.dynamic_slice_in_dim(gates, first, local_experts, 1).reshape(
        groups, length, local_experts
    )
    order = jnp.arange(length, dtype=jnp.int32)
    before = (order[:, None] < order[None, :]).astype(BF)
    rank = jnp.einsum("nsj,st->ntj", hot.astype(BF), before, preferred_element_type=F32).astype(
        jnp.int32
    )
    slots = jnp.arange(CAP, dtype=jnp.int32)
    nf_seq = nf_all.reshape(groups, length, width)
    cot_seq = cot_all.reshape(groups, length, width)
    moe = jnp.zeros((groups, length, width), F32)
    back = jnp.zeros((groups, length, width), F32)
    gate_grads = []
    in_grads = []
    out_grads = []
    for j in range(local_experts):
        pick = (
            (rank[:, None, :, j] == slots[None, :, None]) & hot[:, None, :, j]
        ).astype(BF)
        gate = jnp.einsum(
            "ncs,ns->nc", pick.astype(F32), own_gates[:, :, j], precision=lax.Precision.HIGHEST
        ).reshape(-1, 1)

        def take(source):
            return jnp.einsum("ncs,nsd->ncd", pick, source, preferred_element_type=F32).astype(
                BF
            ).reshape(groups * CAP, width)

        def put(rows):
            return jnp.einsum(
                "ncs,ncd->nsd",
                pick,
                rows.reshape(groups, CAP, width),
                preferred_element_type=F32,
            )

        rows = take(nf_seq)
        projected = dot(rows, expert_in[j])
        gate_part, up_part = projected[:, :ff], projected[:, ff:]
        sigmoid = jax.nn.sigmoid(gate_part)
        silu = gate_part * sigmoid
        active = silu * up_part
        scaled = (active * gate).astype(BF)
        result = dot(scaled, expert_out[j]).astype(BF)
        moe = moe + put(result)
        cot_rows = take(cot_seq)
        pulled = dot_nt(cot_rows, expert_out[j])
        gate_grad = jnp.sum(active * pulled, axis=1)
        grad_active = pulled * gate
        grad_projected = jnp.concatenate(
            [
                grad_active * up_part * sigmoid * (1.0 + gate_part * (1.0 - sigmoid)),
                grad_active * silu,
            ],
            axis=1,
        ).astype(BF)
        back = back + put(dot_nt(grad_projected, expert_in[j]).astype(BF))
        gate_grads.append(
            jnp.einsum(
                "ncs,nc->ns",
                pick.astype(F32),
                gate_grad.reshape(groups, CAP),
                precision=lax.Precision.HIGHEST,
            )
        )
        in_grads.append(dot_tn(rows, grad_projected).astype(BF))
        out_grads.append(dot_tn(scaled, cot_rows).astype(BF))
    gate_grads = jnp.stack(gate_grads, axis=-1).reshape(groups * length, local_experts)
    sent = gate_grads.astype(BF)
    rest = (gate_grads - sent.astype(F32)).astype(BF)
    blank = jnp.zeros((groups * length, EXPERTS), BF)
    extra = jnp.concatenate(
        [
            lax.dynamic_update_slice_in_dim(blank, sent, first, 1),
            lax.dynamic_update_slice_in_dim(blank, rest, first, 1),
        ],
        axis=1,
    )
    packed = jnp.concatenate([back.reshape(groups * length, width).astype(BF), extra], axis=1)
    summed = reduce(packed).astype(F32)
    output = (hidden + reduce(moe.reshape(groups * length, width).astype(BF)).astype(F32)).astype(
        BF
    )

    grad_gates = summed[:, width : width + EXPERTS] + summed[:, width + EXPERTS :]
    my_gates = lax.dynamic_slice_in_dim(gates, me_f * length, length, 0)
    centered = grad_gates - jnp.sum(my_gates * grad_gates, axis=1, keepdims=True)
    grad_logits = (my_gates * centered).astype(BF)
    router_grad = dot_tn(normed_ffn, grad_logits)
    grad_normed_ffn = summed[:, :width] + dot_nt(grad_logits, full_router)
    grad_out = cotangent.astype(F32)
    norm_value, ffn_back = jax.vjp(rms_norm, hidden, ffn_gain)
    grad_hidden_norm, ffn_gain_grad = ffn_back(grad_normed_ffn)
    grad_hidden = grad_out + grad_hidden_norm
    grad_attn = grad_hidden.astype(BF)
    attn_columns = jnp.concatenate(trade_columns(grad_attn), axis=0)
    output_grad = dot_tn(mixed_all, attn_columns)
    grad_mixed = dot_nt(grad_attn, full_output).astype(BF)
    grad_mixed = jnp.stack(trade_columns(grad_mixed), axis=0)
    grad_mixed = grad_mixed.reshape(replicas, length, heads, HD).transpose(0, 2, 1, 3)
    grad_weights = jnp.einsum("nhsd,nhtd->nhst", grad_mixed, value, preferred_element_type=F32)
    grad_value = jnp.einsum(
        "nhst,nhsd->nthd", weights, grad_mixed, preferred_element_type=F32
    ).astype(BF)
    grad_scores = (
        probs * (grad_weights - jnp.sum(probs * grad_weights, axis=-1, keepdims=True))
    ).astype(BF)
    grad_query_rot = (
        jnp.einsum("nhst,nhtd->nhsd", grad_scores, key_rot, preferred_element_type=F32) * scale
    )
    grad_key_rot = (
        jnp.einsum("nhst,nhsd->nhtd", grad_scores, query_rot, preferred_element_type=F32) * scale
    )
    query_value, query_back = jax.vjp(head_prep, query_raw, gain_query)
    key_value, key_back = jax.vjp(head_prep, key_raw, gain_key)
    grad_query_raw, query_gain_grad = query_back(grad_query_rot)
    grad_key_raw, key_gain_grad = key_back(grad_key_rot)
    rows_all = replicas * length
    grad_qkv = jnp.concatenate(
        [
            grad_query_raw.astype(BF).transpose(0, 2, 1, 3).reshape(rows_all, part),
            grad_key_raw.astype(BF).transpose(0, 2, 1, 3).reshape(rows_all, part),
            grad_value.reshape(rows_all, part),
        ],
        axis=1,
    )
    qkv_grad = dot_tn(normed, grad_qkv)
    part_normed = dot_nt(grad_qkv, w_qkv).astype(BF).reshape(replicas, length, width)
    grad_normed = part_normed[0].astype(F32)
    for k in range(1, replicas):
        grad_normed = grad_normed + swap(part_normed[k], k).astype(F32)
    attn_value, attn_back = jax.vjp(rms_norm, inputs, attn_gain)
    grad_inputs_norm, attn_gain_grad = attn_back(grad_normed)
    input_grad = (grad_hidden + grad_inputs_norm).astype(BF)

    share_o = reduce(jnp.concatenate([output_grad, router_grad], axis=1).astype(BF))
    share_qkv = reduce(qkv_grad.astype(BF))
    blocks_o = spread(share_o)
    total_output = join_columns([b[:, :part].astype(F32) for b in blocks_o])
    total_router = sum(b[:, part:].astype(F32) for b in blocks_o)
    blocks_qkv = spread(share_qkv)
    total_query, total_key, total_value = (
        join_columns([b[:, i * part : (i + 1) * part].astype(F32) for b in blocks_qkv])
        for i in range(3)
    )

    def replica_sum(value, flip):
        bits = replicas.bit_length() - 1
        value = value.reshape((2,) * bits + (-1, value.shape[-1]))
        for step in range(bits):
            bit = bits - 1 - step if flip else step
            axis = bits - 1 - bit
            mine = (me_r >> bit) & 1
            keep = lax.dynamic_slice_in_dim(value, mine, 1, axis)
            send = lax.dynamic_slice_in_dim(value, 1 - mine, 1, axis)
            value = keep.astype(F32) + swap(send, 1 << bit).astype(F32)
            if step < bits - 1:
                value = value.astype(BF)
        return value.reshape(-1, value.shape[-1])

    expert_out_grad = jnp.stack([replica_sum(g, j % 2 == 1) for j, g in enumerate(out_grads)])
    expert_in_grad = jnp.stack([replica_sum(g, j % 2 == 1) for j, g in enumerate(in_grads)])

    top_heads = lax.dynamic_update_slice_in_dim(
        jnp.full((replicas * heads,), -jnp.inf, F32), my_max, me_r * heads, 0
    )
    sums = jnp.concatenate([attn_gain_grad, query_gain_grad, key_gain_grad, ffn_gain_grad])
    small = jnp.concatenate([sums, top_heads])
    n_sums = sums.shape[0]
    is_sum = jnp.arange(small.shape[0]) < n_sums

    def merge(a, b):
        return jnp.where(is_sum, a + b, jnp.maximum(a, b))

    step = 1
    while step < replicas:
        small = merge(small, swap(small, step))
        step *= 2
    step = 1
    while step < groups:
        other = lax.ppermute(small, "fsdp", [(f, f ^ step) for f in range(groups)])
        small = merge(small, other)
        step *= 2
    attn_gain_total = small[:width]
    query_gain_total = small[width : width + HD]
    key_gain_total = small[width + HD : width + 2 * HD]
    ffn_gain_total = small[width + 2 * HD : n_sums]
    head_max = small[n_sums:]
    threshold = clip_threshold.astype(F32)
    factor = threshold / jnp.maximum(head_max, threshold)
    column_scale = jnp.repeat(jnp.sqrt(factor), HD)
    clipped_query = (w_query.astype(F32) * column_scale[None, :]).astype(BF)
    clipped_key = (w_key.astype(F32) * column_scale[None, :]).astype(BF)
    return (
        output,
        input_grad,
        attn_gain_total,
        total_query,
        total_key,
        total_value,
        total_output,
        query_gain_total,
        key_gain_total,
        ffn_gain_total,
        total_router,
        expert_in_grad,
        expert_out_grad,
        head_max,
        clipped_query,
        clipped_key,
    )


def solution(mesh):
    both = ("replica", "fsdp")
    return jax.shard_map(
        local,
        mesh=mesh,
        in_specs=(
            P(both, None),
            P(both, None),
            P(both, None),
            P(both, None),
            P(),
            P(),
            P("fsdp", None),
            P("fsdp", None),
            P("fsdp", None),
            P("fsdp", None),
            P(),
            P(),
            P(),
            P("fsdp", None),
            P("fsdp", None, None),
            P("fsdp", None, None),
        ),
        out_specs=(
            P(both, None),
            P(both, None),
            P(),
            P("fsdp", None),
            P("fsdp", None),
            P("fsdp", None),
            P("fsdp", None),
            P(),
            P(),
            P(),
            P("fsdp", None),
            P("fsdp", "replica", None),
            P("fsdp", "replica", None),
            P(),
            P("fsdp", None),
            P("fsdp", None),
        ),
        check_vma=False,
    )
```

```python
import functools

import jax
import jax.numpy as jnp
from jax import lax
from jax.experimental import pallas as pl
from jax.experimental.pallas import tpu as pltpu
from jax.sharding import PartitionSpec as P

HD = 128
EXPERTS = 16
CAP = 144

epsilon = 1e-06
rope_base = 10000.0
BF = jnp.bfloat16
F32 = jnp.float32


def rms_norm(values, gain):
    return values * lax.rsqrt(jnp.mean(values * values, axis=-1, keepdims=True) + epsilon) * gain


def rope_tables(length, width):
    places = jnp.arange(length, dtype=F32)
    rates = rope_base ** (-jnp.arange(width // 2, dtype=F32) * 2.0 / width)
    angle = places[:, None] * rates[None, :]
    return jnp.cos(angle), jnp.sin(angle)


def rotate(values, cosine, sine):
    half = values.shape[-1] // 2
    first = values[..., :half]
    second = values[..., half:]
    return jnp.concatenate(
        [first * cosine - second * sine, second * cosine + first * sine], axis=-1
    )


def dot(left, right):
    return jnp.dot(left, right, preferred_element_type=F32)


def dot_tn(left, right):
    return lax.dot_general(left, right, (((0,), (0,)), ((), ())), preferred_element_type=F32)


def dot_nt(left, right):
    return lax.dot_general(left, right, (((1,), (1,)), ((), ())), preferred_element_type=F32)


EXTRA = 16


def nothing(*refs):
    pass


def after(value, *others):
    held = pl.BlockSpec(memory_space=pl.ANY)
    return pl.pallas_call(
        nothing,
        in_specs=[held] * (1 + len(others)),
        out_specs=held,
        out_shape=jax.ShapeDtypeStruct(value.shape, value.dtype),
        input_output_aliases={0: 0},
        name="after",
    )(value, *others)


def expert_kernel(tile, wide, unread, who, *refs):
    (nf_a, nf_b, cot_a, cot_b, pick_a, pick_b, spread_a, spread_b) = refs[:8]
    (mask_a, mask_b, router, w_in, w_out) = refs[8:13]
    refs = refs[13 + unread :]
    rows, gp, cot_rows, scaled, moe, back_a, back_b, gates_hi, gates_lo = refs
    j = pl.program_id(0)
    cap = pick_a.shape[2]
    length = nf_a.shape[0]
    ff = w_out.shape[1]
    core, expert = who[3], who[4] + j

    @pl.when(j == 0)
    def _():
        for at, (nf, mask) in enumerate(((nf_a, mask_a), (nf_b, mask_b))):
            seen = mask[0] > 0.0
            logits = jnp.where(seen, dot(nf[...], router[...]), -1e30)
            powers = jnp.where(seen, jnp.exp(logits - jnp.max(logits, axis=1, keepdims=True)), 0.0)
            gates = powers / jnp.sum(powers, axis=1, keepdims=True)
            high = gates.astype(BF)
            gates_hi[at] = high
            gates_lo[at] = (gates - high.astype(F32)).astype(BF)

    pa, pb = pick_a[0, 0], pick_b[0, 0]
    lane = lax.broadcasted_iota(jnp.int32, (cap, router.shape[1]), 1)

    def slot_gates(p, at):
        every = dot(p, gates_hi[at]) + dot(p, gates_lo[at])
        return jnp.sum(jnp.where(lane == expert, every, 0.0), axis=1, keepdims=True)

    gate = jnp.concatenate([slot_gates(pa, 0), slot_gates(pb, 1)], axis=0)
    rows[0, :cap] = dot(pa, nf_a[...]).astype(BF)
    rows[0, cap:] = dot(pb, nf_b[...]).astype(BF)
    cot_rows[0, :cap] = dot(pa, cot_a[...]).astype(BF)
    cot_rows[0, cap:] = dot(pb, cot_b[...]).astype(BF)

    def forward(t, total):
        at = pl.multiple_of(t * tile, tile)
        g = dot(rows[0], w_in[0, :, pl.ds(at, tile)])
        u = dot(rows[0], w_in[0, :, pl.ds(ff + at, tile)])
        pulled = dot_nt(cot_rows[0], w_out[0, pl.ds(at, tile), :])
        sigma = jax.nn.sigmoid(g)
        silu = g * sigma
        active = silu * u
        scaled[0, :, pl.ds(at, tile)] = (active * gate).astype(BF)
        ga = pulled * gate
        gp[0, :, pl.ds(at, tile)] = (ga * u * sigma * (1.0 + g * (1.0 - sigma))).astype(BF)
        gp[0, :, pl.ds(ff + at, tile)] = (ga * silu).astype(BF)
        return total + jnp.sum(active * pulled, axis=1, keepdims=True)

    total = lax.fori_loop(0, ff // tile, forward, jnp.zeros((2 * cap, 1), F32))
    line = lax.broadcasted_iota(jnp.int32, (EXTRA, length), 0)
    place = 2 * (core * pl.num_programs(0) + j)
    for back, p, part in ((back_a, pa, total[:cap]), (back_b, pb, total[cap:])):
        by_token = jnp.sum(p.astype(F32) * part, axis=0, keepdims=True)
        high = by_token.astype(BF).astype(F32)
        new = jnp.where(line == place, high, jnp.where(line == place + 1, by_token - high, 0.0))

        @pl.when(j == 0)
        def _(back=back):
            back[length:, :] = jnp.zeros((EXTRA, back.shape[1]), BF)

        old = back[length:, :length].astype(F32)
        back[length:, :length] = (old + new).astype(BF)
    sa, sb = spread_a[0, 0], spread_b[0, 0]
    moe_a = pl.ds(pl.multiple_of(core * length, length), length)
    moe_b = pl.ds(pl.multiple_of((1 - core) * length, length), length)

    def backward(t, _):
        here = pl.ds(pl.multiple_of(t * wide, wide), wide)
        gr = dot_nt(gp[0], w_in[0, here, :]).astype(BF)
        res = dot(scaled[0], w_out[0, :, here]).astype(BF)
        for out, where, s, value in (
            (back_a, pl.ds(0, length), sa, gr[:cap]),
            (back_b, pl.ds(0, length), sb, gr[cap:]),
            (moe, moe_a, sa, res[:cap]),
            (moe, moe_b, sb, res[cap:]),
        ):
            old = jnp.where(j > 0, out[where, here].astype(F32), 0.0)
            out[where, here] = (dot(s, value) + old).astype(BF)
        return 0

    lax.fori_loop(0, w_in.shape[1] // wide, backward, 0)


def expert_block(k, rounds, who, nf, cot, pick, spread, mask, router, w_in, w_out, kept, first):
    length, width = nf[0].shape
    count, _, two_ff = w_in.shape
    groups = pick.shape[0]
    ff = two_ff // 2
    cap = pick.shape[2]
    lanes = router.shape[1]

    def whole(j, who):
        return (0, 0)

    def seq(i):
        return lambda j, who: (who[i], j, 0, 0)

    in_specs = [pl.BlockSpec((length, width), whole)] * 2
    if len(cot) == 2:
        in_specs += [pl.BlockSpec((length, width), whole)] * 2
    else:
        cot = [cot[0]] * 2
        in_specs += [
            pl.BlockSpec((length, width), lambda j, who, i=i: (who[i], 0)) for i in range(2)
        ]
    in_specs += [pl.BlockSpec((1, 1, cap, length), seq(i)) for i in range(2)]
    in_specs += [pl.BlockSpec((1, 1, length, cap), seq(i)) for i in range(2)]
    in_specs += [
        pl.BlockSpec((1, length, lanes), lambda j, who, i=i: (who[i], 0, 0)) for i in range(2)
    ]
    in_specs += [
        pl.BlockSpec((width, lanes), whole),
        pl.BlockSpec((1, width, two_ff), lambda j, who: (j, 0, 0)),
        pl.BlockSpec((1, ff, width), lambda j, who: (j, 0, 0)),
    ]
    args = [*nf, *cot, pick, pick, spread, spread, mask, mask, router, w_in, w_out]
    total = rounds * 2 * cap
    saved = [(count, total, n) for n in (width, two_ff, width, ff)]
    out_shape = [jax.ShapeDtypeStruct(s, BF) for s in saved]
    out_shape += [jax.ShapeDtypeStruct((groups * length, width), BF)]
    out_shape += [jax.ShapeDtypeStruct((length + EXTRA, width), BF)] * 2
    out_specs = [pl.BlockSpec((1, 2 * cap, s[2]), lambda j, who: (j, k, 0)) for s in saved]
    out_specs += [pl.BlockSpec((2 * length, width), lambda j, who: (who[2], 0))]
    out_specs += [pl.BlockSpec((length + EXTRA, width), whole)] * 2
    aliases = {}
    if kept is not None:
        aliases = {1 + len(args) + i: i for i in range(len(kept))}
        in_specs += [pl.BlockSpec(memory_space=pl.ANY)] * len(kept)
        args += list(kept)
    in_specs += [pl.BlockSpec(memory_space=pl.ANY)] * len(first)
    args += list(first)
    results = pl.pallas_call(
        functools.partial(expert_kernel, min(512, ff), min(1024, width), len(aliases) + len(first)),
        grid_spec=pltpu.PrefetchScalarGridSpec(
            num_scalar_prefetch=1,
            grid=(count,),
            in_specs=in_specs,
            out_specs=out_specs,
            scratch_shapes=[pltpu.VMEM((2, length, lanes), BF)] * 2,
        ),
        out_shape=out_shape,
        input_output_aliases=aliases,
        compiler_params=pltpu.CompilerParams(vmem_limit_bytes=60 * 2**20),
        cost_estimate=pl.CostEstimate(
            flops=count * 2 * cap * width * ff * 12 * 2,
            bytes_accessed=count * 3 * width * ff * 2 + 20 * length * width * 2,
            transcendentals=0,
        ),
        name="experts",
    )(who, *args)
    return results[:5], results[5], results[6]


def out_kernel(replicas, groups, who, *refs):
    pieces = refs[:replicas]
    near, far, tokens, gain = refs[replicas : replicas + 4]
    hidden, normed, mixed = refs[replicas + 4 :]
    part = pieces[0].shape[1]
    depth = near.shape[1] // (groups // 2)
    for q in range(replicas):
        mixed[:, pl.ds(pl.multiple_of((who[0] ^ q) * part, part), part)] = pieces[q][...]
    for q in range(replicas):
        total = jnp.zeros((tokens.shape[0], part), F32)
        for k in range(groups // 2):
            for flip, source in enumerate((near, far)):
                at = ((who[2] ^ flip) * (groups // 2) + k) * depth
                left = mixed[:, pl.ds(pl.multiple_of(at, depth), depth)]
                total += dot(left, source[q, k * depth : (k + 1) * depth])
        here = pl.ds(pl.multiple_of((who[0] ^ q) * part, part), part)
        hidden[:, here] = tokens[:, here].astype(F32) + total
    value = hidden[...]
    scale = lax.rsqrt(jnp.mean(value * value, axis=1, keepdims=True) + epsilon)
    normed[...] = (value * scale * gain[...]).astype(BF)


def out_step(who, pieces, near, far, tokens, gain):
    replicas = len(pieces)
    length, width = tokens.shape
    groups = lax.axis_size("fsdp")
    vmem = pl.BlockSpec(memory_space=pltpu.VMEM)
    return pl.pallas_call(
        functools.partial(out_kernel, replicas, groups),
        in_specs=[pl.BlockSpec(memory_space=pltpu.SMEM)] + [vmem] * (replicas + 4),
        out_specs=[vmem] * 3,
        out_shape=[
            jax.ShapeDtypeStruct((length, width), F32),
            jax.ShapeDtypeStruct((length, width), BF),
            jax.ShapeDtypeStruct((length, width), BF),
        ],
        compiler_params=pltpu.CompilerParams(vmem_limit_bytes=48 * 2**20),
        name="attention_out",
    )(who, *pieces, near, far, tokens, gain)


def back_kernel(replicas, groups, experts, who, *refs):
    rounds = groups // 2
    shares = refs[:rounds]
    hidden, normed, cot, gain, gates, router, near, far = refs[rounds : rounds + 8]
    grad_hidden, gain_grad, router_grad = refs[rounds + 8 : rounds + 11]
    attn = refs[rounds + 11 : rounds + 11 + replicas]
    out = refs[rounds + 11 + replicas :]
    length, width = hidden.shape
    lanes = router.shape[1]
    part = width // replicas
    depth = width // groups
    per_chip = experts // rounds
    line = lax.broadcasted_iota(jnp.int32, (EXTRA, lanes), 0)
    lane = lax.broadcasted_iota(jnp.int32, (EXTRA, lanes), 1)
    summed = jnp.zeros((length, width), F32)
    grad_gates = jnp.zeros((length, lanes), F32)
    for k in range(rounds):
        summed += shares[k][:length].astype(F32)
        chip = who[1] ^ k
        place = (lane == chip * per_chip + line // 2) & (line < 2 * per_chip)
        grad_gates += dot_tn(shares[k][length:, :length], place.astype(BF))
    own = gates[...]
    centered = grad_gates - jnp.sum(own * grad_gates, axis=1, keepdims=True)
    grad_logits = (own * centered).astype(BF)
    router_grad[...] = dot_tn(normed[...], grad_logits).astype(BF)
    grad_normed = summed + dot_nt(grad_logits, router[...])
    value = hidden[...]
    scale = lax.rsqrt(jnp.mean(value * value, axis=1, keepdims=True) + epsilon)
    gain_grad[...] = jnp.sum(grad_normed * value * scale, axis=0, keepdims=True)
    pulled = grad_normed * gain[...]
    inner = jnp.mean(pulled * value, axis=1, keepdims=True)
    total = cot[...].astype(F32) + scale * pulled - value * (scale * scale * scale * inner)
    grad_hidden[...] = total
    for q in range(replicas):
        here = pl.ds(pl.multiple_of((who[0] ^ q) * part, part), part)
        attn[q][...] = grad_hidden[:, here].astype(BF)
    for k in range(rounds):
        for flip, source in enumerate((near, far)):
            block = jnp.zeros((length, depth), F32)
            for q in range(replicas):
                block += dot_nt(attn[q][...], source[q, k * depth : (k + 1) * depth])
            at = ((who[2] ^ flip) * (groups // 2) + k) * depth
            out[0][:, pl.ds(pl.multiple_of(at, depth), depth)] = block.astype(BF)


def back_step(who, shares, hidden, normed, cot, gain, gates, router, near, far, experts):
    replicas = near.shape[0]
    length, width = hidden.shape
    groups = 2 * len(shares)
    vmem = pl.BlockSpec(memory_space=pltpu.VMEM)
    piece = jax.ShapeDtypeStruct((length, width // replicas), BF)
    results = pl.pallas_call(
        functools.partial(back_kernel, replicas, groups, experts),
        in_specs=[pl.BlockSpec(memory_space=pltpu.SMEM)] + [vmem] * (len(shares) + 8),
        out_specs=[vmem] * (4 + replicas),
        out_shape=[
            jax.ShapeDtypeStruct((length, width), F32),
            jax.ShapeDtypeStruct((1, width), F32),
            jax.ShapeDtypeStruct((width, router.shape[1]), BF),
            *[piece] * replicas,
            jax.ShapeDtypeStruct((length, width), BF),
        ],
        compiler_params=pltpu.CompilerParams(vmem_limit_bytes=48 * 2**20),
        name="attention_back",
    )(who, *shares, hidden, normed, cot, gain, gates, router, near, far)
    return results[0], results[1], results[2], results[3 : 3 + replicas], results[3 + replicas]


def turn(value, cosine, sine):
    return value * cosine + pltpu.roll(value, value.shape[1] // 2, 1) * sine


def attend_kernel(heads, normed, weight, seg_row, seg_col, cosine, sine, gains, *outs):
    raw, ready, mixed, totals, tops = outs
    allowed = seg_col[0] == seg_row[0]
    lane = lax.broadcasted_iota(jnp.int32, totals.shape, 1)
    top_lane = lax.broadcasted_iota(jnp.int32, tops.shape[1:], 1)
    part = heads * HD
    totals[...] = jnp.zeros(totals.shape, F32)
    tops[0] = jnp.zeros(tops.shape[1:], F32)
    for i in range(2):
        raw[:, i * part : (i + 1) * part] = dot(normed[...], weight[:, i * part : (i + 1) * part])
    ready[:, 2 * part :] = dot(normed[...], weight[:, 2 * part : 3 * part]).astype(BF)
    for h in range(heads):
        rotated = []
        for i in range(2):
            at = slice(i * part + h * HD, i * part + (h + 1) * HD)
            head = raw[:, at]
            norm = lax.rsqrt(jnp.mean(head * head, axis=1, keepdims=True) + epsilon)
            rotated.append(turn(head * norm * gains[i : i + 1], cosine[...], sine[...]).astype(BF))
            ready[:, at] = rotated[i]
        scores = dot_nt(rotated[0], rotated[1]) * HD**-0.5
        scores = jnp.where(allowed, scores, -1e30)
        peak = jnp.max(scores, axis=1, keepdims=True)
        powers = jnp.exp(scores - peak)
        total = peak + jnp.log(jnp.sum(powers, axis=1, keepdims=True))
        weights = jnp.exp(scores - total).astype(BF)
        here = slice(h * HD, (h + 1) * HD)
        mixed[:, here] = dot(weights, ready[:, 2 * part + h * HD : 2 * part + (h + 1) * HD]).astype(BF)
        totals[...] = jnp.where(lane == h, total, totals[...])
        tops[0] = jnp.where(top_lane == h, jnp.max(peak, axis=0, keepdims=True), tops[0])


def attend(normed, weight, segments, cosine, sine, gains, heads):
    count, length = segments.shape
    rows, width = normed.shape
    part = heads * HD
    one = lambda n: (n, 0)
    fixed = lambda n: (0, 0)
    return pl.pallas_call(
        functools.partial(attend_kernel, heads),
        grid=(count,),
        in_specs=[
            pl.BlockSpec((length, width), one),
            pl.BlockSpec((width, 3 * part), fixed, pipeline_mode=pl.Buffered(1)),
            pl.BlockSpec((1, 1, length), lambda n: (n, 0, 0)),
            pl.BlockSpec((1, length, 1), lambda n: (n, 0, 0)),
            pl.BlockSpec((length, HD), fixed),
            pl.BlockSpec((length, HD), fixed),
            pl.BlockSpec((2, HD), fixed),
        ],
        out_specs=[
            pl.BlockSpec((length, 2 * part), one),
            pl.BlockSpec((length, 3 * part), one),
            pl.BlockSpec((length, part), one),
            pl.BlockSpec((length, 128), one),
            pl.BlockSpec((1, 1, 128), lambda n: (n, 0, 0)),
        ],
        out_shape=[
            jax.ShapeDtypeStruct((rows, 2 * part), F32),
            jax.ShapeDtypeStruct((rows, 3 * part), BF),
            jax.ShapeDtypeStruct((rows, part), BF),
            jax.ShapeDtypeStruct((rows, 128), F32),
            jax.ShapeDtypeStruct((count, 1, 128), F32),
        ],
        compiler_params=pltpu.CompilerParams(vmem_limit_bytes=48 * 2**20),
        cost_estimate=pl.CostEstimate(
            flops=rows * width * 3 * part * 4, bytes_accessed=8 * rows * width, transcendentals=0
        ),
        name="attention",
    )(normed, weight, segments[:, None, :], segments[:, :, None], cosine, sine, gains)


def attend_back_kernel(heads, pull, raw, ready, totals, seg_row, seg_col, cosine, sine, gains, grad, gain_grads):
    allowed = seg_col[0] == seg_row[0]
    lane = lax.broadcasted_iota(jnp.int32, totals.shape, 1)
    part = heads * HD
    sums = [jnp.zeros((1, HD), F32)] * 2
    for h in range(heads):
        at = [slice(i * part + h * HD, i * part + (h + 1) * HD) for i in range(3)]
        query, key, value = (ready[:, a] for a in at)
        pulled = pull[:, h * HD : (h + 1) * HD]
        total = jnp.sum(jnp.where(lane == h, totals[...], 0.0), axis=1, keepdims=True)
        scores = dot_nt(query, key) * HD**-0.5
        probs = jnp.where(allowed, jnp.exp(jnp.where(allowed, scores - total, 0.0)), 0.0)
        grad_weights = dot_nt(pulled, value)
        grad[:, at[2]] = dot_tn(probs.astype(BF), pulled).astype(BF)
        inner = jnp.sum(probs * grad_weights, axis=1, keepdims=True)
        grad_scores = (probs * (grad_weights - inner)).astype(BF)
        both = (dot(grad_scores, key), dot_tn(grad_scores, query))
        for i, g in enumerate(both):
            g = g * HD**-0.5
            back = g * cosine[...] - pltpu.roll(g, HD // 2, 1) * sine[...]
            head = raw[:, at[i]]
            norm = lax.rsqrt(jnp.mean(head * head, axis=1, keepdims=True) + epsilon)
            sums[i] = sums[i] + jnp.sum(back * head * norm, axis=0, keepdims=True)
            scaled = back * gains[i : i + 1]
            mean = jnp.mean(scaled * head, axis=1, keepdims=True)
            grad[:, at[i]] = (norm * scaled - head * (norm * norm * norm * mean)).astype(BF)
    for i in range(2):
        gain_grads[0, i : i + 1] = sums[i]


def attend_back(pull, raw, ready, totals, segments, cosine, sine, gains, heads):
    count, length = segments.shape
    rows = raw.shape[0]
    part = heads * HD
    one = lambda n: (n, 0)
    fixed = lambda n: (0, 0)
    return pl.pallas_call(
        functools.partial(attend_back_kernel, heads),
        grid=(count,),
        in_specs=[
            pl.BlockSpec((length, part), one),
            pl.BlockSpec((length, 2 * part), one),
            pl.BlockSpec((length, 3 * part), one),
            pl.BlockSpec((length, 128), one),
            pl.BlockSpec((1, 1, length), lambda n: (n, 0, 0)),
            pl.BlockSpec((1, length, 1), lambda n: (n, 0, 0)),
            pl.BlockSpec((length, HD), fixed),
            pl.BlockSpec((length, HD), fixed),
            pl.BlockSpec((2, HD), fixed),
        ],
        out_specs=[
            pl.BlockSpec((length, 3 * part), one),
            pl.BlockSpec((1, 2, HD), lambda n: (n, 0, 0)),
        ],
        out_shape=[
            jax.ShapeDtypeStruct((rows, 3 * part), BF),
            jax.ShapeDtypeStruct((count, 2, HD), F32),
        ],
        compiler_params=pltpu.CompilerParams(vmem_limit_bytes=32 * 2**20),
        cost_estimate=pl.CostEstimate(
            flops=0, bytes_accessed=0, transcendentals=0
        ),
        name="attention_grad",
    )(pull, raw, ready, totals, segments[:, None, :], segments[:, :, None], cosine, sine, gains)


def weight_grad_kernel(half, quarters, left, right, *outs):
    j, i = pl.program_id(0), pl.program_id(1)
    block = dot_tn(left[0], right[0]).astype(BF)
    for at, out in enumerate(outs):

        @pl.when((j == at // 2) & ((i >= half) == (at % 2 == 1)))
        def _(out=out):
            out[0] = block


def weight_grads(quarters, left, right, parts):
    count, rows, width = left.shape
    size, n = width // parts, right.shape[2]
    half = parts // 2

    def spot(at):
        def index(j, i, quarters):
            step = j * parts + i - (at // 2 * parts + at % 2 * half)
            return (jnp.clip(step, 0, half - 1), 0, 0)

        return index

    return pl.pallas_call(
        functools.partial(weight_grad_kernel, half),
        grid_spec=pltpu.PrefetchScalarGridSpec(
            num_scalar_prefetch=1,
            grid=(count, parts),
            in_specs=[
                pl.BlockSpec((1, rows, size), lambda j, i, quarters: (j, 0, quarters[j, i])),
                pl.BlockSpec((1, rows, n), lambda j, i, quarters: (j, 0, 0)),
            ],
            out_specs=[pl.BlockSpec((1, size, n), spot(at)) for at in range(2 * count)],
        ),
        out_shape=[jax.ShapeDtypeStruct((half, size, n), BF)] * (2 * count),
        compiler_params=pltpu.CompilerParams(vmem_limit_bytes=56 * 2**20),
        cost_estimate=pl.CostEstimate(flops=0, bytes_accessed=0, transcendentals=0),
        name="weight_grads",
    )(quarters, left, right)


def product_kernel(left, right, out):
    out[...] = dot_tn(left[...], right[...]).astype(BF)


def product(left, right):
    rows, width = left.shape
    n = right.shape[1]
    size = min(width, 256)
    return pl.pallas_call(
        product_kernel,
        grid=(width // size,),
        in_specs=[
            pl.BlockSpec((rows, size), lambda i: (0, i)),
            pl.BlockSpec((rows, n), lambda i: (0, 0)),
        ],
        out_specs=pl.BlockSpec((size, n), lambda i: (i, 0)),
        out_shape=jax.ShapeDtypeStruct((width, n), BF),
        compiler_params=pltpu.CompilerParams(vmem_limit_bytes=32 * 2**20),
        cost_estimate=pl.CostEstimate(flops=0, bytes_accessed=0, transcendentals=0),
        name="product",
    )(left, right)


def spread_kernel(grad, weight, *outs):
    block = dot_nt(grad[...], weight[...]).astype(BF)
    for at, out in enumerate(outs):

        @pl.when(pl.program_id(0) == at)
        def _(out=out):
            out[...] = block


def normed_grads(grad, weight, count):
    rows, n = grad.shape
    width = weight.shape[0]
    length = rows // count
    return pl.pallas_call(
        spread_kernel,
        grid=(count,),
        in_specs=[
            pl.BlockSpec((length, n), lambda i: (i, 0)),
            pl.BlockSpec((width, n), lambda i: (0, 0), pipeline_mode=pl.Buffered(1)),
        ],
        out_specs=[pl.BlockSpec((length, width), lambda i: (0, 0))] * count,
        out_shape=[jax.ShapeDtypeStruct((length, width), BF)] * count,
        compiler_params=pltpu.CompilerParams(vmem_limit_bytes=48 * 2**20),
        cost_estimate=pl.CostEstimate(flops=10**11, bytes_accessed=0, transcendentals=0),
        name="normed_grads",
    )(grad, weight)


def halve_kernel(half, blocks, keep, got, send_out, keep_out):
    block = (keep[0].astype(F32) + got[0].astype(F32)).astype(BF)

    @pl.when(pl.program_id(0) < half)
    def _():
        send_out[0] = block

    @pl.when(pl.program_id(0) >= half)
    def _():
        keep_out[0] = block


def halve(blocks, keep, got):
    count, size, n = keep.shape
    half = count // 2
    here = pl.BlockSpec((1, size, n), lambda i, blocks: (blocks[i], 0, 0))
    return pl.pallas_call(
        functools.partial(halve_kernel, half),
        grid_spec=pltpu.PrefetchScalarGridSpec(
            num_scalar_prefetch=1,
            grid=(count,),
            in_specs=[here, here],
            out_specs=[
                pl.BlockSpec((1, size, n), lambda i, blocks: (jnp.minimum(i, half - 1), 0, 0)),
                pl.BlockSpec((1, size, n), lambda i, blocks: (jnp.maximum(i - half, 0), 0, 0)),
            ],
        ),
        out_shape=[jax.ShapeDtypeStruct((half, size, n), BF)] * 2,
        compiler_params=pltpu.CompilerParams(vmem_limit_bytes=32 * 2**20),
        cost_estimate=pl.CostEstimate(flops=0, bytes_accessed=0, transcendentals=0),
        name="halve",
    )(blocks, keep, got)


def join_kernel(*refs):
    out = refs[-1]
    for j in range((len(refs) - 1) // 2):

        @pl.when(pl.program_id(0) == j)
        def _(j=j):
            out[0] = refs[2 * j][...].astype(F32) + refs[2 * j + 1][...].astype(F32)


def join(pairs):
    size, n = pairs[0][0].shape
    step = min(size, 256)
    count = len(pairs)

    def spot(at):
        def index(j, i):
            k = j * (size // step) + i - at * (size // step)
            return (jnp.clip(k, 0, size // step - 1), 0)

        return index

    return pl.pallas_call(
        join_kernel,
        grid=(count, size // step),
        in_specs=[pl.BlockSpec((step, n), spot(at // 2)) for at in range(2 * count)],
        out_specs=pl.BlockSpec((1, step, n), lambda j, i: (j, i, 0)),
        out_shape=jax.ShapeDtypeStruct((count, size, n), F32),
        compiler_params=pltpu.CompilerParams(vmem_limit_bytes=48 * 2**20),
        name="join",
    )(*[v for pair in pairs for v in pair])


def local(
    tokens,
    cotangent,
    segment_ids,
    expert_index,
    clip_threshold,
    attn_norm_gain,
    w_query,
    w_key,
    w_value,
    w_output,
    query_gain,
    key_gain,
    ffn_norm_gain,
    router,
    expert_in,
    expert_out,
):
    replicas = lax.axis_size("replica")
    groups = lax.axis_size("fsdp")
    me_r = lax.axis_index("replica")
    me_f = lax.axis_index("fsdp")
    core = me_f % 2
    length, width = tokens.shape
    part = width // replicas
    heads = part // HD
    ff = expert_out.shape[1]
    local_experts = expert_in.shape[0]
    scale = HD ** (-0.5)
    attn_gain = attn_norm_gain.astype(F32)
    ffn_gain = ffn_norm_gain.astype(F32)
    gain_query = query_gain.astype(F32)
    gain_key = key_gain.astype(F32)

    def swap(value, k):
        return lax.ppermute(value, "replica", [(r, r ^ k) for r in range(replicas)])

    def columns(value, k, axis=1):
        return lax.dynamic_slice_in_dim(value, (me_r ^ k) * part, part, axis)

    def spread(value):
        return [value] + [swap(value, k) for k in range(1, replicas)]

    def trade_columns(value):
        return [columns(value, 0)] + [swap(columns(value, k), k) for k in range(1, replicas)]

    def join_columns(blocks):
        out = jnp.zeros((blocks[0].shape[0], part * replicas), blocks[0].dtype)
        for k, block in enumerate(blocks):
            out = lax.dynamic_update_slice_in_dim(out, block, (me_r ^ k) * part, 1)
        return out

    def cross(value, k):
        return lax.ppermute(value, "fsdp", [(f, f ^ k) for f in range(groups)])

    def pass_on(up, down, hop):
        chips = groups // 2
        pairs = [(2 * a + i, 2 * a + 2 + i) for a in range(hop - 1, chips - 1) for i in (0, 1)]
        back = [(2 * a + 2 + i, 2 * a + i) for a in range(chips - hop) for i in (0, 1)]
        return lax.ppermute(up, "fsdp", pairs), lax.ppermute(down, "fsdp", back)

    def choose(up, down, k):
        chips = groups // 2
        found = {}
        for a in range(chips):
            b = a ^ k
            found.setdefault((b > a, abs(b - a)), []).append(a)
        picked = None
        for (above, hop), at in found.items():
            source = down[hop] if above else up[hop]
            if picked is None:
                picked = source
            else:
                here = functools.reduce(jnp.logical_or, [me_f // 2 == a for a in at])
                picked = jnp.where(here, source, picked)
        return picked

    def gather(value):
        return lax.all_gather(value, "fsdp", axis=0, tiled=True)

    def reduce(value):
        return lax.psum_scatter(value, "fsdp", scatter_dimension=0, tiled=True)

    bits = replicas.bit_length() - 1

    def next_bit(j, step):
        return 1 << (bits - 1 - step if j % 2 else step)

    def next_halves(traded, j, step):
        keep, got = traded
        left = keep.shape[0]
        place = jnp.arange(left, dtype=jnp.int32)
        here = left // 2 if j % 2 else 1
        mine = (me_r & next_bit(j, step)) != 0
        other = ((place & here) != 0) != mine
        spots = jnp.where(other, jnp.cumsum(other) - 1, left // 2 + jnp.cumsum(~other) - 1)
        return halve(jnp.zeros((left,), jnp.int32).at[spots].set(place), keep, got)

    index_table = expert_index.astype(BF).reshape(w_query.shape[0], -1)
    sent = [columns(w_output, 0), router, index_table]
    sizes = [v.shape[1] for v in sent]
    sent.append(jnp.zeros((w_query.shape[0], -sum(sizes) % 128), BF))
    quarter = gather(jnp.concatenate(sent, axis=1))
    full_router = quarter[:, part : part + EXPERTS]
    full_index = quarter[:, part + EXPERTS : part + EXPERTS + sizes[2]].astype(jnp.int32)
    full_index = full_index.reshape(groups * length, -1)
    ids = jnp.arange(EXPERTS, dtype=jnp.int32)
    mask = jnp.any(full_index[:, :, None] == ids, axis=1).reshape(groups, length, EXPERTS)
    first = me_f * local_experts
    hot = lax.dynamic_slice_in_dim(mask, first, local_experts, 2)
    order = jnp.arange(length, dtype=jnp.int32)
    before = (order[:, None] < order[None, :]).astype(BF)
    rank = jnp.einsum("nsj,st->njt", hot.astype(BF), before, preferred_element_type=F32)
    rank = jnp.where(hot.transpose(0, 2, 1), rank.astype(jnp.int32), -1)
    slots = jnp.arange(CAP, dtype=jnp.int32)
    pick = (rank[:, :, None, :] == slots[:, None]).astype(BF)
    spots = (rank[:, :, :, None] == slots).astype(BF)
    lanes = 128
    mask_wide = jnp.pad(mask.astype(F32), ((0, 0), (0, 0), (0, lanes - EXPERTS)))
    router_wide = jnp.pad(full_router, ((0, 0), (0, lanes - EXPERTS)))
    tables = (pick, spots, mask_wide, router_wide)
    segments = jnp.concatenate(spread(segment_ids), axis=0)
    tokens_all = spread(tokens)
    normed = jnp.concatenate(
        [rms_norm(v.astype(F32), attn_gain).astype(BF) for v in tokens_all], axis=0
    )
    rounds = groups // 2
    where = jnp.stack([me_r, me_f // 2, core]).astype(jnp.int32)
    half = lax.dynamic_slice(quarter, (core * (width // 2), 0), (width // 2, part))
    near = spread(after(half, normed))
    near[1] = after(near[1], *tables)
    normed = after(normed, *near[1:])
    near = jnp.stack(near)
    far = cross(near, 1)
    w_qkv = gather(jnp.concatenate([columns(w, 0) for w in (w_query, w_key, w_value)], axis=1))
    cot_all = gather(cotangent)
    cot_pair = (cotangent, cross(cotangent, 1))

    cosine, sine = rope_tables(length, HD)
    cosine = jnp.concatenate([cosine, cosine], axis=1)
    sine = jnp.concatenate([-sine, sine], axis=1)
    gains = jnp.stack([gain_query, gain_key])
    raw, ready, mixed_heads, totals, tops = attend(normed, w_qkv, segments, cosine, sine, gains, heads
    )
    my_max = jnp.max(tops, axis=(0, 1))[:heads]
    mixed_heads = mixed_heads.reshape(replicas, length, part)
    pieces = [mixed_heads[0]] + [swap(mixed_heads[k], k) for k in range(1, replicas)]
    inputs = tokens.astype(F32)
    hidden, normed_ffn, mixed = out_step(where, pieces, near, far, tokens, ffn_gain[None, :])
    mixed_all = spread(mixed)

    def first_bit(j):
        return 1 << (bits - 1 if j % 2 else 0)

    numbers = jnp.arange(replicas, dtype=jnp.int32)
    quarters = []
    for j in range(local_experts):
        other = ((numbers ^ me_r) & first_bit(j)) != 0
        place = jnp.where(other, jnp.cumsum(other) - 1, replicas // 2 + jnp.cumsum(~other) - 1)
        quarters.append(jnp.zeros((replicas,), jnp.int32).at[place].set(numbers))
    quarters = jnp.stack(quarters)
    kept = None
    shares = []
    added = []
    pending = []
    up, down = [normed_ffn], [normed_ffn]
    for k in range(rounds):
        chip = (me_f // 2) ^ k
        who = jnp.stack([2 * chip + core, 2 * chip + 1 - core, chip, core, first])
        if k + 1 < rounds:
            next_up, next_down = pass_on(up[-1], down[-1], k + 1)
        mine = choose(up, down, k) if k else normed_ffn
        nf = (mine, cross(mine, 1))
        kept, back_a, back_b = expert_block(k, rounds, who, nf, (cot_all,) if k else cot_pair, pick, spots, mask_wide, router_wide, expert_in, expert_out, kept, pending
        )
        if k + 1 < rounds:
            up.append(after(next_up, back_a))
            down.append(after(next_down, back_a))
        else:
            rows, grad_projected, cot_rows, scaled, moe = kept
            out_blocks = weight_grads(quarters, scaled, cot_rows, replicas)
        if k == rounds - 1:
            back_b = after(back_b, *out_blocks, *shares[1:])
        share = (back_a.astype(F32) + cross(back_b, 1).astype(F32)).astype(BF)
        added.append(share)
        if k == rounds - 2:
            pending = [*added[1:], mixed_all[-1]]
        else:
            pending = mixed_all[1:-1] if k == rounds - 3 else []
        shares.append(share if k == 0 else cross(share, 2 * k))
    out_traded = [
        (out_blocks[2 * j + 1], swap(out_blocks[2 * j], first_bit(j))) for j in range(local_experts)
    ]
    in_blocks = weight_grads(quarters, after(rows, share), grad_projected, replicas)
    shares[-1] = after(shares[-1], *in_blocks, *[v[1] for v in out_traded])
    output = (hidden + reduce(after(moe, shares[-1])).astype(F32)).astype(BF)

    my_mask = lax.dynamic_index_in_dim(mask_wide, me_f, 0, keepdims=False) > 0.0
    logits = jnp.where(my_mask, dot(normed_ffn, router_wide), -jnp.inf)
    powers = jnp.exp(logits - jnp.max(logits, axis=1, keepdims=True))
    my_gates = powers / jnp.sum(powers, axis=1, keepdims=True)
    grad_hidden, ffn_gain_grad, router_grad, attn_pieces, grad_mixed = back_step(
        where, shares, hidden, normed_ffn, cotangent, ffn_gain[None, :], my_gates, router_wide, near, far, EXPERTS
    )
    ffn_gain_grad = ffn_gain_grad[0]
    router_grad = router_grad[:, :EXPERTS]
    grad_mixed = jnp.stack(trade_columns(grad_mixed), axis=0)
    sends = [after(in_blocks[2 * j], grad_mixed) for j in range(local_experts)]
    in_traded = [
        (in_blocks[2 * j + 1], swap(v, first_bit(j))) for j, v in enumerate(sends)
    ]
    grad_mixed = after(grad_mixed, *sends)
    grad_qkv, gain_grads = attend_back(grad_mixed.reshape(replicas * length, part), raw, ready, totals, segments, cosine, sine, gains, heads
    )
    query_gain_grad, key_gain_grad = jnp.sum(gain_grads, axis=0)
    qkv_grad = product(normed, grad_qkv)
    w_late = after(w_qkv, qkv_grad, *[v[1] for v in in_traded])
    attn_columns = [attn_pieces[0]] + [
        swap(after(attn_pieces[k], *sends), k) for k in range(1, replicas)
    ]
    in_halves = [next_halves(v, j, 1) for j, v in enumerate(in_traded)]
    in_sends = [after(v, *attn_columns[1:]) for v, _ in in_halves]
    in_done = [(keep, swap(v, next_bit(j, 1))) for j, (v, (_, keep)) in enumerate(zip(in_sends, in_halves))]
    w_late = after(w_late, *in_sends)
    part_normed = normed_grads(grad_qkv, w_late, replicas)
    grad_normed = after(part_normed[0], *[v[1] for v in in_done]).astype(F32)
    for k in range(1, replicas):
        grad_normed = grad_normed + swap(part_normed[k], k).astype(F32)
    attn_value, attn_back = jax.vjp(rms_norm, inputs, attn_gain)
    grad_inputs_norm, attn_gain_grad = attn_back(grad_normed)
    input_grad = (grad_hidden + grad_inputs_norm).astype(BF)

    share_qkv = reduce(qkv_grad)
    attn_columns = jnp.concatenate(attn_columns, axis=0)
    output_grad = dot_tn(jnp.concatenate(mixed_all, axis=0), attn_columns)
    share_qkv = after(share_qkv, output)
    share_o = after(reduce(jnp.concatenate([output_grad.astype(BF), router_grad], axis=1)), share_qkv)
    blocks_o = spread(share_o)
    total_output = join_columns([b[:, :part].astype(F32) for b in blocks_o])
    total_router = sum(b[:, part:].astype(F32) for b in blocks_o)
    blocks_qkv = spread(share_qkv)
    total_query, total_key, total_value = (
        join_columns([b[:, i * part : (i + 1) * part].astype(F32) for b in blocks_qkv])
        for i in range(3)
    )

    out_last = [(keep, after(got, grad_normed)) for keep, got in out_traded]
    out_halves = [next_halves(v, j, 1) for j, v in enumerate(out_last)]
    out_done = [
        (keep, swap(after(v, *blocks_qkv[1:]), next_bit(j, 1)))
        for j, (v, keep) in enumerate(out_halves)
    ]

    def settle(traded):
        pairs = []
        for j, (keep, got) in enumerate(traded):
            for step in range(2, bits):
                send, keep = next_halves((keep, got), j, step)
                got = swap(send, next_bit(j, step))
            pairs.append((keep[0], got[0]))
        return join(pairs)

    expert_in_grad = settle(in_done)
    expert_out_grad = settle(out_done)

    top_heads = lax.dynamic_update_slice_in_dim(
        jnp.full((replicas * heads,), -jnp.inf, F32), my_max, me_r * heads, 0
    )
    sums = jnp.concatenate([attn_gain_grad, query_gain_grad, key_gain_grad, ffn_gain_grad])
    small = jnp.concatenate([sums, top_heads])
    n_sums = sums.shape[0]
    is_sum = jnp.arange(small.shape[0]) < n_sums

    def merge(a, b):
        return jnp.where(is_sum, a + b, jnp.maximum(a, b))

    small = functools.reduce(merge, spread(small))
    small = merge(small, cross(small, 1))
    small = functools.reduce(merge, [small] + [cross(small, 2 * k) for k in range(1, rounds)])
    attn_gain_total = small[:width]
    query_gain_total = small[width : width + HD]
    key_gain_total = small[width + HD : width + 2 * HD]
    ffn_gain_total = small[width + 2 * HD : n_sums]
    head_max = small[n_sums:]
    threshold = clip_threshold.astype(F32)
    factor = threshold / jnp.maximum(head_max, threshold)
    column_scale = jnp.repeat(jnp.sqrt(factor), HD)
    clipped_query = (w_query.astype(F32) * column_scale[None, :]).astype(BF)
    clipped_key = (w_key.astype(F32) * column_scale[None, :]).astype(BF)
    return (
        output,
        input_grad,
        attn_gain_total,
        total_query,
        total_key,
        total_value,
        total_output,
        query_gain_total,
        key_gain_total,
        ffn_gain_total,
        total_router,
        expert_in_grad,
        expert_out_grad,
        head_max,
        clipped_query,
        clipped_key,
    )


def solution(mesh):
    both = ("replica", "fsdp")
    return jax.shard_map(
        local,
        mesh=mesh,
        in_specs=(
            P(both, None),
            P(both, None),
            P(both, None),
            P(both, None),
            P(),
            P(),
            P("fsdp", None),
            P("fsdp", None),
            P("fsdp", None),
            P("fsdp", None),
            P(),
            P(),
            P(),
            P("fsdp", None),
            P("fsdp", None, None),
            P("fsdp", None, None),
        ),
        out_specs=(
            P(both, None),
            P(both, None),
            P(),
            P("fsdp", None),
            P("fsdp", None),
            P("fsdp", None),
            P("fsdp", None),
            P(),
            P(),
            P(),
            P("fsdp", None),
            P("fsdp", "replica", None),
            P("fsdp", "replica", None),
            P(),
            P("fsdp", None),
            P("fsdp", None),
        ),
        check_vma=False,
    )
```

```python
import functools

import jax
import jax.numpy as jnp
from jax import lax
from jax.experimental import pallas as pl
from jax.experimental.pallas import tpu as pltpu
from jax.sharding import PartitionSpec as P

HD = 128
EXPERTS = 16
CAP = 144

epsilon = 1e-06
rope_base = 10000.0
BF = jnp.bfloat16
F32 = jnp.float32


def rms_norm(values, gain):
    return values * lax.rsqrt(jnp.mean(values * values, axis=-1, keepdims=True) + epsilon) * gain


def rope_tables(length, width):
    places = jnp.arange(length, dtype=F32)
    rates = rope_base ** (-jnp.arange(width // 2, dtype=F32) * 2.0 / width)
    angle = places[:, None] * rates[None, :]
    return jnp.cos(angle), jnp.sin(angle)


def rotate(values, cosine, sine):
    half = values.shape[-1] // 2
    first = values[..., :half]
    second = values[..., half:]
    return jnp.concatenate(
        [first * cosine - second * sine, second * cosine + first * sine], axis=-1
    )


def dot(left, right):
    return jnp.dot(left, right, preferred_element_type=F32)


def dot_tn(left, right):
    return lax.dot_general(left, right, (((0,), (0,)), ((), ())), preferred_element_type=F32)


def dot_nt(left, right):
    return lax.dot_general(left, right, (((1,), (1,)), ((), ())), preferred_element_type=F32)


EXTRA = 16


def nothing(*refs):
    pass


def after(value, *others):
    held = pl.BlockSpec(memory_space=pl.ANY)
    return pl.pallas_call(
        nothing,
        in_specs=[held] * (1 + len(others)),
        out_specs=held,
        out_shape=jax.ShapeDtypeStruct(value.shape, value.dtype),
        input_output_aliases={0: 0},
        name="after",
    )(value, *others)


def expert_kernel(tile, wide, unread, who, *refs):
    (nf_a, nf_b, cot_a, cot_b, pick_a, pick_b, spread_a, spread_b) = refs[:8]
    (mask_a, mask_b, router, w_in, w_out) = refs[8:13]
    refs = refs[13 + unread :]
    rows, gp, cot_rows, scaled, moe, back_a, back_b, gates_hi, gates_lo = refs
    j = pl.program_id(0)
    cap = pick_a.shape[2]
    length = nf_a.shape[0]
    ff = w_out.shape[1]
    core, expert = who[3], who[4] + j

    @pl.when(j == 0)
    def _():
        for at, (nf, mask) in enumerate(((nf_a, mask_a), (nf_b, mask_b))):
            seen = mask[0] > 0.0
            logits = jnp.where(seen, dot(nf[...], router[...]), -1e30)
            powers = jnp.where(seen, jnp.exp(logits - jnp.max(logits, axis=1, keepdims=True)), 0.0)
            gates = powers / jnp.sum(powers, axis=1, keepdims=True)
            high = gates.astype(BF)
            gates_hi[at] = high
            gates_lo[at] = (gates - high.astype(F32)).astype(BF)

    pa, pb = pick_a[0, 0], pick_b[0, 0]
    lane = lax.broadcasted_iota(jnp.int32, (cap, router.shape[1]), 1)

    def slot_gates(p, at):
        every = dot(p, gates_hi[at]) + dot(p, gates_lo[at])
        return jnp.sum(jnp.where(lane == expert, every, 0.0), axis=1, keepdims=True)

    gate = jnp.concatenate([slot_gates(pa, 0), slot_gates(pb, 1)], axis=0)
    rows[0, :cap] = dot(pa, nf_a[...]).astype(BF)
    rows[0, cap:] = dot(pb, nf_b[...]).astype(BF)
    cot_rows[0, :cap] = dot(pa, cot_a[...]).astype(BF)
    cot_rows[0, cap:] = dot(pb, cot_b[...]).astype(BF)

    def forward(t, total):
        at = pl.multiple_of(t * tile, tile)
        g = dot(rows[0], w_in[0, :, pl.ds(at, tile)])
        u = dot(rows[0], w_in[0, :, pl.ds(ff + at, tile)])
        pulled = dot_nt(cot_rows[0], w_out[0, pl.ds(at, tile), :])
        sigma = jax.nn.sigmoid(g)
        silu = g * sigma
        active = silu * u
        scaled[0, :, pl.ds(at, tile)] = (active * gate).astype(BF)
        ga = pulled * gate
        gp[0, :, pl.ds(at, tile)] = (ga * u * sigma * (1.0 + g * (1.0 - sigma))).astype(BF)
        gp[0, :, pl.ds(ff + at, tile)] = (ga * silu).astype(BF)
        return total + jnp.sum(active * pulled, axis=1, keepdims=True)

    total = lax.fori_loop(0, ff // tile, forward, jnp.zeros((2 * cap, 1), F32))
    line = lax.broadcasted_iota(jnp.int32, (EXTRA, length), 0)
    place = 2 * (core * pl.num_programs(0) + j)
    for back, p, part in ((back_a, pa, total[:cap]), (back_b, pb, total[cap:])):
        by_token = jnp.sum(p.astype(F32) * part, axis=0, keepdims=True)
        high = by_token.astype(BF).astype(F32)
        new = jnp.where(line == place, high, jnp.where(line == place + 1, by_token - high, 0.0))

        @pl.when(j == 0)
        def _(back=back):
            back[length:, :] = jnp.zeros((EXTRA, back.shape[1]), BF)

        old = back[length:, :length].astype(F32)
        back[length:, :length] = (old + new).astype(BF)
    sa, sb = spread_a[0, 0], spread_b[0, 0]
    moe_a = pl.ds(pl.multiple_of(core * length, length), length)
    moe_b = pl.ds(pl.multiple_of((1 - core) * length, length), length)

    def backward(t, _):
        here = pl.ds(pl.multiple_of(t * wide, wide), wide)
        gr = dot_nt(gp[0], w_in[0, here, :]).astype(BF)
        res = dot(scaled[0], w_out[0, :, here]).astype(BF)
        for out, where, s, value in (
            (back_a, pl.ds(0, length), sa, gr[:cap]),
            (back_b, pl.ds(0, length), sb, gr[cap:]),
            (moe, moe_a, sa, res[:cap]),
            (moe, moe_b, sb, res[cap:]),
        ):
            old = jnp.where(j > 0, out[where, here].astype(F32), 0.0)
            out[where, here] = (dot(s, value) + old).astype(BF)
        return 0

    lax.fori_loop(0, w_in.shape[1] // wide, backward, 0)


def expert_block(k, rounds, who, nf, cot, pick, spread, mask, router, w_in, w_out, kept, first):
    length, width = nf[0].shape
    count, _, two_ff = w_in.shape
    groups = pick.shape[0]
    ff = two_ff // 2
    cap = pick.shape[2]
    lanes = router.shape[1]

    def whole(j, who):
        return (0, 0)

    def seq(i):
        return lambda j, who: (who[i], j, 0, 0)

    in_specs = [pl.BlockSpec((length, width), whole)] * 2
    if len(cot) == 2:
        in_specs += [pl.BlockSpec((length, width), whole)] * 2
    else:
        cot = [cot[0]] * 2
        in_specs += [
            pl.BlockSpec((length, width), lambda j, who, i=i: (who[i], 0)) for i in range(2)
        ]
    in_specs += [pl.BlockSpec((1, 1, cap, length), seq(i)) for i in range(2)]
    in_specs += [pl.BlockSpec((1, 1, length, cap), seq(i)) for i in range(2)]
    in_specs += [
        pl.BlockSpec((1, length, lanes), lambda j, who, i=i: (who[i], 0, 0)) for i in range(2)
    ]
    in_specs += [
        pl.BlockSpec((width, lanes), whole),
        pl.BlockSpec((1, width, two_ff), lambda j, who: (j, 0, 0)),
        pl.BlockSpec((1, ff, width), lambda j, who: (j, 0, 0)),
    ]
    args = [*nf, *cot, pick, pick, spread, spread, mask, mask, router, w_in, w_out]
    total = rounds * 2 * cap
    saved = [(count, total, n) for n in (width, two_ff, width, ff)]
    out_shape = [jax.ShapeDtypeStruct(s, BF) for s in saved]
    out_shape += [jax.ShapeDtypeStruct((groups * length, width), BF)]
    out_shape += [jax.ShapeDtypeStruct((length + EXTRA, width), BF)] * 2
    out_specs = [pl.BlockSpec((1, 2 * cap, s[2]), lambda j, who: (j, k, 0)) for s in saved]
    out_specs += [pl.BlockSpec((2 * length, width), lambda j, who: (who[2], 0))]
    out_specs += [pl.BlockSpec((length + EXTRA, width), whole)] * 2
    aliases = {}
    if kept is not None:
        aliases = {1 + len(args) + i: i for i in range(len(kept))}
        in_specs += [pl.BlockSpec(memory_space=pl.ANY)] * len(kept)
        args += list(kept)
    in_specs += [pl.BlockSpec(memory_space=pl.ANY)] * len(first)
    args += list(first)
    results = pl.pallas_call(
        functools.partial(expert_kernel, min(512, ff), min(1024, width), len(aliases) + len(first)),
        grid_spec=pltpu.PrefetchScalarGridSpec(
            num_scalar_prefetch=1,
            grid=(count,),
            in_specs=in_specs,
            out_specs=out_specs,
            scratch_shapes=[pltpu.VMEM((2, length, lanes), BF)] * 2,
        ),
        out_shape=out_shape,
        input_output_aliases=aliases,
        compiler_params=pltpu.CompilerParams(vmem_limit_bytes=60 * 2**20),
        cost_estimate=pl.CostEstimate(
            flops=count * 2 * cap * width * ff * 12 * 2,
            bytes_accessed=count * 3 * width * ff * 2 + 20 * length * width * 2,
            transcendentals=0,
        ),
        name="experts",
    )(who, *args)
    return results[:5], results[5], results[6]


def out_kernel(replicas, groups, who, *refs):
    pieces = refs[:replicas]
    near, far, tokens, gain = refs[replicas : replicas + 4]
    hidden, normed, mixed = refs[replicas + 4 :]
    part = pieces[0].shape[1]
    depth = near.shape[1] // (groups // 2)
    for q in range(replicas):
        mixed[:, pl.ds(pl.multiple_of((who[0] ^ q) * part, part), part)] = pieces[q][...]
    for q in range(replicas):
        total = jnp.zeros((tokens.shape[0], part), F32)
        for k in range(groups // 2):
            for flip, source in enumerate((near, far)):
                at = ((who[2] ^ flip) * (groups // 2) + k) * depth
                left = mixed[:, pl.ds(pl.multiple_of(at, depth), depth)]
                total += dot(left, source[q, k * depth : (k + 1) * depth])
        here = pl.ds(pl.multiple_of((who[0] ^ q) * part, part), part)
        hidden[:, here] = tokens[:, here].astype(F32) + total
    value = hidden[...]
    scale = lax.rsqrt(jnp.mean(value * value, axis=1, keepdims=True) + epsilon)
    normed[...] = (value * scale * gain[...]).astype(BF)


def out_step(who, pieces, near, far, tokens, gain):
    replicas = len(pieces)
    length, width = tokens.shape
    groups = lax.axis_size("fsdp")
    vmem = pl.BlockSpec(memory_space=pltpu.VMEM)
    return pl.pallas_call(
        functools.partial(out_kernel, replicas, groups),
        in_specs=[pl.BlockSpec(memory_space=pltpu.SMEM)] + [vmem] * (replicas + 4),
        out_specs=[vmem] * 3,
        out_shape=[
            jax.ShapeDtypeStruct((length, width), F32),
            jax.ShapeDtypeStruct((length, width), BF),
            jax.ShapeDtypeStruct((length, width), BF),
        ],
        compiler_params=pltpu.CompilerParams(vmem_limit_bytes=60 * 2**20),
        name="attention_out",
    )(who, *pieces, near, far, tokens, gain)


def back_kernel(replicas, groups, experts, who, *refs):
    rounds = groups // 2
    shares = refs[:rounds]
    hidden, normed, cot, gain, gates, router, near, far = refs[rounds : rounds + 8]
    grad_hidden, gain_grad, router_grad = refs[rounds + 8 : rounds + 11]
    pieces = refs[rounds + 11 : rounds + 11 + replicas]
    mixed = refs[rounds + 11 + replicas]
    length, width = hidden.shape
    lanes = router.shape[1]
    part = width // replicas
    depth = width // groups
    per_chip = experts // rounds
    line = lax.broadcasted_iota(jnp.int32, (EXTRA, lanes), 0)
    lane = lax.broadcasted_iota(jnp.int32, (EXTRA, lanes), 1)
    summed = jnp.zeros((length, width), F32)
    grad_gates = jnp.zeros((length, lanes), F32)
    for k in range(rounds):
        summed += shares[k][:length].astype(F32)
        chip = who[1] ^ k
        place = (lane == chip * per_chip + line // 2) & (line < 2 * per_chip)
        grad_gates += dot_tn(shares[k][length:, :length], place.astype(BF))
    own = gates[...]
    centered = grad_gates - jnp.sum(own * grad_gates, axis=1, keepdims=True)
    grad_logits = (own * centered).astype(BF)
    router_grad[...] = dot_tn(normed[...], grad_logits).astype(BF)
    grad_normed = summed + dot_nt(grad_logits, router[...])
    value = hidden[...]
    scale = lax.rsqrt(jnp.mean(value * value, axis=1, keepdims=True) + epsilon)
    gain_grad[...] = jnp.sum(grad_normed * value * scale, axis=0, keepdims=True)
    pulled = grad_normed * gain[...]
    inner = jnp.mean(pulled * value, axis=1, keepdims=True)
    total = cot[...].astype(F32) + scale * pulled - value * (scale * scale * scale * inner)
    grad_hidden[...] = total
    for q in range(replicas):
        here = pl.ds(pl.multiple_of((who[0] ^ q) * part, part), part)
        pieces[q][:, part:] = grad_hidden[:, here].astype(BF)
    for k in range(rounds):
        for flip, source in enumerate((near, far)):
            block = jnp.zeros((length, depth), F32)
            for q in range(replicas):
                block += dot_nt(pieces[q][:, part:], source[q, k * depth : (k + 1) * depth])
            at = ((who[2] ^ flip) * (groups // 2) + k) * depth
            mixed[:, pl.ds(pl.multiple_of(at, depth), depth)] = block.astype(BF)
    for q in range(replicas):
        here = pl.ds(pl.multiple_of((who[0] ^ q) * part, part), part)
        pieces[q][:, :part] = mixed[:, here]


def back_step(who, shares, hidden, normed, cot, gain, gates, router, near, far, experts):
    replicas = near.shape[0]
    length, width = hidden.shape
    groups = 2 * len(shares)
    vmem = pl.BlockSpec(memory_space=pltpu.VMEM)
    piece = jax.ShapeDtypeStruct((length, 2 * width // replicas), BF)
    results = pl.pallas_call(
        functools.partial(back_kernel, replicas, groups, experts),
        in_specs=[pl.BlockSpec(memory_space=pltpu.SMEM)] + [vmem] * (len(shares) + 8),
        out_specs=[vmem] * (3 + replicas),
        scratch_shapes=[pltpu.VMEM((length, width), BF)],
        out_shape=[
            jax.ShapeDtypeStruct((length, width), F32),
            jax.ShapeDtypeStruct((1, width), F32),
            jax.ShapeDtypeStruct((width, router.shape[1]), BF),
            *[piece] * replicas,
        ],
        compiler_params=pltpu.CompilerParams(vmem_limit_bytes=60 * 2**20),
        cost_estimate=pl.CostEstimate(flops=10**11, bytes_accessed=0, transcendentals=0),
        name="attention_back",
    )(who, *shares, hidden, normed, cot, gain, gates, router, near, far)
    return results[0], results[1], results[2], results[3:]


def turn(value, cosine, sine):
    return value * cosine + pltpu.roll(value, value.shape[1] // 2, 1) * sine


def attend_kernel(heads, normed, weight, seg_row, seg_col, cosine, sine, gains, *outs):
    raw, ready, mixed, totals, tops = outs
    allowed = seg_col[0] == seg_row[0]
    lane = lax.broadcasted_iota(jnp.int32, totals.shape, 1)
    top_lane = lax.broadcasted_iota(jnp.int32, tops.shape[1:], 1)
    part = heads * HD
    totals[...] = jnp.zeros(totals.shape, F32)
    tops[0] = jnp.zeros(tops.shape[1:], F32)
    for i in range(2):
        raw[:, i * part : (i + 1) * part] = dot(normed[...], weight[:, i * part : (i + 1) * part])
    ready[:, 2 * part :] = dot(normed[...], weight[:, 2 * part : 3 * part]).astype(BF)
    for h in range(heads):
        rotated = []
        for i in range(2):
            at = slice(i * part + h * HD, i * part + (h + 1) * HD)
            head = raw[:, at]
            norm = lax.rsqrt(jnp.mean(head * head, axis=1, keepdims=True) + epsilon)
            rotated.append(turn(head * norm * gains[i : i + 1], cosine[...], sine[...]).astype(BF))
            ready[:, at] = rotated[i]
        scores = dot_nt(rotated[0], rotated[1]) * HD**-0.5
        scores = jnp.where(allowed, scores, -1e30)
        peak = jnp.max(scores, axis=1, keepdims=True)
        powers = jnp.exp(scores - peak)
        total = peak + jnp.log(jnp.sum(powers, axis=1, keepdims=True))
        weights = jnp.exp(scores - total).astype(BF)
        here = slice(h * HD, (h + 1) * HD)
        mixed[:, here] = dot(weights, ready[:, 2 * part + h * HD : 2 * part + (h + 1) * HD]).astype(BF)
        totals[...] = jnp.where(lane == h, total, totals[...])
        tops[0] = jnp.where(top_lane == h, jnp.max(peak, axis=0, keepdims=True), tops[0])


def attend(normed, weight, segments, cosine, sine, gains, heads):
    count, length = segments.shape
    rows, width = normed.shape
    part = heads * HD
    one = lambda n: (n, 0)
    fixed = lambda n: (0, 0)
    return pl.pallas_call(
        functools.partial(attend_kernel, heads),
        grid=(count,),
        in_specs=[
            pl.BlockSpec((length, width), one),
            pl.BlockSpec((width, 3 * part), fixed, pipeline_mode=pl.Buffered(1)),
            pl.BlockSpec((1, 1, length), lambda n: (n, 0, 0)),
            pl.BlockSpec((1, length, 1), lambda n: (n, 0, 0)),
            pl.BlockSpec((length, HD), fixed),
            pl.BlockSpec((length, HD), fixed),
            pl.BlockSpec((2, HD), fixed),
        ],
        out_specs=[
            pl.BlockSpec((length, 2 * part), one),
            pl.BlockSpec((length, 3 * part), one),
            pl.BlockSpec((length, part), one),
            pl.BlockSpec((length, 128), one),
            pl.BlockSpec((1, 1, 128), lambda n: (n, 0, 0)),
        ],
        out_shape=[
            jax.ShapeDtypeStruct((rows, 2 * part), F32),
            jax.ShapeDtypeStruct((rows, 3 * part), BF),
            jax.ShapeDtypeStruct((rows, part), BF),
            jax.ShapeDtypeStruct((rows, 128), F32),
            jax.ShapeDtypeStruct((count, 1, 128), F32),
        ],
        compiler_params=pltpu.CompilerParams(vmem_limit_bytes=60 * 2**20),
        cost_estimate=pl.CostEstimate(flops=0, bytes_accessed=0, transcendentals=0),
        name="attention",
    )(normed, weight, segments[:, None, :], segments[:, :, None], cosine, sine, gains)


def attend_back_kernel(heads, pull, raw, ready, totals, seg_row, seg_col, cosine, sine, gains, grad, gain_grads):
    allowed = seg_col[0] == seg_row[0]
    lane = lax.broadcasted_iota(jnp.int32, totals.shape, 1)
    part = heads * HD
    sums = [jnp.zeros((1, HD), F32)] * 2
    for h in range(heads):
        at = [slice(i * part + h * HD, i * part + (h + 1) * HD) for i in range(3)]
        query, key, value = (ready[:, a] for a in at)
        pulled = pull[:, h * HD : (h + 1) * HD]
        total = jnp.sum(jnp.where(lane == h, totals[...], 0.0), axis=1, keepdims=True)
        scores = dot_nt(query, key) * HD**-0.5
        probs = jnp.where(allowed, jnp.exp(jnp.where(allowed, scores - total, 0.0)), 0.0)
        grad_weights = dot_nt(pulled, value)
        grad[:, at[2]] = dot_tn(probs.astype(BF), pulled).astype(BF)
        inner = jnp.sum(probs * grad_weights, axis=1, keepdims=True)
        grad_scores = (probs * (grad_weights - inner)).astype(BF)
        both = (dot(grad_scores, key), dot_tn(grad_scores, query))
        for i, g in enumerate(both):
            g = g * HD**-0.5
            back = g * cosine[...] - pltpu.roll(g, HD // 2, 1) * sine[...]
            head = raw[:, at[i]]
            norm = lax.rsqrt(jnp.mean(head * head, axis=1, keepdims=True) + epsilon)
            sums[i] = sums[i] + jnp.sum(back * head * norm, axis=0, keepdims=True)
            scaled = back * gains[i : i + 1]
            mean = jnp.mean(scaled * head, axis=1, keepdims=True)
            grad[:, at[i]] = (norm * scaled - head * (norm * norm * norm * mean)).astype(BF)
    for i in range(2):
        gain_grads[0, i : i + 1] = sums[i]


def attend_back(pull, raw, ready, totals, segments, cosine, sine, gains, heads):
    count, length = segments.shape
    rows = raw.shape[0]
    part = heads * HD
    one = lambda n: (n, 0)
    fixed = lambda n: (0, 0)
    return pl.pallas_call(
        functools.partial(attend_back_kernel, heads),
        grid=(count,),
        in_specs=[
            pl.BlockSpec((length, part), one),
            pl.BlockSpec((length, 2 * part), one),
            pl.BlockSpec((length, 3 * part), one),
            pl.BlockSpec((length, 128), one),
            pl.BlockSpec((1, 1, length), lambda n: (n, 0, 0)),
            pl.BlockSpec((1, length, 1), lambda n: (n, 0, 0)),
            pl.BlockSpec((length, HD), fixed),
            pl.BlockSpec((length, HD), fixed),
            pl.BlockSpec((2, HD), fixed),
        ],
        out_specs=[
            pl.BlockSpec((length, 3 * part), one),
            pl.BlockSpec((1, 2, HD), lambda n: (n, 0, 0)),
        ],
        out_shape=[
            jax.ShapeDtypeStruct((rows, 3 * part), BF),
            jax.ShapeDtypeStruct((count, 2, HD), F32),
        ],
        compiler_params=pltpu.CompilerParams(vmem_limit_bytes=32 * 2**20),
        cost_estimate=pl.CostEstimate(
            flops=0, bytes_accessed=0, transcendentals=0
        ),
        name="attention_grad",
    )(pull, raw, ready, totals, segments[:, None, :], segments[:, :, None], cosine, sine, gains)


def weight_grad_kernel(half, quarters, left, right, *outs):
    j, i = pl.program_id(0), pl.program_id(1)
    block = dot_tn(left[0], right[0]).astype(BF)
    for at, out in enumerate(outs):

        @pl.when((j == at // 2) & ((i >= half) == (at % 2 == 1)))
        def _(out=out):
            out[0] = block


def weight_grads(quarters, left, right, parts, cost):
    count, rows, width = left.shape
    size, n = width // parts, right.shape[2]
    half = parts // 2

    def spot(at):
        def index(j, i, quarters):
            step = j * parts + i - (at // 2 * parts + at % 2 * half)
            return (jnp.clip(step, 0, half - 1), 0, 0)

        return index

    return pl.pallas_call(
        functools.partial(weight_grad_kernel, half),
        grid_spec=pltpu.PrefetchScalarGridSpec(
            num_scalar_prefetch=1,
            grid=(count, parts),
            in_specs=[
                pl.BlockSpec((1, rows, size), lambda j, i, quarters: (j, 0, quarters[j, i])),
                pl.BlockSpec((1, rows, n), lambda j, i, quarters: (j, 0, 0)),
            ],
            out_specs=[pl.BlockSpec((1, size, n), spot(at)) for at in range(2 * count)],
        ),
        out_shape=[jax.ShapeDtypeStruct((half, size, n), BF)] * (2 * count),
        compiler_params=pltpu.CompilerParams(vmem_limit_bytes=56 * 2**20),
        cost_estimate=pl.CostEstimate(flops=cost, bytes_accessed=0, transcendentals=0),
        name="weight_grads",
    )(quarters, left, right)


def product_kernel(left, right, out):
    out[...] = dot_tn(left[...], right[...]).astype(BF)


def product(left, right):
    rows, width = left.shape
    n = right.shape[1]
    size = min(width, 256)
    return pl.pallas_call(
        product_kernel,
        grid=(width // size,),
        in_specs=[
            pl.BlockSpec((rows, size), lambda i: (0, i)),
            pl.BlockSpec((rows, n), lambda i: (0, 0)),
        ],
        out_specs=pl.BlockSpec((size, n), lambda i: (i, 0)),
        out_shape=jax.ShapeDtypeStruct((width, n), BF),
        compiler_params=pltpu.CompilerParams(vmem_limit_bytes=32 * 2**20),
        cost_estimate=pl.CostEstimate(flops=0, bytes_accessed=0, transcendentals=0),
        name="product",
    )(left, right)


def spread_kernel(grad, weight, *outs):
    block = dot_nt(grad[...], weight[...]).astype(BF)
    for at, out in enumerate(outs):

        @pl.when(pl.program_id(0) == at)
        def _(out=out):
            out[...] = block


def normed_grads(grad, weight, count):
    rows, n = grad.shape
    width = weight.shape[0]
    length = rows // count
    return pl.pallas_call(
        spread_kernel,
        grid=(count,),
        in_specs=[
            pl.BlockSpec((length, n), lambda i: (i, 0)),
            pl.BlockSpec((width, n), lambda i: (0, 0), pipeline_mode=pl.Buffered(1)),
        ],
        out_specs=[pl.BlockSpec((length, width), lambda i: (0, 0))] * count,
        out_shape=[jax.ShapeDtypeStruct((length, width), BF)] * count,
        compiler_params=pltpu.CompilerParams(vmem_limit_bytes=48 * 2**20),
        cost_estimate=pl.CostEstimate(flops=0, bytes_accessed=0, transcendentals=0),
        name="normed_grads",
    )(grad, weight)


def halve_kernel(half, blocks, keep, got, send_out, keep_out):
    block = (keep[0].astype(F32) + got[0].astype(F32)).astype(BF)

    @pl.when(pl.program_id(0) < half)
    def _():
        send_out[0] = block

    @pl.when(pl.program_id(0) >= half)
    def _():
        keep_out[0] = block


def halve(blocks, keep, got, cost):
    count, size, n = keep.shape
    half = count // 2
    here = pl.BlockSpec((1, size, n), lambda i, blocks: (blocks[i], 0, 0))
    return pl.pallas_call(
        functools.partial(halve_kernel, half),
        grid_spec=pltpu.PrefetchScalarGridSpec(
            num_scalar_prefetch=1,
            grid=(count,),
            in_specs=[here, here],
            out_specs=[
                pl.BlockSpec((1, size, n), lambda i, blocks: (jnp.minimum(i, half - 1), 0, 0)),
                pl.BlockSpec((1, size, n), lambda i, blocks: (jnp.maximum(i - half, 0), 0, 0)),
            ],
        ),
        out_shape=[jax.ShapeDtypeStruct((half, size, n), BF)] * 2,
        compiler_params=pltpu.CompilerParams(vmem_limit_bytes=32 * 2**20),
        cost_estimate=pl.CostEstimate(flops=cost, bytes_accessed=0, transcendentals=0),
        name="halve",
    )(blocks, keep, got)


def join_kernel(*refs):
    out = refs[-1]
    for j in range((len(refs) - 1) // 2):

        @pl.when(pl.program_id(0) == j)
        def _(j=j):
            out[0] = refs[2 * j][...].astype(F32) + refs[2 * j + 1][...].astype(F32)


def join(pairs, cost):
    size, n = pairs[0][0].shape
    step = min(size, 256)
    count = len(pairs)

    def spot(at):
        def index(j, i):
            k = j * (size // step) + i - at * (size // step)
            return (jnp.clip(k, 0, size // step - 1), 0)

        return index

    return pl.pallas_call(
        join_kernel,
        grid=(count, size // step),
        in_specs=[pl.BlockSpec((step, n), spot(at // 2)) for at in range(2 * count)],
        out_specs=pl.BlockSpec((1, step, n), lambda j, i: (j, i, 0)),
        out_shape=jax.ShapeDtypeStruct((count, size, n), F32),
        compiler_params=pltpu.CompilerParams(vmem_limit_bytes=60 * 2**20),
        cost_estimate=pl.CostEstimate(flops=cost, bytes_accessed=0, transcendentals=0),
        name="join",
    )(*[v for pair in pairs for v in pair])


def input_kernel(count, heads, who, *refs):
    pieces = refs[:count]
    tokens, gain, grad_hidden, ffn, gains, tops, grad, small = refs[count:]
    width = tokens.shape[1]
    pulled = pieces[0][...].astype(F32)
    for piece in pieces[1:]:
        pulled = pulled + piece[...].astype(F32)
    value = tokens[...].astype(F32)
    scale = lax.rsqrt(jnp.mean(value * value, axis=1, keepdims=True) + epsilon)
    small[:, :width] = jnp.sum(pulled * value * scale, axis=0, keepdims=True)
    small[:, width : 2 * width] = ffn[...]
    for i in range(2):
        at = 2 * width + i * HD
        small[:, at : at + HD] = jnp.sum(gains[:, i], axis=0, keepdims=True)
    top = jnp.max(tops[:, 0], axis=0, keepdims=True)
    lane = lax.broadcasted_iota(jnp.int32, top.shape, 1)
    top = jnp.where(lane < heads, top, -3e38)
    small[:, 2 * width + 2 * HD :] = pltpu.roll(top, who[0] * heads, 1)
    pulled = pulled * gain[...]
    inner = jnp.mean(pulled * value, axis=1, keepdims=True)
    back = scale * pulled - value * (scale * scale * scale * inner)
    grad[...] = (grad_hidden[...] + back).astype(BF)


def input_step(who, pieces, tokens, gain, grad_hidden, ffn, gains, tops, heads):
    length, width = tokens.shape
    vmem = pl.BlockSpec(memory_space=pltpu.VMEM)
    return pl.pallas_call(
        functools.partial(input_kernel, len(pieces), heads),
        in_specs=[pl.BlockSpec(memory_space=pltpu.SMEM)] + [vmem] * (len(pieces) + 6),
        out_specs=[vmem] * 2,
        out_shape=[
            jax.ShapeDtypeStruct((length, width), BF),
            jax.ShapeDtypeStruct((1, 2 * width + 2 * HD + 128), F32),
        ],
        compiler_params=pltpu.CompilerParams(vmem_limit_bytes=60 * 2**20),
        cost_estimate=pl.CostEstimate(flops=10**11, bytes_accessed=0, transcendentals=0),
        name="input_grad",
    )(who, *pieces, tokens, gain, grad_hidden, ffn, gains, tops)


def gather_kernel(count, arrays, who, *refs):
    blocks, outs = refs[:count], refs[count:]
    part = outs[0].shape[1] // count
    total = 0.0
    for k, block in enumerate(blocks):
        here = pl.ds(pl.multiple_of((who[0] ^ k) * part, part), part)
        for i in range(arrays):
            outs[i][:, here] = block[:, i * part : (i + 1) * part].astype(F32)
        if len(outs) > arrays:
            total += block[:, arrays * part :].astype(F32)
    if len(outs) > arrays:
        outs[-1][...] = total


def gather_step(who, blocks, arrays):
    rows, wide = blocks[0].shape
    lanes = 128 if wide % (arrays * 256) else 0
    part = (wide - lanes) // arrays
    count = len(blocks)
    vmem = pl.BlockSpec(memory_space=pltpu.VMEM)
    return pl.pallas_call(
        functools.partial(gather_kernel, count, arrays),
        in_specs=[pl.BlockSpec(memory_space=pltpu.SMEM)] + [vmem] * count,
        out_specs=[vmem] * (arrays + (lanes > 0)),
        out_shape=[jax.ShapeDtypeStruct((rows, part * count), F32)] * arrays
        + [jax.ShapeDtypeStruct((rows, lanes), F32)] * (lanes > 0),
        compiler_params=pltpu.CompilerParams(vmem_limit_bytes=48 * 2**20),
        cost_estimate=pl.CostEstimate(flops=0, bytes_accessed=0, transcendentals=0),
        name="gather_columns",
    )(who, *blocks)


def local(
    tokens,
    cotangent,
    segment_ids,
    expert_index,
    clip_threshold,
    attn_norm_gain,
    w_query,
    w_key,
    w_value,
    w_output,
    query_gain,
    key_gain,
    ffn_norm_gain,
    router,
    expert_in,
    expert_out,
):
    replicas = lax.axis_size("replica")
    groups = lax.axis_size("fsdp")
    me_r = lax.axis_index("replica")
    me_f = lax.axis_index("fsdp")
    core = me_f % 2
    length, width = tokens.shape
    part = width // replicas
    heads = part // HD
    ff = expert_out.shape[1]
    local_experts = expert_in.shape[0]
    scale = HD ** (-0.5)
    attn_gain = attn_norm_gain.astype(F32)
    ffn_gain = ffn_norm_gain.astype(F32)
    gain_query = query_gain.astype(F32)
    gain_key = key_gain.astype(F32)

    def swap(value, k):
        return lax.ppermute(value, "replica", [(r, r ^ k) for r in range(replicas)])

    def columns(value, k, axis=1):
        return lax.dynamic_slice_in_dim(value, (me_r ^ k) * part, part, axis)

    def spread(value):
        return [value] + [swap(value, k) for k in range(1, replicas)]

    def trade_columns(value):
        return [columns(value, 0)] + [swap(columns(value, k), k) for k in range(1, replicas)]

    def join_columns(blocks):
        out = jnp.zeros((blocks[0].shape[0], part * replicas), blocks[0].dtype)
        for k, block in enumerate(blocks):
            out = lax.dynamic_update_slice_in_dim(out, block, (me_r ^ k) * part, 1)
        return out

    def cross(value, k):
        return lax.ppermute(value, "fsdp", [(f, f ^ k) for f in range(groups)])

    def pass_on(up, down, hop):
        chips = groups // 2
        pairs = [(2 * a + i, 2 * a + 2 + i) for a in range(hop - 1, chips - 1) for i in (0, 1)]
        back = [(2 * a + 2 + i, 2 * a + i) for a in range(chips - hop) for i in (0, 1)]
        return lax.ppermute(up, "fsdp", pairs), lax.ppermute(down, "fsdp", back)

    def choose(up, down, k):
        chips = groups // 2
        found = {}
        for a in range(chips):
            b = a ^ k
            found.setdefault((b > a, abs(b - a)), []).append(a)
        picked = None
        for (above, hop), at in found.items():
            source = down[hop] if above else up[hop]
            if picked is None:
                picked = source
            else:
                here = functools.reduce(jnp.logical_or, [me_f // 2 == a for a in at])
                picked = jnp.where(here, source, picked)
        return picked

    def gather(value):
        return lax.all_gather(value, "fsdp", axis=0, tiled=True)

    def reduce(value):
        return lax.psum_scatter(value, "fsdp", scatter_dimension=0, tiled=True)

    bits = replicas.bit_length() - 1

    def next_bit(j, step):
        return 1 << (bits - 1 - step if j % 2 else step)

    def next_halves(traded, j, step, cost=0):
        keep, got = traded
        left = keep.shape[0]
        place = jnp.arange(left, dtype=jnp.int32)
        here = left // 2 if j % 2 else 1
        mine = (me_r & next_bit(j, step)) != 0
        other = ((place & here) != 0) != mine
        spots = jnp.where(other, jnp.cumsum(other) - 1, left // 2 + jnp.cumsum(~other) - 1)
        return halve(jnp.zeros((left,), jnp.int32).at[spots].set(place), keep, got, cost)

    index_table = expert_index.astype(BF).reshape(w_query.shape[0], -1)
    sent = [columns(w_output, 0), router, index_table]
    sizes = [v.shape[1] for v in sent]
    sent.append(jnp.zeros((w_query.shape[0], -sum(sizes) % 128), BF))
    quarter = gather(jnp.concatenate(sent, axis=1))
    full_router = quarter[:, part : part + EXPERTS]
    full_index = quarter[:, part + EXPERTS : part + EXPERTS + sizes[2]].astype(jnp.int32)
    full_index = full_index.reshape(groups * length, -1)
    ids = jnp.arange(EXPERTS, dtype=jnp.int32)
    mask = jnp.any(full_index[:, :, None] == ids, axis=1).reshape(groups, length, EXPERTS)
    first = me_f * local_experts
    hot = lax.dynamic_slice_in_dim(mask, first, local_experts, 2)
    order = jnp.arange(length, dtype=jnp.int32)
    before = (order[:, None] < order[None, :]).astype(BF)
    rank = jnp.einsum("nsj,st->njt", hot.astype(BF), before, preferred_element_type=F32)
    rank = jnp.where(hot.transpose(0, 2, 1), rank.astype(jnp.int32), -1)
    slots = jnp.arange(CAP, dtype=jnp.int32)
    pick = (rank[:, :, None, :] == slots[:, None]).astype(BF)
    spots = (rank[:, :, :, None] == slots).astype(BF)
    lanes = 128
    mask_wide = jnp.pad(mask.astype(F32), ((0, 0), (0, 0), (0, lanes - EXPERTS)))
    router_wide = jnp.pad(full_router, ((0, 0), (0, lanes - EXPERTS)))
    tables = (pick, spots, mask_wide, router_wide)
    segments = spread(segment_ids)
    tokens_all = spread(after(tokens, *segments[1:]))
    segments = jnp.concatenate(segments, axis=0)
    normed = jnp.concatenate(
        [rms_norm(v.astype(F32), attn_gain).astype(BF) for v in tokens_all], axis=0
    )
    rounds = groups // 2
    where = jnp.stack([me_r, me_f // 2, core]).astype(jnp.int32)
    half = lax.dynamic_slice(quarter, (core * (width // 2), 0), (width // 2, part))
    near = spread(after(half, *tokens_all[1:]))
    near[1] = after(near[1], *tables, segments, normed)
    normed = after(normed, *near[1:])
    w_qkv = gather(jnp.concatenate([columns(w, 0) for w in (w_query, w_key, w_value)], axis=1))
    cot_all = gather(cotangent)
    cot_pair = (cotangent, cross(cotangent, 1))

    cosine, sine = rope_tables(length, HD)
    cosine = jnp.concatenate([cosine, cosine], axis=1)
    sine = jnp.concatenate([-sine, sine], axis=1)
    gains = jnp.stack([gain_query, gain_key])
    raw, ready, mixed_heads, totals, tops = attend(normed, w_qkv, segments, cosine, sine, gains, heads
    )
    near = jnp.stack([after(near[0], raw), *near[1:]])
    far = cross(near, 1)
    mixed_heads = mixed_heads.reshape(replicas, length, part)
    pieces = [mixed_heads[0]] + [swap(mixed_heads[k], k) for k in range(1, replicas)]
    inputs = tokens.astype(F32)
    hidden, normed_ffn, mixed = out_step(where, pieces, near, far, tokens, ffn_gain[None, :])
    mixed_all = spread(mixed)

    def first_bit(j):
        return 1 << (bits - 1 if j % 2 else 0)

    numbers = jnp.arange(replicas, dtype=jnp.int32)
    quarters = []
    for j in range(local_experts):
        other = ((numbers ^ me_r) & first_bit(j)) != 0
        place = jnp.where(other, jnp.cumsum(other) - 1, replicas // 2 + jnp.cumsum(~other) - 1)
        quarters.append(jnp.zeros((replicas,), jnp.int32).at[place].set(numbers))
    quarters = jnp.stack(quarters)
    kept = None
    shares = []
    added = []
    pending = []
    up, down = [normed_ffn], [normed_ffn]
    for k in range(rounds):
        chip = (me_f // 2) ^ k
        who = jnp.stack([2 * chip + core, 2 * chip + 1 - core, chip, core, first])
        if k + 1 < rounds:
            next_up, next_down = pass_on(up[-1], down[-1], k + 1)
        mine = choose(up, down, k) if k else normed_ffn
        nf = (mine, cross(mine, 1))
        kept, back_a, back_b = expert_block(k, rounds, who, nf, (cot_all,) if k else cot_pair, pick, spots, mask_wide, router_wide, expert_in, expert_out, kept, pending
        )
        if k + 1 < rounds:
            up.append(after(next_up, back_a))
            down.append(after(next_down, back_a))
        else:
            rows, grad_projected, cot_rows, scaled, moe = kept
            out_blocks = weight_grads(quarters, after(scaled, mixed_all[-1]), cot_rows, replicas, 0)
        if k == rounds - 1:
            back_b = after(back_b, *out_blocks, *shares[1:])
        share = (back_a.astype(F32) + cross(back_b, 1).astype(F32)).astype(BF)
        added.append(share)
        if k == rounds - 2:
            pending = added[1:]
        else:
            pending = mixed_all[1:-1] if k == rounds - 3 else []
        shares.append(share if k == 0 else cross(share, 2 * k))
    out_traded = [
        (out_blocks[2 * j + 1], swap(out_blocks[2 * j], first_bit(j))) for j in range(local_experts)
    ]
    in_blocks = weight_grads(quarters, after(rows, share), grad_projected, replicas, 10**11)
    shares[-1] = after(shares[-1], *in_blocks, *[v[1] for v in out_traded])
    moe_sum = reduce(after(moe, shares[-1]))
    output = (hidden + moe_sum.astype(F32)).astype(BF)

    my_mask = lax.dynamic_index_in_dim(mask_wide, me_f, 0, keepdims=False) > 0.0
    logits = jnp.where(my_mask, dot(normed_ffn, router_wide), -jnp.inf)
    powers = jnp.exp(logits - jnp.max(logits, axis=1, keepdims=True))
    my_gates = powers / jnp.sum(powers, axis=1, keepdims=True)
    grad_hidden, ffn_gain_grad, router_grad, pieces = back_step(
        where, shares, hidden, normed_ffn, cotangent, ffn_gain[None, :], my_gates, router_wide, near, far, EXPERTS
    )
    grad_mixed = jnp.concatenate(
        [pieces[0]] + [swap(pieces[k], k) for k in range(1, replicas)], axis=0
    )
    sends = [
        after(in_blocks[2 * j], grad_mixed, *[v[1] for v in out_traded]) for j in range(local_experts)
    ]
    in_traded = [
        (in_blocks[2 * j + 1], swap(v, first_bit(j))) for j, v in enumerate(sends)
    ]
    grad_mixed = after(grad_mixed, *sends)
    grad_qkv, gain_grads = attend_back(grad_mixed, raw, ready, totals, segments, cosine, sine, gains, heads
    )
    qkv_grad = product(normed, grad_qkv)
    part_normed = normed_grads(grad_qkv, w_qkv, replicas)
    received = [v[1] for v in in_traded]
    received[0] = after(received[0], *received[1:], moe_sum)
    in_traded = [(v[0], got) for v, got in zip(in_traded, received)]
    in_halves = [next_halves(v, j, 1, 10**11) for j, v in enumerate(in_traded)]
    in_sends = [v for v, _ in in_halves]
    in_done = [(keep, swap(v, next_bit(j, 1))) for j, (v, keep) in enumerate(in_halves)]
    pieces = [after(part_normed[0], *in_sends)]
    pieces += [swap(part_normed[k], k) for k in range(1, replicas)]
    input_grad, small = input_step(
        where, pieces, tokens, attn_gain[None, :], grad_hidden, ffn_gain_grad, gain_grads, tops, heads
    )
    second = [v[1] for v in in_done]
    output_grad = dot_tn(jnp.concatenate(mixed_all, axis=0), grad_mixed[:, part:])
    share_o = reduce(jnp.concatenate([output_grad.astype(BF), router_grad], axis=1))
    share_qkv = reduce(qkv_grad)
    blocks = spread(after(jnp.concatenate([share_qkv, share_o], axis=1), *second))
    out_halves = [next_halves((k, after(v, input_grad)), j, 1) for j, (k, v) in enumerate(out_traded)]
    out_done = [
        (keep, swap(after(v, *second, moe_sum), next_bit(j, 1))) for j, (v, keep) in enumerate(out_halves)
    ]
    total_query, total_key, total_value, total_output, total_router = gather_step(where, blocks, 4)
    total_router = total_router[:, :EXPERTS]

    def settle(traded, cost):
        pairs = []
        for j, (keep, got) in enumerate(traded):
            for step in range(2, bits):
                send, keep = next_halves((keep, got), j, step)
                got = swap(send, next_bit(j, step))
            pairs.append((keep[0], got[0]))
        return join(pairs, cost)

    expert_in_grad = settle(in_done, 10**11)
    expert_out_grad = settle([(k, after(v, expert_in_grad)) for k, v in out_done], 0)

    small = after(small, *second)
    n_sums = 2 * width + 2 * HD
    is_sum = jnp.arange(small.shape[1]) < n_sums

    def merge(a, b):
        return jnp.where(is_sum, a + b, jnp.maximum(a, b))

    small = functools.reduce(merge, spread(small))
    small = merge(small, cross(small, 1))
    small = functools.reduce(merge, [small] + [cross(small, 2 * k) for k in range(1, rounds)])
    small = small[0]
    attn_gain_total = small[:width]
    ffn_gain_total = small[width : 2 * width]
    query_gain_total = small[2 * width : 2 * width + HD]
    key_gain_total = small[2 * width + HD : n_sums]
    head_max = small[n_sums : n_sums + replicas * heads]
    threshold = clip_threshold.astype(F32)
    factor = threshold / jnp.maximum(head_max, threshold)
    column_scale = jnp.repeat(jnp.sqrt(factor), HD)
    clipped_query = (w_query.astype(F32) * column_scale[None, :]).astype(BF)
    clipped_key = (w_key.astype(F32) * column_scale[None, :]).astype(BF)
    return (
        output,
        input_grad,
        attn_gain_total,
        total_query,
        total_key,
        total_value,
        total_output,
        query_gain_total,
        key_gain_total,
        ffn_gain_total,
        total_router,
        expert_in_grad,
        expert_out_grad,
        head_max,
        clipped_query,
        clipped_key,
    )


def solution(mesh):
    both = ("replica", "fsdp")
    return jax.shard_map(
        local,
        mesh=mesh,
        in_specs=(
            P(both, None),
            P(both, None),
            P(both, None),
            P(both, None),
            P(),
            P(),
            P("fsdp", None),
            P("fsdp", None),
            P("fsdp", None),
            P("fsdp", None),
            P(),
            P(),
            P(),
            P("fsdp", None),
            P("fsdp", None, None),
            P("fsdp", None, None),
        ),
        out_specs=(
            P(both, None),
            P(both, None),
            P(),
            P("fsdp", None),
            P("fsdp", None),
            P("fsdp", None),
            P("fsdp", None),
            P(),
            P(),
            P(),
            P("fsdp", None),
            P("fsdp", "replica", None),
            P("fsdp", "replica", None),
            P(),
            P("fsdp", None),
            P("fsdp", None),
        ),
        check_vma=False,
    )
```

```python
import functools

import jax
import jax.numpy as jnp
from jax import lax
from jax.experimental import pallas as pl
from jax.experimental.pallas import tpu as pltpu
from jax.sharding import PartitionSpec as P

HD = 128
EXPERTS = 16
CAP = 144

epsilon = 1e-06
rope_base = 10000.0
BF = jnp.bfloat16
F32 = jnp.float32


def rms_norm(values, gain):
    return values * lax.rsqrt(jnp.mean(values * values, axis=-1, keepdims=True) + epsilon) * gain


def rope_tables(length, width):
    places = jnp.arange(length, dtype=F32)
    rates = rope_base ** (-jnp.arange(width // 2, dtype=F32) * 2.0 / width)
    angle = places[:, None] * rates[None, :]
    return jnp.cos(angle), jnp.sin(angle)


def rotate(values, cosine, sine):
    half = values.shape[-1] // 2
    first = values[..., :half]
    second = values[..., half:]
    return jnp.concatenate(
        [first * cosine - second * sine, second * cosine + first * sine], axis=-1
    )


def dot(left, right):
    return jnp.dot(left, right, preferred_element_type=F32)


def dot_tn(left, right):
    return lax.dot_general(left, right, (((0,), (0,)), ((), ())), preferred_element_type=F32)


def dot_nt(left, right):
    return lax.dot_general(left, right, (((1,), (1,)), ((), ())), preferred_element_type=F32)


EXTRA = 16


def nothing(*refs):
    pass


def after(value, *others):
    held = pl.BlockSpec(memory_space=pl.ANY)
    return pl.pallas_call(
        nothing,
        in_specs=[held] * (1 + len(others)),
        out_specs=held,
        out_shape=jax.ShapeDtypeStruct(value.shape, value.dtype),
        input_output_aliases={0: 0},
        name="after",
    )(value, *others)


def expert_kernel(tile, wide, unread, who, *refs):
    (nf_a, nf_b, cot_a, cot_b, pick_a, pick_b, spread_a, spread_b) = refs[:8]
    (mask_a, mask_b, router, w_in, w_out) = refs[8:13]
    refs = refs[13 + unread :]
    rows, gp, cot_rows, scaled, moe, back_a, back_b, gates_hi, gates_lo = refs
    j = pl.program_id(0)
    cap = pick_a.shape[2]
    length = nf_a.shape[0]
    ff = w_out.shape[1]
    core, expert = who[3], who[4] + j

    @pl.when(j == 0)
    def _():
        for at, (nf, mask) in enumerate(((nf_a, mask_a), (nf_b, mask_b))):
            seen = mask[0] > 0.0
            logits = jnp.where(seen, dot(nf[...], router[...]), -1e30)
            powers = jnp.where(seen, jnp.exp(logits - jnp.max(logits, axis=1, keepdims=True)), 0.0)
            gates = powers / jnp.sum(powers, axis=1, keepdims=True)
            high = gates.astype(BF)
            gates_hi[at] = high
            gates_lo[at] = (gates - high.astype(F32)).astype(BF)

    pa, pb = pick_a[0, 0], pick_b[0, 0]
    lane = lax.broadcasted_iota(jnp.int32, (cap, router.shape[1]), 1)

    def slot_gates(p, at):
        every = dot(p, gates_hi[at]) + dot(p, gates_lo[at])
        return jnp.sum(jnp.where(lane == expert, every, 0.0), axis=1, keepdims=True)

    gate = jnp.concatenate([slot_gates(pa, 0), slot_gates(pb, 1)], axis=0)
    rows[0, :cap] = dot(pa, nf_a[...]).astype(BF)
    rows[0, cap:] = dot(pb, nf_b[...]).astype(BF)
    cot_rows[0, :cap] = dot(pa, cot_a[...]).astype(BF)
    cot_rows[0, cap:] = dot(pb, cot_b[...]).astype(BF)

    def forward(t, total):
        at = pl.multiple_of(t * tile, tile)
        g = dot(rows[0], w_in[0, :, pl.ds(at, tile)])
        u = dot(rows[0], w_in[0, :, pl.ds(ff + at, tile)])
        pulled = dot_nt(cot_rows[0], w_out[0, pl.ds(at, tile), :])
        sigma = jax.nn.sigmoid(g)
        silu = g * sigma
        active = silu * u
        scaled[0, :, pl.ds(at, tile)] = (active * gate).astype(BF)
        ga = pulled * gate
        gp[0, :, pl.ds(at, tile)] = (ga * u * sigma * (1.0 + g * (1.0 - sigma))).astype(BF)
        gp[0, :, pl.ds(ff + at, tile)] = (ga * silu).astype(BF)
        return total + jnp.sum(active * pulled, axis=1, keepdims=True)

    total = lax.fori_loop(0, ff // tile, forward, jnp.zeros((2 * cap, 1), F32))
    line = lax.broadcasted_iota(jnp.int32, (EXTRA, length), 0)
    place = 2 * (core * pl.num_programs(0) + j)
    for back, p, part in ((back_a, pa, total[:cap]), (back_b, pb, total[cap:])):
        by_token = jnp.sum(p.astype(F32) * part, axis=0, keepdims=True)
        high = by_token.astype(BF).astype(F32)
        new = jnp.where(line == place, high, jnp.where(line == place + 1, by_token - high, 0.0))

        @pl.when(j == 0)
        def _(back=back):
            back[length:, :] = jnp.zeros((EXTRA, back.shape[1]), BF)

        old = back[length:, :length].astype(F32)
        back[length:, :length] = (old + new).astype(BF)
    sa, sb = spread_a[0, 0], spread_b[0, 0]
    moe_a = pl.ds(pl.multiple_of(core * length, length), length)
    moe_b = pl.ds(pl.multiple_of((1 - core) * length, length), length)

    def backward(t, _):
        here = pl.ds(pl.multiple_of(t * wide, wide), wide)
        gr = dot_nt(gp[0], w_in[0, here, :]).astype(BF)
        res = dot(scaled[0], w_out[0, :, here]).astype(BF)
        for out, where, s, value in (
            (back_a, pl.ds(0, length), sa, gr[:cap]),
            (back_b, pl.ds(0, length), sb, gr[cap:]),
            (moe, moe_a, sa, res[:cap]),
            (moe, moe_b, sb, res[cap:]),
        ):
            old = jnp.where(j > 0, out[where, here].astype(F32), 0.0)
            out[where, here] = (dot(s, value) + old).astype(BF)
        return 0

    lax.fori_loop(0, w_in.shape[1] // wide, backward, 0)


def expert_block(k, rounds, who, nf, cot, pick, spread, mask, router, w_in, w_out, kept, first):
    length, width = nf[0].shape
    count, _, two_ff = w_in.shape
    groups = pick.shape[0]
    ff = two_ff // 2
    cap = pick.shape[2]
    lanes = router.shape[1]

    def whole(j, who):
        return (0, 0)

    def seq(i):
        return lambda j, who: (who[i], j, 0, 0)

    in_specs = [pl.BlockSpec((length, width), whole)] * 2
    if len(cot) == 2:
        in_specs += [pl.BlockSpec((length, width), whole)] * 2
    else:
        cot = [cot[0]] * 2
        in_specs += [
            pl.BlockSpec((length, width), lambda j, who, i=i: (who[i], 0)) for i in range(2)
        ]
    in_specs += [pl.BlockSpec((1, 1, cap, length), seq(i)) for i in range(2)]
    in_specs += [pl.BlockSpec((1, 1, length, cap), seq(i)) for i in range(2)]
    in_specs += [
        pl.BlockSpec((1, length, lanes), lambda j, who, i=i: (who[i], 0, 0)) for i in range(2)
    ]
    in_specs += [
        pl.BlockSpec((width, lanes), whole),
        pl.BlockSpec((1, width, two_ff), lambda j, who: (j, 0, 0)),
        pl.BlockSpec((1, ff, width), lambda j, who: (j, 0, 0)),
    ]
    args = [*nf, *cot, pick, pick, spread, spread, mask, mask, router, w_in, w_out]
    total = rounds * 2 * cap
    saved = [(count, total, n) for n in (width, two_ff, width, ff)]
    out_shape = [jax.ShapeDtypeStruct(s, BF) for s in saved]
    out_shape += [jax.ShapeDtypeStruct((groups * length, width), BF)]
    out_shape += [jax.ShapeDtypeStruct((length + EXTRA, width), BF)] * 2
    out_specs = [pl.BlockSpec((1, 2 * cap, s[2]), lambda j, who: (j, k, 0)) for s in saved]
    out_specs += [pl.BlockSpec((2 * length, width), lambda j, who: (who[2], 0))]
    out_specs += [pl.BlockSpec((length + EXTRA, width), whole)] * 2
    aliases = {}
    if kept is not None:
        aliases = {1 + len(args) + i: i for i in range(len(kept))}
        in_specs += [pl.BlockSpec(memory_space=pl.ANY)] * len(kept)
        args += list(kept)
    in_specs += [pl.BlockSpec(memory_space=pl.ANY)] * len(first)
    args += list(first)
    results = pl.pallas_call(
        functools.partial(expert_kernel, min(512, ff), min(1024, width), len(aliases) + len(first)),
        grid_spec=pltpu.PrefetchScalarGridSpec(
            num_scalar_prefetch=1,
            grid=(count,),
            in_specs=in_specs,
            out_specs=out_specs,
            scratch_shapes=[pltpu.VMEM((2, length, lanes), BF)] * 2,
        ),
        out_shape=out_shape,
        input_output_aliases=aliases,
        compiler_params=pltpu.CompilerParams(vmem_limit_bytes=60 * 2**20),
        cost_estimate=pl.CostEstimate(
            flops=count * 2 * cap * width * ff * 12 * 2,
            bytes_accessed=count * 3 * width * ff * 2 + 20 * length * width * 2,
            transcendentals=0,
        ),
        name="experts",
    )(who, *args)
    return results[:5], results[5], results[6]


def out_kernel(replicas, groups, who, *refs):
    pieces = refs[:replicas]
    near, far, tokens, gain = refs[replicas : replicas + 4]
    hidden, normed, mixed = refs[replicas + 4 :]
    part = pieces[0].shape[1]
    depth = near.shape[1] // (groups // 2)
    for q in range(replicas):
        mixed[:, pl.ds(pl.multiple_of((who[0] ^ q) * part, part), part)] = pieces[q][...]
    for q in range(replicas):
        total = jnp.zeros((tokens.shape[0], part), F32)
        for k in range(groups // 2):
            for flip, source in enumerate((near, far)):
                at = ((who[2] ^ flip) * (groups // 2) + k) * depth
                left = mixed[:, pl.ds(pl.multiple_of(at, depth), depth)]
                total += dot(left, source[q, k * depth : (k + 1) * depth])
        here = pl.ds(pl.multiple_of((who[0] ^ q) * part, part), part)
        hidden[:, here] = tokens[:, here].astype(F32) + total
    value = hidden[...]
    scale = lax.rsqrt(jnp.mean(value * value, axis=1, keepdims=True) + epsilon)
    normed[...] = (value * scale * gain[...]).astype(BF)


def out_step(who, pieces, near, far, tokens, gain):
    replicas = len(pieces)
    length, width = tokens.shape
    groups = lax.axis_size("fsdp")
    vmem = pl.BlockSpec(memory_space=pltpu.VMEM)
    return pl.pallas_call(
        functools.partial(out_kernel, replicas, groups),
        in_specs=[pl.BlockSpec(memory_space=pltpu.SMEM)] + [vmem] * (replicas + 4),
        out_specs=[vmem] * 3,
        out_shape=[
            jax.ShapeDtypeStruct((length, width), F32),
            jax.ShapeDtypeStruct((length, width), BF),
            jax.ShapeDtypeStruct((length, width), BF),
        ],
        compiler_params=pltpu.CompilerParams(vmem_limit_bytes=60 * 2**20),
        name="attention_out",
    )(who, *pieces, near, far, tokens, gain)


def back_kernel(replicas, groups, experts, who, *refs):
    rounds = groups // 2
    shares = refs[:rounds]
    hidden, normed, cot, gain, gates, router, near, far = refs[rounds : rounds + 8]
    grad_hidden, gain_grad, router_grad = refs[rounds + 8 : rounds + 11]
    pieces = refs[rounds + 11 : rounds + 11 + replicas]
    mixed = refs[rounds + 11 + replicas]
    length, width = hidden.shape
    lanes = router.shape[1]
    part = width // replicas
    depth = width // groups
    per_chip = experts // rounds
    line = lax.broadcasted_iota(jnp.int32, (EXTRA, lanes), 0)
    lane = lax.broadcasted_iota(jnp.int32, (EXTRA, lanes), 1)
    summed = jnp.zeros((length, width), F32)
    grad_gates = jnp.zeros((length, lanes), F32)
    for k in range(rounds):
        summed += shares[k][:length].astype(F32)
        chip = who[1] ^ k
        place = (lane == chip * per_chip + line // 2) & (line < 2 * per_chip)
        grad_gates += dot_tn(shares[k][length:, :length], place.astype(BF))
    own = gates[...]
    centered = grad_gates - jnp.sum(own * grad_gates, axis=1, keepdims=True)
    grad_logits = (own * centered).astype(BF)
    router_grad[...] = dot_tn(normed[...], grad_logits).astype(BF)
    grad_normed = summed + dot_nt(grad_logits, router[...])
    value = hidden[...]
    scale = lax.rsqrt(jnp.mean(value * value, axis=1, keepdims=True) + epsilon)
    gain_grad[...] = jnp.sum(grad_normed * value * scale, axis=0, keepdims=True)
    pulled = grad_normed * gain[...]
    inner = jnp.mean(pulled * value, axis=1, keepdims=True)
    total = cot[...].astype(F32) + scale * pulled - value * (scale * scale * scale * inner)
    grad_hidden[...] = total
    for q in range(replicas):
        here = pl.ds(pl.multiple_of((who[0] ^ q) * part, part), part)
        pieces[q][:, part:] = grad_hidden[:, here].astype(BF)
    for k in range(rounds):
        for flip, source in enumerate((near, far)):
            block = jnp.zeros((length, depth), F32)
            for q in range(replicas):
                block += dot_nt(pieces[q][:, part:], source[q, k * depth : (k + 1) * depth])
            at = ((who[2] ^ flip) * (groups // 2) + k) * depth
            mixed[:, pl.ds(pl.multiple_of(at, depth), depth)] = block.astype(BF)
    for q in range(replicas):
        here = pl.ds(pl.multiple_of((who[0] ^ q) * part, part), part)
        pieces[q][:, :part] = mixed[:, here]


def back_step(who, shares, hidden, normed, cot, gain, gates, router, near, far, experts):
    replicas = near.shape[0]
    length, width = hidden.shape
    groups = 2 * len(shares)
    vmem = pl.BlockSpec(memory_space=pltpu.VMEM)
    piece = jax.ShapeDtypeStruct((length, 2 * width // replicas), BF)
    results = pl.pallas_call(
        functools.partial(back_kernel, replicas, groups, experts),
        in_specs=[pl.BlockSpec(memory_space=pltpu.SMEM)] + [vmem] * (len(shares) + 8),
        out_specs=[vmem] * (3 + replicas),
        scratch_shapes=[pltpu.VMEM((length, width), BF)],
        out_shape=[
            jax.ShapeDtypeStruct((length, width), F32),
            jax.ShapeDtypeStruct((1, width), F32),
            jax.ShapeDtypeStruct((width, router.shape[1]), BF),
            *[piece] * replicas,
        ],
        compiler_params=pltpu.CompilerParams(vmem_limit_bytes=60 * 2**20),
        cost_estimate=pl.CostEstimate(flops=10**11, bytes_accessed=0, transcendentals=0),
        name="attention_back",
    )(who, *shares, hidden, normed, cot, gain, gates, router, near, far)
    return results[0], results[1], results[2], results[3:]


def turn(value, cosine, sine):
    return value * cosine + pltpu.roll(value, value.shape[1] // 2, 1) * sine


def attend_kernel(heads, normed, weight, seg_row, seg_col, cosine, sine, gains, *outs):
    raw, ready, mixed, totals, tops = outs
    allowed = seg_col[0] == seg_row[0]
    lane = lax.broadcasted_iota(jnp.int32, totals.shape, 1)
    top_lane = lax.broadcasted_iota(jnp.int32, tops.shape[1:], 1)
    part = heads * HD
    totals[...] = jnp.zeros(totals.shape, F32)
    tops[0] = jnp.zeros(tops.shape[1:], F32)
    for i in range(2):
        raw[:, i * part : (i + 1) * part] = dot(normed[...], weight[:, i * part : (i + 1) * part])
    ready[:, 2 * part :] = dot(normed[...], weight[:, 2 * part : 3 * part]).astype(BF)
    for h in range(heads):
        rotated = []
        for i in range(2):
            at = slice(i * part + h * HD, i * part + (h + 1) * HD)
            head = raw[:, at]
            norm = lax.rsqrt(jnp.mean(head * head, axis=1, keepdims=True) + epsilon)
            rotated.append(turn(head * norm * gains[i : i + 1], cosine[...], sine[...]).astype(BF))
            ready[:, at] = rotated[i]
        scores = dot_nt(rotated[0], rotated[1]) * HD**-0.5
        scores = jnp.where(allowed, scores, -1e30)
        peak = jnp.max(scores, axis=1, keepdims=True)
        powers = jnp.exp(scores - peak)
        total = peak + jnp.log(jnp.sum(powers, axis=1, keepdims=True))
        weights = jnp.exp(scores - total).astype(BF)
        here = slice(h * HD, (h + 1) * HD)
        mixed[:, here] = dot(weights, ready[:, 2 * part + h * HD : 2 * part + (h + 1) * HD]).astype(BF)
        totals[...] = jnp.where(lane == h, total, totals[...])
        tops[0] = jnp.where(top_lane == h, jnp.max(peak, axis=0, keepdims=True), tops[0])


def attend(normed, weight, segments, cosine, sine, gains, heads):
    count, length = segments.shape
    rows, width = normed.shape
    part = heads * HD
    one = lambda n: (n, 0)
    fixed = lambda n: (0, 0)
    return pl.pallas_call(
        functools.partial(attend_kernel, heads),
        grid=(count,),
        in_specs=[
            pl.BlockSpec((length, width), one),
            pl.BlockSpec((width, 3 * part), fixed, pipeline_mode=pl.Buffered(1)),
            pl.BlockSpec((1, 1, length), lambda n: (n, 0, 0)),
            pl.BlockSpec((1, length, 1), lambda n: (n, 0, 0)),
            pl.BlockSpec((length, HD), fixed),
            pl.BlockSpec((length, HD), fixed),
            pl.BlockSpec((2, HD), fixed),
        ],
        out_specs=[
            pl.BlockSpec((length, 2 * part), one),
            pl.BlockSpec((length, 3 * part), one),
            pl.BlockSpec((length, part), one),
            pl.BlockSpec((length, 128), one),
            pl.BlockSpec((1, 1, 128), lambda n: (n, 0, 0)),
        ],
        out_shape=[
            jax.ShapeDtypeStruct((rows, 2 * part), F32),
            jax.ShapeDtypeStruct((rows, 3 * part), BF),
            jax.ShapeDtypeStruct((rows, part), BF),
            jax.ShapeDtypeStruct((rows, 128), F32),
            jax.ShapeDtypeStruct((count, 1, 128), F32),
        ],
        compiler_params=pltpu.CompilerParams(vmem_limit_bytes=60 * 2**20),
        cost_estimate=pl.CostEstimate(flops=0, bytes_accessed=0, transcendentals=0),
        name="attention",
    )(normed, weight, segments[:, None, :], segments[:, :, None], cosine, sine, gains)


def attend_back_kernel(heads, pull, raw, ready, totals, seg_row, seg_col, cosine, sine, gains, grad, gain_grads):
    allowed = seg_col[0] == seg_row[0]
    lane = lax.broadcasted_iota(jnp.int32, totals.shape, 1)
    part = heads * HD
    sums = [jnp.zeros((1, HD), F32)] * 2
    for h in range(heads):
        at = [slice(i * part + h * HD, i * part + (h + 1) * HD) for i in range(3)]
        query, key, value = (ready[:, a] for a in at)
        pulled = pull[:, h * HD : (h + 1) * HD]
        total = jnp.sum(jnp.where(lane == h, totals[...], 0.0), axis=1, keepdims=True)
        scores = dot_nt(query, key) * HD**-0.5
        probs = jnp.where(allowed, jnp.exp(jnp.where(allowed, scores - total, 0.0)), 0.0)
        grad_weights = dot_nt(pulled, value)
        grad[:, at[2]] = dot_tn(probs.astype(BF), pulled).astype(BF)
        inner = jnp.sum(probs * grad_weights, axis=1, keepdims=True)
        grad_scores = (probs * (grad_weights - inner)).astype(BF)
        both = (dot(grad_scores, key), dot_tn(grad_scores, query))
        for i, g in enumerate(both):
            g = g * HD**-0.5
            back = g * cosine[...] - pltpu.roll(g, HD // 2, 1) * sine[...]
            head = raw[:, at[i]]
            norm = lax.rsqrt(jnp.mean(head * head, axis=1, keepdims=True) + epsilon)
            sums[i] = sums[i] + jnp.sum(back * head * norm, axis=0, keepdims=True)
            scaled = back * gains[i : i + 1]
            mean = jnp.mean(scaled * head, axis=1, keepdims=True)
            grad[:, at[i]] = (norm * scaled - head * (norm * norm * norm * mean)).astype(BF)
    for i in range(2):
        gain_grads[0, i : i + 1] = sums[i]


def attend_back(pull, raw, ready, totals, segments, cosine, sine, gains, heads):
    count, length = segments.shape
    rows = raw.shape[0]
    part = heads * HD
    one = lambda n: (n, 0)
    fixed = lambda n: (0, 0)
    return pl.pallas_call(
        functools.partial(attend_back_kernel, heads),
        grid=(count,),
        in_specs=[
            pl.BlockSpec((length, part), one),
            pl.BlockSpec((length, 2 * part), one),
            pl.BlockSpec((length, 3 * part), one),
            pl.BlockSpec((length, 128), one),
            pl.BlockSpec((1, 1, length), lambda n: (n, 0, 0)),
            pl.BlockSpec((1, length, 1), lambda n: (n, 0, 0)),
            pl.BlockSpec((length, HD), fixed),
            pl.BlockSpec((length, HD), fixed),
            pl.BlockSpec((2, HD), fixed),
        ],
        out_specs=[
            pl.BlockSpec((length, 3 * part), one),
            pl.BlockSpec((1, 2, HD), lambda n: (n, 0, 0)),
        ],
        out_shape=[
            jax.ShapeDtypeStruct((rows, 3 * part), BF),
            jax.ShapeDtypeStruct((count, 2, HD), F32),
        ],
        compiler_params=pltpu.CompilerParams(vmem_limit_bytes=32 * 2**20),
        cost_estimate=pl.CostEstimate(
            flops=0, bytes_accessed=0, transcendentals=0
        ),
        name="attention_grad",
    )(pull, raw, ready, totals, segments[:, None, :], segments[:, :, None], cosine, sine, gains)


def weight_grad_kernel(half, quarters, left, right, *outs):
    j, i = pl.program_id(0), pl.program_id(1)
    block = dot_tn(left[0], right[0]).astype(BF)
    for at, out in enumerate(outs):

        @pl.when((j == at // 2) & ((i >= half) == (at % 2 == 1)))
        def _(out=out):
            out[0] = block


def weight_grads(quarters, left, right, parts, cost):
    count, rows, width = left.shape
    size, n = width // parts, right.shape[2]
    half = parts // 2

    def spot(at):
        def index(j, i, quarters):
            step = j * parts + i - (at // 2 * parts + at % 2 * half)
            return (jnp.clip(step, 0, half - 1), 0, 0)

        return index

    return pl.pallas_call(
        functools.partial(weight_grad_kernel, half),
        grid_spec=pltpu.PrefetchScalarGridSpec(
            num_scalar_prefetch=1,
            grid=(count, parts),
            in_specs=[
                pl.BlockSpec((1, rows, size), lambda j, i, quarters: (j, 0, quarters[j, i])),
                pl.BlockSpec((1, rows, n), lambda j, i, quarters: (j, 0, 0)),
            ],
            out_specs=[pl.BlockSpec((1, size, n), spot(at)) for at in range(2 * count)],
        ),
        out_shape=[jax.ShapeDtypeStruct((half, size, n), BF)] * (2 * count),
        compiler_params=pltpu.CompilerParams(vmem_limit_bytes=56 * 2**20),
        cost_estimate=pl.CostEstimate(flops=cost, bytes_accessed=0, transcendentals=0),
        name="weight_grads",
    )(quarters, left, right)


def product_kernel(left, right, out):
    out[...] = dot_tn(left[...], right[...]).astype(BF)


def product(left, right):
    rows, width = left.shape
    n = right.shape[1]
    size = min(width, 256)
    return pl.pallas_call(
        product_kernel,
        grid=(width // size,),
        in_specs=[
            pl.BlockSpec((rows, size), lambda i: (0, i)),
            pl.BlockSpec((rows, n), lambda i: (0, 0)),
        ],
        out_specs=pl.BlockSpec((size, n), lambda i: (i, 0)),
        out_shape=jax.ShapeDtypeStruct((width, n), BF),
        compiler_params=pltpu.CompilerParams(vmem_limit_bytes=32 * 2**20),
        cost_estimate=pl.CostEstimate(flops=0, bytes_accessed=0, transcendentals=0),
        name="product",
    )(left, right)


def spread_kernel(grad, weight, *outs):
    block = dot_nt(grad[...], weight[...]).astype(BF)
    for at, out in enumerate(outs):

        @pl.when(pl.program_id(0) == at)
        def _(out=out):
            out[...] = block


def normed_grads(grad, weight, count):
    rows, n = grad.shape
    width = weight.shape[0]
    length = rows // count
    return pl.pallas_call(
        spread_kernel,
        grid=(count,),
        in_specs=[
            pl.BlockSpec((length, n), lambda i: (i, 0)),
            pl.BlockSpec((width, n), lambda i: (0, 0), pipeline_mode=pl.Buffered(1)),
        ],
        out_specs=[pl.BlockSpec((length, width), lambda i: (0, 0))] * count,
        out_shape=[jax.ShapeDtypeStruct((length, width), BF)] * count,
        compiler_params=pltpu.CompilerParams(vmem_limit_bytes=48 * 2**20),
        cost_estimate=pl.CostEstimate(flops=0, bytes_accessed=0, transcendentals=0),
        name="normed_grads",
    )(grad, weight)


def halve_kernel(half, blocks, keep, got, send_out, keep_out):
    block = (keep[0].astype(F32) + got[0].astype(F32)).astype(BF)

    @pl.when(pl.program_id(0) < half)
    def _():
        send_out[0] = block

    @pl.when(pl.program_id(0) >= half)
    def _():
        keep_out[0] = block


def halve(blocks, keep, got, cost):
    count, size, n = keep.shape
    half = count // 2
    here = pl.BlockSpec((1, size, n), lambda i, blocks: (blocks[i], 0, 0))
    return pl.pallas_call(
        functools.partial(halve_kernel, half),
        grid_spec=pltpu.PrefetchScalarGridSpec(
            num_scalar_prefetch=1,
            grid=(count,),
            in_specs=[here, here],
            out_specs=[
                pl.BlockSpec((1, size, n), lambda i, blocks: (jnp.minimum(i, half - 1), 0, 0)),
                pl.BlockSpec((1, size, n), lambda i, blocks: (jnp.maximum(i - half, 0), 0, 0)),
            ],
        ),
        out_shape=[jax.ShapeDtypeStruct((half, size, n), BF)] * 2,
        compiler_params=pltpu.CompilerParams(vmem_limit_bytes=32 * 2**20),
        cost_estimate=pl.CostEstimate(flops=cost, bytes_accessed=0, transcendentals=0),
        name="halve",
    )(blocks, keep, got)


def join_kernel(*refs):
    out = refs[-1]
    for j in range((len(refs) - 1) // 2):

        @pl.when(pl.program_id(0) == j)
        def _(j=j):
            out[0] = refs[2 * j][...].astype(F32) + refs[2 * j + 1][...].astype(F32)


def join(pairs, cost):
    size, n = pairs[0][0].shape
    step = min(size, 256)
    count = len(pairs)

    def spot(at):
        def index(j, i):
            k = j * (size // step) + i - at * (size // step)
            return (jnp.clip(k, 0, size // step - 1), 0)

        return index

    return pl.pallas_call(
        join_kernel,
        grid=(count, size // step),
        in_specs=[pl.BlockSpec((step, n), spot(at // 2)) for at in range(2 * count)],
        out_specs=pl.BlockSpec((1, step, n), lambda j, i: (j, i, 0)),
        out_shape=jax.ShapeDtypeStruct((count, size, n), F32),
        compiler_params=pltpu.CompilerParams(vmem_limit_bytes=60 * 2**20),
        cost_estimate=pl.CostEstimate(flops=cost, bytes_accessed=0, transcendentals=0),
        name="join",
    )(*[v for pair in pairs for v in pair])


def input_kernel(count, heads, who, *refs):
    pieces = refs[:count]
    tokens, gain, grad_hidden, ffn, gains, tops, grad, small = refs[count:]
    width = tokens.shape[1]
    pulled = pieces[0][...].astype(F32)
    for piece in pieces[1:]:
        pulled = pulled + piece[...].astype(F32)
    value = tokens[...].astype(F32)
    scale = lax.rsqrt(jnp.mean(value * value, axis=1, keepdims=True) + epsilon)
    small[:, :width] = jnp.sum(pulled * value * scale, axis=0, keepdims=True)
    small[:, width : 2 * width] = ffn[...]
    for i in range(2):
        at = 2 * width + i * HD
        small[:, at : at + HD] = jnp.sum(gains[:, i], axis=0, keepdims=True)
    top = jnp.max(tops[:, 0], axis=0, keepdims=True)
    lane = lax.broadcasted_iota(jnp.int32, top.shape, 1)
    top = jnp.where(lane < heads, top, -3e38)
    small[:, 2 * width + 2 * HD :] = pltpu.roll(top, who[0] * heads, 1)
    pulled = pulled * gain[...]
    inner = jnp.mean(pulled * value, axis=1, keepdims=True)
    back = scale * pulled - value * (scale * scale * scale * inner)
    grad[...] = (grad_hidden[...] + back).astype(BF)


def input_step(who, pieces, tokens, gain, grad_hidden, ffn, gains, tops, heads):
    length, width = tokens.shape
    vmem = pl.BlockSpec(memory_space=pltpu.VMEM)
    return pl.pallas_call(
        functools.partial(input_kernel, len(pieces), heads),
        in_specs=[pl.BlockSpec(memory_space=pltpu.SMEM)] + [vmem] * (len(pieces) + 6),
        out_specs=[vmem] * 2,
        out_shape=[
            jax.ShapeDtypeStruct((length, width), BF),
            jax.ShapeDtypeStruct((1, 2 * width + 2 * HD + 128), F32),
        ],
        compiler_params=pltpu.CompilerParams(vmem_limit_bytes=60 * 2**20),
        cost_estimate=pl.CostEstimate(flops=10**11, bytes_accessed=0, transcendentals=0),
        name="input_grad",
    )(who, *pieces, tokens, gain, grad_hidden, ffn, gains, tops)


def gather_kernel(count, arrays, who, *refs):
    blocks, outs = refs[:count], refs[count:]
    part = outs[0].shape[1] // count
    total = 0.0
    for k, block in enumerate(blocks):
        here = pl.ds(pl.multiple_of((who[0] ^ k) * part, part), part)
        for i in range(arrays):
            outs[i][:, here] = block[:, i * part : (i + 1) * part].astype(F32)
        if len(outs) > arrays:
            total += block[:, arrays * part :].astype(F32)
    if len(outs) > arrays:
        outs[-1][...] = total


def gather_step(who, blocks, arrays):
    rows, wide = blocks[0].shape
    lanes = 128 if wide % (arrays * 256) else 0
    part = (wide - lanes) // arrays
    count = len(blocks)
    vmem = pl.BlockSpec(memory_space=pltpu.VMEM)
    return pl.pallas_call(
        functools.partial(gather_kernel, count, arrays),
        in_specs=[pl.BlockSpec(memory_space=pltpu.SMEM)] + [vmem] * count,
        out_specs=[vmem] * (arrays + (lanes > 0)),
        out_shape=[jax.ShapeDtypeStruct((rows, part * count), F32)] * arrays
        + [jax.ShapeDtypeStruct((rows, lanes), F32)] * (lanes > 0),
        compiler_params=pltpu.CompilerParams(vmem_limit_bytes=48 * 2**20),
        cost_estimate=pl.CostEstimate(flops=0, bytes_accessed=0, transcendentals=0),
        name="gather_columns",
    )(who, *blocks)


def local(
    tokens,
    cotangent,
    segment_ids,
    expert_index,
    clip_threshold,
    attn_norm_gain,
    w_query,
    w_key,
    w_value,
    w_output,
    query_gain,
    key_gain,
    ffn_norm_gain,
    router,
    expert_in,
    expert_out,
):
    replicas = lax.axis_size("replica")
    groups = lax.axis_size("fsdp")
    me_r = lax.axis_index("replica")
    me_f = lax.axis_index("fsdp")
    core = me_f % 2
    length, width = tokens.shape
    part = width // replicas
    heads = part // HD
    ff = expert_out.shape[1]
    local_experts = expert_in.shape[0]
    scale = HD ** (-0.5)
    attn_gain = attn_norm_gain.astype(F32)
    ffn_gain = ffn_norm_gain.astype(F32)
    gain_query = query_gain.astype(F32)
    gain_key = key_gain.astype(F32)

    def swap(value, k):
        return lax.ppermute(value, "replica", [(r, r ^ k) for r in range(replicas)])

    def columns(value, k, axis=1):
        return lax.dynamic_slice_in_dim(value, (me_r ^ k) * part, part, axis)

    def spread(value):
        return [value] + [swap(value, k) for k in range(1, replicas)]

    def trade_columns(value):
        return [columns(value, 0)] + [swap(columns(value, k), k) for k in range(1, replicas)]

    def join_columns(blocks):
        out = jnp.zeros((blocks[0].shape[0], part * replicas), blocks[0].dtype)
        for k, block in enumerate(blocks):
            out = lax.dynamic_update_slice_in_dim(out, block, (me_r ^ k) * part, 1)
        return out

    def cross(value, k):
        return lax.ppermute(value, "fsdp", [(f, f ^ k) for f in range(groups)])

    def pass_on(up, down, hop):
        chips = groups // 2
        pairs = [(2 * a + i, 2 * a + 2 + i) for a in range(hop - 1, chips - 1) for i in (0, 1)]
        back = [(2 * a + 2 + i, 2 * a + i) for a in range(chips - hop) for i in (0, 1)]
        return lax.ppermute(up, "fsdp", pairs), lax.ppermute(down, "fsdp", back)

    def choose(up, down, k):
        chips = groups // 2
        found = {}
        for a in range(chips):
            b = a ^ k
            found.setdefault((b > a, abs(b - a)), []).append(a)
        picked = None
        for (above, hop), at in found.items():
            source = down[hop] if above else up[hop]
            if picked is None:
                picked = source
            else:
                here = functools.reduce(jnp.logical_or, [me_f // 2 == a for a in at])
                picked = jnp.where(here, source, picked)
        return picked

    def gather(value):
        return lax.all_gather(value, "fsdp", axis=0, tiled=True)

    def reduce(value):
        return lax.psum_scatter(value, "fsdp", scatter_dimension=0, tiled=True)

    bits = replicas.bit_length() - 1

    def next_bit(j, step):
        return 1 << (bits - 1 - step if j % 2 else step)

    def next_halves(traded, j, step, cost=0):
        keep, got = traded
        left = keep.shape[0]
        place = jnp.arange(left, dtype=jnp.int32)
        here = left // 2 if j % 2 else 1
        mine = (me_r & next_bit(j, step)) != 0
        other = ((place & here) != 0) != mine
        spots = jnp.where(other, jnp.cumsum(other) - 1, left // 2 + jnp.cumsum(~other) - 1)
        return halve(jnp.zeros((left,), jnp.int32).at[spots].set(place), keep, got, cost)

    index_table = expert_index.astype(BF).reshape(w_query.shape[0], -1)
    sent = [columns(w_output, 0), router, index_table]
    sizes = [v.shape[1] for v in sent]
    sent.append(jnp.zeros((w_query.shape[0], -sum(sizes) % 128), BF))
    quarter = gather(jnp.concatenate(sent, axis=1))
    full_router = quarter[:, part : part + EXPERTS]
    full_index = quarter[:, part + EXPERTS : part + EXPERTS + sizes[2]].astype(jnp.int32)
    full_index = full_index.reshape(groups * length, -1)
    ids = jnp.arange(EXPERTS, dtype=jnp.int32)
    mask = jnp.any(full_index[:, :, None] == ids, axis=1).reshape(groups, length, EXPERTS)
    first = me_f * local_experts
    hot = lax.dynamic_slice_in_dim(mask, first, local_experts, 2)
    order = jnp.arange(length, dtype=jnp.int32)
    before = (order[:, None] < order[None, :]).astype(BF)
    rank = jnp.einsum("nsj,st->njt", hot.astype(BF), before, preferred_element_type=F32)
    rank = jnp.where(hot.transpose(0, 2, 1), rank.astype(jnp.int32), -1)
    slots = jnp.arange(CAP, dtype=jnp.int32)
    pick = (rank[:, :, None, :] == slots[:, None]).astype(BF)
    spots = (rank[:, :, :, None] == slots).astype(BF)
    lanes = 128
    mask_wide = jnp.pad(mask.astype(F32), ((0, 0), (0, 0), (0, lanes - EXPERTS)))
    router_wide = jnp.pad(full_router, ((0, 0), (0, lanes - EXPERTS)))
    tables = (pick, spots, mask_wide, router_wide)
    tokens_all = spread(tokens)
    normed = jnp.concatenate(
        [rms_norm(v.astype(F32), attn_gain).astype(BF) for v in tokens_all], axis=0
    )
    rounds = groups // 2
    where = jnp.stack([me_r, me_f // 2, core]).astype(jnp.int32)
    half = lax.dynamic_slice(quarter, (core * (width // 2), 0), (width // 2, part))
    near = spread(after(half, *tokens_all[1:]))
    near[1] = after(near[1], *tables, normed)
    segments = jnp.concatenate(spread(after(segment_ids, near[2])), axis=0)
    normed = after(normed, *near[1:])
    w_qkv = gather(jnp.concatenate([columns(w, 0) for w in (w_query, w_key, w_value)], axis=1))
    cot_all = gather(cotangent)
    cot_pair = (cotangent, cross(cotangent, 1))

    cosine, sine = rope_tables(length, HD)
    cosine = jnp.concatenate([cosine, cosine], axis=1)
    sine = jnp.concatenate([-sine, sine], axis=1)
    gains = jnp.stack([gain_query, gain_key])
    raw, ready, mixed_heads, totals, tops = attend(normed, w_qkv, segments, cosine, sine, gains, heads
    )
    near = jnp.stack([after(near[0], raw), *near[1:]])
    far = cross(near, 1)
    mixed_heads = mixed_heads.reshape(replicas, length, part)
    pieces = [mixed_heads[0]] + [swap(mixed_heads[k], k) for k in range(1, replicas)]
    inputs = tokens.astype(F32)
    hidden, normed_ffn, mixed = out_step(where, pieces, near, far, tokens, ffn_gain[None, :])
    mixed_all = spread(mixed)

    def first_bit(j):
        return 1 << (bits - 1 if j % 2 else 0)

    numbers = jnp.arange(replicas, dtype=jnp.int32)
    quarters = []
    for j in range(local_experts):
        other = ((numbers ^ me_r) & first_bit(j)) != 0
        place = jnp.where(other, jnp.cumsum(other) - 1, replicas // 2 + jnp.cumsum(~other) - 1)
        quarters.append(jnp.zeros((replicas,), jnp.int32).at[place].set(numbers))
    quarters = jnp.stack(quarters)
    kept = None
    shares = []
    added = []
    pending = []
    up, down = [normed_ffn], [normed_ffn]
    for k in range(rounds):
        chip = (me_f // 2) ^ k
        who = jnp.stack([2 * chip + core, 2 * chip + 1 - core, chip, core, first])
        if k + 1 < rounds:
            next_up, next_down = pass_on(up[-1], down[-1], k + 1)
        mine = choose(up, down, k) if k else normed_ffn
        nf = (mine, cross(mine, 1))
        kept, back_a, back_b = expert_block(k, rounds, who, nf, (cot_all,) if k else cot_pair, pick, spots, mask_wide, router_wide, expert_in, expert_out, kept, pending
        )
        if k + 1 < rounds:
            up.append(after(next_up, back_a))
            down.append(after(next_down, back_a))
        else:
            rows, grad_projected, cot_rows, scaled, moe = kept
            out_blocks = weight_grads(quarters, after(scaled, mixed_all[-1]), cot_rows, replicas, 0)
        if k == rounds - 1:
            back_b = after(back_b, *out_blocks, *shares[1:])
        share = (back_a.astype(F32) + cross(back_b, 1).astype(F32)).astype(BF)
        added.append(share)
        if k == rounds - 2:
            pending = added[1:]
        else:
            pending = mixed_all[1:-1] if k == rounds - 3 else []
        shares.append(share if k == 0 else cross(share, 2 * k))
    out_traded = [
        (out_blocks[2 * j + 1], swap(out_blocks[2 * j], first_bit(j))) for j in range(local_experts)
    ]
    in_blocks = weight_grads(quarters, after(rows, share), grad_projected, replicas, 10**11)
    shares[-1] = after(shares[-1], *in_blocks, *[v[1] for v in out_traded])
    moe_sum = reduce(after(moe, shares[-1]))
    output = (hidden + moe_sum.astype(F32)).astype(BF)

    my_mask = lax.dynamic_index_in_dim(mask_wide, me_f, 0, keepdims=False) > 0.0
    logits = jnp.where(my_mask, dot(normed_ffn, router_wide), -jnp.inf)
    powers = jnp.exp(logits - jnp.max(logits, axis=1, keepdims=True))
    my_gates = powers / jnp.sum(powers, axis=1, keepdims=True)
    grad_hidden, ffn_gain_grad, router_grad, pieces = back_step(
        where, shares, hidden, normed_ffn, cotangent, ffn_gain[None, :], my_gates, router_wide, near, far, EXPERTS
    )
    grad_mixed = jnp.concatenate(
        [pieces[0]] + [swap(pieces[k], k) for k in range(1, replicas)], axis=0
    )
    sends = [
        after(in_blocks[2 * j], grad_mixed, *[v[1] for v in out_traded]) for j in range(local_experts)
    ]
    in_traded = [
        (in_blocks[2 * j + 1], swap(v, first_bit(j))) for j, v in enumerate(sends)
    ]
    ready = after(ready, *sends)
    grad_qkv, gain_grads = attend_back(grad_mixed, raw, ready, totals, segments, cosine, sine, gains, heads
    )
    qkv_grad = product(normed, grad_qkv)
    part_normed = normed_grads(grad_qkv, w_qkv, replicas)
    received = [v[1] for v in in_traded]
    received[0] = after(received[0], *received[1:], moe_sum)
    in_traded = [(v[0], got) for v, got in zip(in_traded, received)]
    in_halves = [next_halves(v, j, 1, 10**11) for j, v in enumerate(in_traded)]
    in_sends = [v for v, _ in in_halves]
    in_done = [(keep, swap(v, next_bit(j, 1))) for j, (v, keep) in enumerate(in_halves)]
    mixed_rows = after(jnp.concatenate(mixed_all, axis=0), *in_sends)
    output_grad = dot_tn(mixed_rows, grad_mixed[:, part:])
    o_grad = jnp.concatenate([output_grad.astype(BF), router_grad], axis=1)
    share_o = reduce(o_grad)
    out_halves = [next_halves((k, after(v, part_normed[0])), j, 1) for j, (k, v) in enumerate(out_traded)]
    pieces = [after(part_normed[0], *in_sends, o_grad, *[v for v, _ in out_halves])]
    pieces += [swap(part_normed[k], k) for k in range(1, replicas)]
    input_grad, small = input_step(
        where, pieces, tokens, attn_gain[None, :], grad_hidden, ffn_gain_grad, gain_grads, tops, heads
    )
    second = [v[1] for v in in_done]
    share_qkv = reduce(qkv_grad)
    blocks = spread(after(jnp.concatenate([share_qkv, share_o], axis=1), *second, input_grad))
    out_done = [
        (keep, swap(after(v, *second, moe_sum), next_bit(j, 1))) for j, (v, keep) in enumerate(out_halves)
    ]
    total_query, total_key, total_value, total_output, total_router = gather_step(where, blocks, 4)
    total_router = total_router[:, :EXPERTS]

    def settle(traded, cost):
        pairs = []
        for j, (keep, got) in enumerate(traded):
            for step in range(2, bits):
                send, keep = next_halves((keep, got), j, step)
                got = swap(send, next_bit(j, step))
            pairs.append((keep[0], got[0]))
        return join(pairs, cost)

    expert_in_grad = settle(in_done, 10**11)
    expert_out_grad = settle([(k, after(v, expert_in_grad)) for k, v in out_done], 0)

    n_sums = 2 * width + 2 * HD
    is_sum = jnp.arange(small.shape[1]) < n_sums

    def merge(a, b):
        return jnp.where(is_sum, a + b, jnp.maximum(a, b))

    small = functools.reduce(merge, spread(small))
    small = after(small, *blocks[1:], expert_in_grad)
    small = merge(small, cross(small, 1))
    step = 1
    while step < rounds:
        small = merge(small, cross(small, 2 * step))
        step *= 2
    small = small[0]
    attn_gain_total = small[:width]
    ffn_gain_total = small[width : 2 * width]
    query_gain_total = small[2 * width : 2 * width + HD]
    key_gain_total = small[2 * width + HD : n_sums]
    head_max = small[n_sums : n_sums + replicas * heads]
    threshold = clip_threshold.astype(F32)
    factor = threshold / jnp.maximum(head_max, threshold)
    column_scale = jnp.repeat(jnp.sqrt(factor), HD)
    clipped_query = (w_query.astype(F32) * column_scale[None, :]).astype(BF)
    clipped_key = (w_key.astype(F32) * column_scale[None, :]).astype(BF)
    return (
        output,
        input_grad,
        attn_gain_total,
        total_query,
        total_key,
        total_value,
        total_output,
        query_gain_total,
        key_gain_total,
        ffn_gain_total,
        total_router,
        expert_in_grad,
        expert_out_grad,
        head_max,
        clipped_query,
        clipped_key,
    )


def solution(mesh):
    both = ("replica", "fsdp")
    return jax.shard_map(
        local,
        mesh=mesh,
        in_specs=(
            P(both, None),
            P(both, None),
            P(both, None),
            P(both, None),
            P(),
            P(),
            P("fsdp", None),
            P("fsdp", None),
            P("fsdp", None),
            P("fsdp", None),
            P(),
            P(),
            P(),
            P("fsdp", None),
            P("fsdp", None, None),
            P("fsdp", None, None),
        ),
        out_specs=(
            P(both, None),
            P(both, None),
            P(),
            P("fsdp", None),
            P("fsdp", None),
            P("fsdp", None),
            P("fsdp", None),
            P(),
            P(),
            P(),
            P("fsdp", None),
            P("fsdp", "replica", None),
            P("fsdp", "replica", None),
            P(),
            P("fsdp", None),
            P("fsdp", None),
        ),
        check_vma=False,
    )
```

```python
import functools

import jax
import jax.numpy as jnp
from jax import lax
from jax.experimental import pallas as pl
from jax.experimental.pallas import tpu as pltpu
from jax.sharding import PartitionSpec as P

HD = 128
EXPERTS = 16
CAP = 144

epsilon = 1e-06
rope_base = 10000.0
BF = jnp.bfloat16
F32 = jnp.float32


def rms_norm(values, gain):
    return values * lax.rsqrt(jnp.mean(values * values, axis=-1, keepdims=True) + epsilon) * gain


def rope_tables(length, width):
    places = jnp.arange(length, dtype=F32)
    rates = rope_base ** (-jnp.arange(width // 2, dtype=F32) * 2.0 / width)
    angle = places[:, None] * rates[None, :]
    return jnp.cos(angle), jnp.sin(angle)


def rotate(values, cosine, sine):
    half = values.shape[-1] // 2
    first = values[..., :half]
    second = values[..., half:]
    return jnp.concatenate(
        [first * cosine - second * sine, second * cosine + first * sine], axis=-1
    )


def dot(left, right):
    return jnp.dot(left, right, preferred_element_type=F32)


def dot_tn(left, right):
    return lax.dot_general(left, right, (((0,), (0,)), ((), ())), preferred_element_type=F32)


def dot_nt(left, right):
    return lax.dot_general(left, right, (((1,), (1,)), ((), ())), preferred_element_type=F32)


EXTRA = 16


def nothing(*refs):
    pass


def after(value, *others):
    held = pl.BlockSpec(memory_space=pl.ANY)
    return pl.pallas_call(
        nothing,
        in_specs=[held] * (1 + len(others)),
        out_specs=held,
        out_shape=jax.ShapeDtypeStruct(value.shape, value.dtype),
        input_output_aliases={0: 0},
        name="after",
    )(value, *others)


def expert_kernel(tile, wide, unread, who, *refs):
    (nf_a, nf_b, cot_a, cot_b, pick_a, pick_b, spread_a, spread_b) = refs[:8]
    (mask_a, mask_b, router, w_in, w_out) = refs[8:13]
    refs = refs[13 + unread :]
    rows, gp, cot_rows, scaled, moe, back_a, back_b, gates_hi, gates_lo = refs
    j = pl.program_id(0)
    cap = pick_a.shape[2]
    length = nf_a.shape[0]
    ff = w_out.shape[1]
    core, expert = who[3], who[4] + j

    @pl.when(j == 0)
    def _():
        for at, (nf, mask) in enumerate(((nf_a, mask_a), (nf_b, mask_b))):
            seen = mask[0] > 0.0
            logits = jnp.where(seen, dot(nf[...], router[...]), -1e30)
            powers = jnp.where(seen, jnp.exp(logits - jnp.max(logits, axis=1, keepdims=True)), 0.0)
            gates = powers / jnp.sum(powers, axis=1, keepdims=True)
            high = gates.astype(BF)
            gates_hi[at] = high
            gates_lo[at] = (gates - high.astype(F32)).astype(BF)

    pa, pb = pick_a[0, 0], pick_b[0, 0]
    lane = lax.broadcasted_iota(jnp.int32, (cap, router.shape[1]), 1)

    def slot_gates(p, at):
        every = dot(p, gates_hi[at]) + dot(p, gates_lo[at])
        return jnp.sum(jnp.where(lane == expert, every, 0.0), axis=1, keepdims=True)

    gate = jnp.concatenate([slot_gates(pa, 0), slot_gates(pb, 1)], axis=0)
    rows[0, :cap] = dot(pa, nf_a[...]).astype(BF)
    rows[0, cap:] = dot(pb, nf_b[...]).astype(BF)
    cot_rows[0, :cap] = dot(pa, cot_a[...]).astype(BF)
    cot_rows[0, cap:] = dot(pb, cot_b[...]).astype(BF)

    def forward(t, total):
        at = pl.multiple_of(t * tile, tile)
        g = dot(rows[0], w_in[0, :, pl.ds(at, tile)])
        u = dot(rows[0], w_in[0, :, pl.ds(ff + at, tile)])
        pulled = dot_nt(cot_rows[0], w_out[0, pl.ds(at, tile), :])
        sigma = jax.nn.sigmoid(g)
        silu = g * sigma
        active = silu * u
        scaled[0, :, pl.ds(at, tile)] = (active * gate).astype(BF)
        ga = pulled * gate
        gp[0, :, pl.ds(at, tile)] = (ga * u * sigma * (1.0 + g * (1.0 - sigma))).astype(BF)
        gp[0, :, pl.ds(ff + at, tile)] = (ga * silu).astype(BF)
        return total + jnp.sum(active * pulled, axis=1, keepdims=True)

    total = lax.fori_loop(0, ff // tile, forward, jnp.zeros((2 * cap, 1), F32))
    line = lax.broadcasted_iota(jnp.int32, (EXTRA, length), 0)
    place = 2 * (core * pl.num_programs(0) + j)
    for back, p, part in ((back_a, pa, total[:cap]), (back_b, pb, total[cap:])):
        by_token = jnp.sum(p.astype(F32) * part, axis=0, keepdims=True)
        high = by_token.astype(BF).astype(F32)
        new = jnp.where(line == place, high, jnp.where(line == place + 1, by_token - high, 0.0))

        @pl.when(j == 0)
        def _(back=back):
            back[length:, :] = jnp.zeros((EXTRA, back.shape[1]), BF)

        old = back[length:, :length].astype(F32)
        back[length:, :length] = (old + new).astype(BF)
    sa, sb = spread_a[0, 0], spread_b[0, 0]
    moe_a = pl.ds(pl.multiple_of(core * length, length), length)
    moe_b = pl.ds(pl.multiple_of((1 - core) * length, length), length)

    def backward(t, _):
        here = pl.ds(pl.multiple_of(t * wide, wide), wide)
        gr = dot_nt(gp[0], w_in[0, here, :]).astype(BF)
        res = dot(scaled[0], w_out[0, :, here]).astype(BF)
        for out, where, s, value in (
            (back_a, pl.ds(0, length), sa, gr[:cap]),
            (back_b, pl.ds(0, length), sb, gr[cap:]),
            (moe, moe_a, sa, res[:cap]),
            (moe, moe_b, sb, res[cap:]),
        ):
            old = jnp.where(j > 0, out[where, here].astype(F32), 0.0)
            out[where, here] = (dot(s, value) + old).astype(BF)
        return 0

    lax.fori_loop(0, w_in.shape[1] // wide, backward, 0)


def expert_block(k, rounds, who, nf, cot, pick, spread, mask, router, w_in, w_out, kept, first):
    length, width = nf[0].shape
    count, _, two_ff = w_in.shape
    groups = pick.shape[0]
    ff = two_ff // 2
    cap = pick.shape[2]
    lanes = router.shape[1]

    def whole(j, who):
        return (0, 0)

    def seq(i):
        return lambda j, who: (who[i], j, 0, 0)

    in_specs = [pl.BlockSpec((length, width), whole)] * 2
    if len(cot) == 2:
        in_specs += [pl.BlockSpec((length, width), whole)] * 2
    else:
        cot = [cot[0]] * 2
        in_specs += [
            pl.BlockSpec((length, width), lambda j, who, i=i: (who[i], 0)) for i in range(2)
        ]
    in_specs += [pl.BlockSpec((1, 1, cap, length), seq(i)) for i in range(2)]
    in_specs += [pl.BlockSpec((1, 1, length, cap), seq(i)) for i in range(2)]
    in_specs += [
        pl.BlockSpec((1, length, lanes), lambda j, who, i=i: (who[i], 0, 0)) for i in range(2)
    ]
    in_specs += [
        pl.BlockSpec((width, lanes), whole),
        pl.BlockSpec((1, width, two_ff), lambda j, who: (j, 0, 0)),
        pl.BlockSpec((1, ff, width), lambda j, who: (j, 0, 0)),
    ]
    args = [*nf, *cot, pick, pick, spread, spread, mask, mask, router, w_in, w_out]
    total = rounds * 2 * cap
    saved = [(count, total, n) for n in (width, two_ff, width, ff)]
    out_shape = [jax.ShapeDtypeStruct(s, BF) for s in saved]
    out_shape += [jax.ShapeDtypeStruct((groups * length, width), BF)]
    out_shape += [jax.ShapeDtypeStruct((length + EXTRA, width), BF)] * 2
    out_specs = [pl.BlockSpec((1, 2 * cap, s[2]), lambda j, who: (j, k, 0)) for s in saved]
    out_specs += [pl.BlockSpec((2 * length, width), lambda j, who: (who[2], 0))]
    out_specs += [pl.BlockSpec((length + EXTRA, width), whole)] * 2
    aliases = {}
    if kept is not None:
        aliases = {1 + len(args) + i: i for i in range(len(kept))}
        in_specs += [pl.BlockSpec(memory_space=pl.ANY)] * len(kept)
        args += list(kept)
    in_specs += [pl.BlockSpec(memory_space=pl.ANY)] * len(first)
    args += list(first)
    results = pl.pallas_call(
        functools.partial(expert_kernel, min(512, ff), min(1024, width), len(aliases) + len(first)),
        grid_spec=pltpu.PrefetchScalarGridSpec(
            num_scalar_prefetch=1,
            grid=(count,),
            in_specs=in_specs,
            out_specs=out_specs,
            scratch_shapes=[pltpu.VMEM((2, length, lanes), BF)] * 2,
        ),
        out_shape=out_shape,
        input_output_aliases=aliases,
        compiler_params=pltpu.CompilerParams(vmem_limit_bytes=60 * 2**20),
        cost_estimate=pl.CostEstimate(
            flops=count * 2 * cap * width * ff * 12 * 2,
            bytes_accessed=count * 3 * width * ff * 2 + 20 * length * width * 2,
            transcendentals=0,
        ),
        name="experts",
    )(who, *args)
    return results[:5], results[5], results[6]


def out_kernel(replicas, groups, who, *refs):
    pieces = refs[:replicas]
    near, far, tokens, gain = refs[replicas : replicas + 4]
    hidden, normed, mixed = refs[replicas + 4 :]
    part = pieces[0].shape[1]
    depth = near.shape[1] // (groups // 2)
    for q in range(replicas):
        mixed[:, pl.ds(pl.multiple_of((who[0] ^ q) * part, part), part)] = pieces[q][...]
    for q in range(replicas):
        total = jnp.zeros((tokens.shape[0], part), F32)
        for k in range(groups // 2):
            for flip, source in enumerate((near, far)):
                at = ((who[2] ^ flip) * (groups // 2) + k) * depth
                left = mixed[:, pl.ds(pl.multiple_of(at, depth), depth)]
                total += dot(left, source[q, k * depth : (k + 1) * depth])
        here = pl.ds(pl.multiple_of((who[0] ^ q) * part, part), part)
        hidden[:, here] = tokens[:, here].astype(F32) + total
    value = hidden[...]
    scale = lax.rsqrt(jnp.mean(value * value, axis=1, keepdims=True) + epsilon)
    normed[...] = (value * scale * gain[...]).astype(BF)


def out_step(who, pieces, near, far, tokens, gain):
    replicas = len(pieces)
    length, width = tokens.shape
    groups = lax.axis_size("fsdp")
    vmem = pl.BlockSpec(memory_space=pltpu.VMEM)
    return pl.pallas_call(
        functools.partial(out_kernel, replicas, groups),
        in_specs=[pl.BlockSpec(memory_space=pltpu.SMEM)] + [vmem] * (replicas + 4),
        out_specs=[vmem] * 3,
        out_shape=[
            jax.ShapeDtypeStruct((length, width), F32),
            jax.ShapeDtypeStruct((length, width), BF),
            jax.ShapeDtypeStruct((length, width), BF),
        ],
        compiler_params=pltpu.CompilerParams(vmem_limit_bytes=60 * 2**20),
        name="attention_out",
    )(who, *pieces, near, far, tokens, gain)


def back_kernel(replicas, groups, experts, who, *refs):
    rounds = groups // 2
    shares = refs[:rounds]
    hidden, normed, cot, gain, gates, router, near, far = refs[rounds : rounds + 8]
    grad_hidden, gain_grad, router_grad = refs[rounds + 8 : rounds + 11]
    pieces = refs[rounds + 11 : rounds + 11 + replicas]
    mixed = refs[rounds + 11 + replicas]
    length, width = hidden.shape
    lanes = router.shape[1]
    part = width // replicas
    depth = width // groups
    per_chip = experts // rounds
    line = lax.broadcasted_iota(jnp.int32, (EXTRA, lanes), 0)
    lane = lax.broadcasted_iota(jnp.int32, (EXTRA, lanes), 1)
    summed = jnp.zeros((length, width), F32)
    grad_gates = jnp.zeros((length, lanes), F32)
    for k in range(rounds):
        summed += shares[k][:length].astype(F32)
        chip = who[1] ^ k
        place = (lane == chip * per_chip + line // 2) & (line < 2 * per_chip)
        grad_gates += dot_tn(shares[k][length:, :length], place.astype(BF))
    own = gates[...]
    centered = grad_gates - jnp.sum(own * grad_gates, axis=1, keepdims=True)
    grad_logits = (own * centered).astype(BF)
    router_grad[...] = dot_tn(normed[...], grad_logits).astype(BF)
    grad_normed = summed + dot_nt(grad_logits, router[...])
    value = hidden[...]
    scale = lax.rsqrt(jnp.mean(value * value, axis=1, keepdims=True) + epsilon)
    gain_grad[...] = jnp.sum(grad_normed * value * scale, axis=0, keepdims=True)
    pulled = grad_normed * gain[...]
    inner = jnp.mean(pulled * value, axis=1, keepdims=True)
    total = cot[...].astype(F32) + scale * pulled - value * (scale * scale * scale * inner)
    grad_hidden[...] = total
    for q in range(replicas):
        here = pl.ds(pl.multiple_of((who[0] ^ q) * part, part), part)
        pieces[q][:, part:] = grad_hidden[:, here].astype(BF)
    for k in range(rounds):
        for flip, source in enumerate((near, far)):
            block = jnp.zeros((length, depth), F32)
            for q in range(replicas):
                block += dot_nt(pieces[q][:, part:], source[q, k * depth : (k + 1) * depth])
            at = ((who[2] ^ flip) * (groups // 2) + k) * depth
            mixed[:, pl.ds(pl.multiple_of(at, depth), depth)] = block.astype(BF)
    for q in range(replicas):
        here = pl.ds(pl.multiple_of((who[0] ^ q) * part, part), part)
        pieces[q][:, :part] = mixed[:, here]


def back_step(who, shares, hidden, normed, cot, gain, gates, router, near, far, experts):
    replicas = near.shape[0]
    length, width = hidden.shape
    groups = 2 * len(shares)
    vmem = pl.BlockSpec(memory_space=pltpu.VMEM)
    piece = jax.ShapeDtypeStruct((length, 2 * width // replicas), BF)
    results = pl.pallas_call(
        functools.partial(back_kernel, replicas, groups, experts),
        in_specs=[pl.BlockSpec(memory_space=pltpu.SMEM)] + [vmem] * (len(shares) + 8),
        out_specs=[vmem] * (3 + replicas),
        scratch_shapes=[pltpu.VMEM((length, width), BF)],
        out_shape=[
            jax.ShapeDtypeStruct((length, width), F32),
            jax.ShapeDtypeStruct((1, width), F32),
            jax.ShapeDtypeStruct((width, router.shape[1]), BF),
            *[piece] * replicas,
        ],
        compiler_params=pltpu.CompilerParams(vmem_limit_bytes=60 * 2**20),
        cost_estimate=pl.CostEstimate(flops=10**11, bytes_accessed=0, transcendentals=0),
        name="attention_back",
    )(who, *shares, hidden, normed, cot, gain, gates, router, near, far)
    return results[0], results[1], results[2], results[3:]


def turn(value, cosine, sine):
    return value * cosine + pltpu.roll(value, value.shape[1] // 2, 1) * sine


def attend_kernel(heads, normed, weight, seg_row, seg_col, cosine, sine, gains, *outs):
    raw, ready, mixed, totals, tops = outs
    allowed = seg_col[0] == seg_row[0]
    lane = lax.broadcasted_iota(jnp.int32, totals.shape, 1)
    top_lane = lax.broadcasted_iota(jnp.int32, tops.shape[1:], 1)
    part = heads * HD
    totals[...] = jnp.zeros(totals.shape, F32)
    tops[0] = jnp.zeros(tops.shape[1:], F32)
    for i in range(2):
        raw[:, i * part : (i + 1) * part] = dot(normed[...], weight[:, i * part : (i + 1) * part])
    ready[:, 2 * part :] = dot(normed[...], weight[:, 2 * part : 3 * part]).astype(BF)
    for h in range(heads):
        rotated = []
        for i in range(2):
            at = slice(i * part + h * HD, i * part + (h + 1) * HD)
            head = raw[:, at]
            norm = lax.rsqrt(jnp.mean(head * head, axis=1, keepdims=True) + epsilon)
            rotated.append(turn(head * norm * gains[i : i + 1], cosine[...], sine[...]).astype(BF))
            ready[:, at] = rotated[i]
        scores = dot_nt(rotated[0], rotated[1]) * HD**-0.5
        scores = jnp.where(allowed, scores, -1e30)
        peak = jnp.max(scores, axis=1, keepdims=True)
        powers = jnp.exp(scores - peak)
        total = peak + jnp.log(jnp.sum(powers, axis=1, keepdims=True))
        weights = jnp.exp(scores - total).astype(BF)
        here = slice(h * HD, (h + 1) * HD)
        mixed[:, here] = dot(weights, ready[:, 2 * part + h * HD : 2 * part + (h + 1) * HD]).astype(BF)
        totals[...] = jnp.where(lane == h, total, totals[...])
        tops[0] = jnp.where(top_lane == h, jnp.max(peak, axis=0, keepdims=True), tops[0])


def attend(normed, weight, segments, cosine, sine, gains, heads):
    count, length = segments.shape
    rows, width = normed.shape
    part = heads * HD
    one = lambda n: (n, 0)
    fixed = lambda n: (0, 0)
    return pl.pallas_call(
        functools.partial(attend_kernel, heads),
        grid=(count,),
        in_specs=[
            pl.BlockSpec((length, width), one),
            pl.BlockSpec((width, 3 * part), fixed, pipeline_mode=pl.Buffered(1)),
            pl.BlockSpec((1, 1, length), lambda n: (n, 0, 0)),
            pl.BlockSpec((1, length, 1), lambda n: (n, 0, 0)),
            pl.BlockSpec((length, HD), fixed),
            pl.BlockSpec((length, HD), fixed),
            pl.BlockSpec((2, HD), fixed),
        ],
        out_specs=[
            pl.BlockSpec((length, 2 * part), one),
            pl.BlockSpec((length, 3 * part), one),
            pl.BlockSpec((length, part), one),
            pl.BlockSpec((length, 128), one),
            pl.BlockSpec((1, 1, 128), lambda n: (n, 0, 0)),
        ],
        out_shape=[
            jax.ShapeDtypeStruct((rows, 2 * part), F32),
            jax.ShapeDtypeStruct((rows, 3 * part), BF),
            jax.ShapeDtypeStruct((rows, part), BF),
            jax.ShapeDtypeStruct((rows, 128), F32),
            jax.ShapeDtypeStruct((count, 1, 128), F32),
        ],
        compiler_params=pltpu.CompilerParams(vmem_limit_bytes=60 * 2**20),
        cost_estimate=pl.CostEstimate(flops=0, bytes_accessed=0, transcendentals=0),
        name="attention",
    )(normed, weight, segments[:, None, :], segments[:, :, None], cosine, sine, gains)


def attend_back_kernel(heads, pull, raw, ready, totals, seg_row, seg_col, cosine, sine, gains, grad, gain_grads):
    allowed = seg_col[0] == seg_row[0]
    lane = lax.broadcasted_iota(jnp.int32, totals.shape, 1)
    part = heads * HD
    sums = [jnp.zeros((1, HD), F32)] * 2
    for h in range(heads):
        at = [slice(i * part + h * HD, i * part + (h + 1) * HD) for i in range(3)]
        query, key, value = (ready[:, a] for a in at)
        pulled = pull[:, h * HD : (h + 1) * HD]
        total = jnp.sum(jnp.where(lane == h, totals[...], 0.0), axis=1, keepdims=True)
        scores = dot_nt(query, key) * HD**-0.5
        probs = jnp.where(allowed, jnp.exp(jnp.where(allowed, scores - total, 0.0)), 0.0)
        grad_weights = dot_nt(pulled, value)
        grad[:, at[2]] = dot_tn(probs.astype(BF), pulled).astype(BF)
        inner = jnp.sum(probs * grad_weights, axis=1, keepdims=True)
        grad_scores = (probs * (grad_weights - inner)).astype(BF)
        both = (dot(grad_scores, key), dot_tn(grad_scores, query))
        for i, g in enumerate(both):
            g = g * HD**-0.5
            back = g * cosine[...] - pltpu.roll(g, HD // 2, 1) * sine[...]
            head = raw[:, at[i]]
            norm = lax.rsqrt(jnp.mean(head * head, axis=1, keepdims=True) + epsilon)
            sums[i] = sums[i] + jnp.sum(back * head * norm, axis=0, keepdims=True)
            scaled = back * gains[i : i + 1]
            mean = jnp.mean(scaled * head, axis=1, keepdims=True)
            grad[:, at[i]] = (norm * scaled - head * (norm * norm * norm * mean)).astype(BF)
    for i in range(2):
        gain_grads[0, i : i + 1] = sums[i]


def attend_back(pull, raw, ready, totals, segments, cosine, sine, gains, heads):
    count, length = segments.shape
    rows = raw.shape[0]
    part = heads * HD
    one = lambda n: (n, 0)
    fixed = lambda n: (0, 0)
    return pl.pallas_call(
        functools.partial(attend_back_kernel, heads),
        grid=(count,),
        in_specs=[
            pl.BlockSpec((length, part), one),
            pl.BlockSpec((length, 2 * part), one),
            pl.BlockSpec((length, 3 * part), one),
            pl.BlockSpec((length, 128), one),
            pl.BlockSpec((1, 1, length), lambda n: (n, 0, 0)),
            pl.BlockSpec((1, length, 1), lambda n: (n, 0, 0)),
            pl.BlockSpec((length, HD), fixed),
            pl.BlockSpec((length, HD), fixed),
            pl.BlockSpec((2, HD), fixed),
        ],
        out_specs=[
            pl.BlockSpec((length, 3 * part), one),
            pl.BlockSpec((1, 2, HD), lambda n: (n, 0, 0)),
        ],
        out_shape=[
            jax.ShapeDtypeStruct((rows, 3 * part), BF),
            jax.ShapeDtypeStruct((count, 2, HD), F32),
        ],
        compiler_params=pltpu.CompilerParams(vmem_limit_bytes=32 * 2**20),
        cost_estimate=pl.CostEstimate(
            flops=0, bytes_accessed=0, transcendentals=0
        ),
        name="attention_grad",
    )(pull, raw, ready, totals, segments[:, None, :], segments[:, :, None], cosine, sine, gains)


def weight_grad_kernel(half, quarters, left, right, *outs):
    j, i = pl.program_id(0), pl.program_id(1)
    block = dot_tn(left[0], right[0]).astype(BF)
    for at, out in enumerate(outs):

        @pl.when((j == at // 2) & ((i >= half) == (at % 2 == 1)))
        def _(out=out):
            out[0] = block


def weight_grads(quarters, left, right, parts, cost):
    count, rows, width = left.shape
    size, n = width // parts, right.shape[2]
    half = parts // 2

    def spot(at):
        def index(j, i, quarters):
            step = j * parts + i - (at // 2 * parts + at % 2 * half)
            return (jnp.clip(step, 0, half - 1), 0, 0)

        return index

    return pl.pallas_call(
        functools.partial(weight_grad_kernel, half),
        grid_spec=pltpu.PrefetchScalarGridSpec(
            num_scalar_prefetch=1,
            grid=(count, parts),
            in_specs=[
                pl.BlockSpec((1, rows, size), lambda j, i, quarters: (j, 0, quarters[j, i])),
                pl.BlockSpec((1, rows, n), lambda j, i, quarters: (j, 0, 0)),
            ],
            out_specs=[pl.BlockSpec((1, size, n), spot(at)) for at in range(2 * count)],
        ),
        out_shape=[jax.ShapeDtypeStruct((half, size, n), BF)] * (2 * count),
        compiler_params=pltpu.CompilerParams(vmem_limit_bytes=56 * 2**20),
        cost_estimate=pl.CostEstimate(flops=cost, bytes_accessed=0, transcendentals=0),
        name="weight_grads",
    )(quarters, left, right)


def product_kernel(left, right, out):
    out[...] = dot_tn(left[...], right[...]).astype(BF)


def product(left, right):
    rows, width = left.shape
    n = right.shape[1]
    size = min(width, 256)
    return pl.pallas_call(
        product_kernel,
        grid=(width // size,),
        in_specs=[
            pl.BlockSpec((rows, size), lambda i: (0, i)),
            pl.BlockSpec((rows, n), lambda i: (0, 0)),
        ],
        out_specs=pl.BlockSpec((size, n), lambda i: (i, 0)),
        out_shape=jax.ShapeDtypeStruct((width, n), BF),
        compiler_params=pltpu.CompilerParams(vmem_limit_bytes=32 * 2**20),
        cost_estimate=pl.CostEstimate(flops=0, bytes_accessed=0, transcendentals=0),
        name="product",
    )(left, right)


def spread_kernel(grad, weight, *outs):
    block = dot_nt(grad[...], weight[...]).astype(BF)
    for at, out in enumerate(outs):

        @pl.when(pl.program_id(0) == at)
        def _(out=out):
            out[...] = block


def normed_grads(grad, weight, count):
    rows, n = grad.shape
    width = weight.shape[0]
    length = rows // count
    return pl.pallas_call(
        spread_kernel,
        grid=(count,),
        in_specs=[
            pl.BlockSpec((length, n), lambda i: (i, 0)),
            pl.BlockSpec((width, n), lambda i: (0, 0), pipeline_mode=pl.Buffered(1)),
        ],
        out_specs=[pl.BlockSpec((length, width), lambda i: (0, 0))] * count,
        out_shape=[jax.ShapeDtypeStruct((length, width), BF)] * count,
        compiler_params=pltpu.CompilerParams(vmem_limit_bytes=48 * 2**20),
        cost_estimate=pl.CostEstimate(flops=0, bytes_accessed=0, transcendentals=0),
        name="normed_grads",
    )(grad, weight)


def halve_kernel(half, blocks, keep, got, send_out, keep_out):
    block = (keep[0].astype(F32) + got[0].astype(F32)).astype(BF)

    @pl.when(pl.program_id(0) < half)
    def _():
        send_out[0] = block

    @pl.when(pl.program_id(0) >= half)
    def _():
        keep_out[0] = block


def halve(blocks, keep, got, cost):
    count, size, n = keep.shape
    half = count // 2
    here = pl.BlockSpec((1, size, n), lambda i, blocks: (blocks[i], 0, 0))
    return pl.pallas_call(
        functools.partial(halve_kernel, half),
        grid_spec=pltpu.PrefetchScalarGridSpec(
            num_scalar_prefetch=1,
            grid=(count,),
            in_specs=[here, here],
            out_specs=[
                pl.BlockSpec((1, size, n), lambda i, blocks: (jnp.minimum(i, half - 1), 0, 0)),
                pl.BlockSpec((1, size, n), lambda i, blocks: (jnp.maximum(i - half, 0), 0, 0)),
            ],
        ),
        out_shape=[jax.ShapeDtypeStruct((half, size, n), BF)] * 2,
        compiler_params=pltpu.CompilerParams(vmem_limit_bytes=32 * 2**20),
        cost_estimate=pl.CostEstimate(flops=cost, bytes_accessed=0, transcendentals=0),
        name="halve",
    )(blocks, keep, got)


def join_kernel(*refs):
    out = refs[-1]
    for j in range((len(refs) - 1) // 2):

        @pl.when(pl.program_id(0) == j)
        def _(j=j):
            out[0] = refs[2 * j][...].astype(F32) + refs[2 * j + 1][...].astype(F32)


def join(pairs, cost):
    size, n = pairs[0][0].shape
    step = min(size, 256)
    count = len(pairs)

    def spot(at):
        def index(j, i):
            k = j * (size // step) + i - at * (size // step)
            return (jnp.clip(k, 0, size // step - 1), 0)

        return index

    return pl.pallas_call(
        join_kernel,
        grid=(count, size // step),
        in_specs=[pl.BlockSpec((step, n), spot(at // 2)) for at in range(2 * count)],
        out_specs=pl.BlockSpec((1, step, n), lambda j, i: (j, i, 0)),
        out_shape=jax.ShapeDtypeStruct((count, size, n), F32),
        compiler_params=pltpu.CompilerParams(vmem_limit_bytes=60 * 2**20),
        cost_estimate=pl.CostEstimate(flops=cost, bytes_accessed=0, transcendentals=0),
        name="join",
    )(*[v for pair in pairs for v in pair])


def input_kernel(count, heads, who, *refs):
    pieces = refs[:count]
    tokens, gain, grad_hidden, ffn, gains, tops, grad, small = refs[count:]
    width = tokens.shape[1]
    pulled = pieces[0][...].astype(F32)
    for piece in pieces[1:]:
        pulled = pulled + piece[...].astype(F32)
    value = tokens[...].astype(F32)
    scale = lax.rsqrt(jnp.mean(value * value, axis=1, keepdims=True) + epsilon)
    small[:, :width] = jnp.sum(pulled * value * scale, axis=0, keepdims=True)
    small[:, width : 2 * width] = ffn[...]
    for i in range(2):
        at = 2 * width + i * HD
        small[:, at : at + HD] = jnp.sum(gains[:, i], axis=0, keepdims=True)
    top = jnp.max(tops[:, 0], axis=0, keepdims=True)
    lane = lax.broadcasted_iota(jnp.int32, top.shape, 1)
    top = jnp.where(lane < heads, top, -3e38)
    small[:, 2 * width + 2 * HD :] = pltpu.roll(top, who[0] * heads, 1)
    pulled = pulled * gain[...]
    inner = jnp.mean(pulled * value, axis=1, keepdims=True)
    back = scale * pulled - value * (scale * scale * scale * inner)
    grad[...] = (grad_hidden[...] + back).astype(BF)


def input_step(who, pieces, tokens, gain, grad_hidden, ffn, gains, tops, heads):
    length, width = tokens.shape
    vmem = pl.BlockSpec(memory_space=pltpu.VMEM)
    return pl.pallas_call(
        functools.partial(input_kernel, len(pieces), heads),
        in_specs=[pl.BlockSpec(memory_space=pltpu.SMEM)] + [vmem] * (len(pieces) + 6),
        out_specs=[vmem] * 2,
        out_shape=[
            jax.ShapeDtypeStruct((length, width), BF),
            jax.ShapeDtypeStruct((1, 2 * width + 2 * HD + 128), F32),
        ],
        compiler_params=pltpu.CompilerParams(vmem_limit_bytes=60 * 2**20),
        cost_estimate=pl.CostEstimate(flops=10**11, bytes_accessed=0, transcendentals=0),
        name="input_grad",
    )(who, *pieces, tokens, gain, grad_hidden, ffn, gains, tops)


def gather_kernel(count, arrays, who, *refs):
    blocks, outs = refs[:count], refs[count:]
    part = outs[0].shape[1] // count
    total = 0.0
    for k, block in enumerate(blocks):
        here = pl.ds(pl.multiple_of((who[0] ^ k) * part, part), part)
        for i in range(arrays):
            outs[i][:, here] = block[:, i * part : (i + 1) * part].astype(F32)
        if len(outs) > arrays:
            total += block[:, arrays * part :].astype(F32)
    if len(outs) > arrays:
        outs[-1][...] = total


def gather_step(who, blocks, arrays):
    rows, wide = blocks[0].shape
    lanes = 128 if wide % (arrays * 256) else 0
    part = (wide - lanes) // arrays
    count = len(blocks)
    vmem = pl.BlockSpec(memory_space=pltpu.VMEM)
    return pl.pallas_call(
        functools.partial(gather_kernel, count, arrays),
        in_specs=[pl.BlockSpec(memory_space=pltpu.SMEM)] + [vmem] * count,
        out_specs=[vmem] * (arrays + (lanes > 0)),
        out_shape=[jax.ShapeDtypeStruct((rows, part * count), F32)] * arrays
        + [jax.ShapeDtypeStruct((rows, lanes), F32)] * (lanes > 0),
        compiler_params=pltpu.CompilerParams(vmem_limit_bytes=48 * 2**20),
        cost_estimate=pl.CostEstimate(flops=0, bytes_accessed=0, transcendentals=0),
        name="gather_columns",
    )(who, *blocks)


def merge_kernel(sums, *refs):
    out = refs[-1]
    total = refs[0][...]
    lane = lax.broadcasted_iota(jnp.int32, total.shape, 1)
    for ref in refs[1:-1]:
        other = ref[...]
        total = jnp.where(lane < sums, total + other, jnp.maximum(total, other))
    out[...] = total


def merge(sums, *values):
    vmem = pl.BlockSpec(memory_space=pltpu.VMEM)
    return pl.pallas_call(
        functools.partial(merge_kernel, sums),
        in_specs=[vmem] * len(values),
        out_specs=vmem,
        out_shape=jax.ShapeDtypeStruct(values[0].shape, F32),
        cost_estimate=pl.CostEstimate(flops=0, bytes_accessed=0, transcendentals=0),
        name="merge",
    )(*values)


def local(
    tokens,
    cotangent,
    segment_ids,
    expert_index,
    clip_threshold,
    attn_norm_gain,
    w_query,
    w_key,
    w_value,
    w_output,
    query_gain,
    key_gain,
    ffn_norm_gain,
    router,
    expert_in,
    expert_out,
):
    replicas = lax.axis_size("replica")
    groups = lax.axis_size("fsdp")
    me_r = lax.axis_index("replica")
    me_f = lax.axis_index("fsdp")
    core = me_f % 2
    length, width = tokens.shape
    part = width // replicas
    heads = part // HD
    ff = expert_out.shape[1]
    local_experts = expert_in.shape[0]
    scale = HD ** (-0.5)
    attn_gain = attn_norm_gain.astype(F32)
    ffn_gain = ffn_norm_gain.astype(F32)
    gain_query = query_gain.astype(F32)
    gain_key = key_gain.astype(F32)

    def swap(value, k):
        return lax.ppermute(value, "replica", [(r, r ^ k) for r in range(replicas)])

    def columns(value, k, axis=1):
        return lax.dynamic_slice_in_dim(value, (me_r ^ k) * part, part, axis)

    def spread(value):
        return [value] + [swap(value, k) for k in range(1, replicas)]

    def trade_columns(value):
        return [columns(value, 0)] + [swap(columns(value, k), k) for k in range(1, replicas)]

    def join_columns(blocks):
        out = jnp.zeros((blocks[0].shape[0], part * replicas), blocks[0].dtype)
        for k, block in enumerate(blocks):
            out = lax.dynamic_update_slice_in_dim(out, block, (me_r ^ k) * part, 1)
        return out

    def cross(value, k):
        return lax.ppermute(value, "fsdp", [(f, f ^ k) for f in range(groups)])

    def pass_on(up, down, hop):
        chips = groups // 2
        pairs = [(2 * a + i, 2 * a + 2 + i) for a in range(hop - 1, chips - 1) for i in (0, 1)]
        back = [(2 * a + 2 + i, 2 * a + i) for a in range(chips - hop) for i in (0, 1)]
        return lax.ppermute(up, "fsdp", pairs), lax.ppermute(down, "fsdp", back)

    def choose(up, down, k):
        chips = groups // 2
        found = {}
        for a in range(chips):
            b = a ^ k
            found.setdefault((b > a, abs(b - a)), []).append(a)
        picked = None
        for (above, hop), at in found.items():
            source = down[hop] if above else up[hop]
            if picked is None:
                picked = source
            else:
                here = functools.reduce(jnp.logical_or, [me_f // 2 == a for a in at])
                picked = jnp.where(here, source, picked)
        return picked

    def gather(value):
        return lax.all_gather(value, "fsdp", axis=0, tiled=True)

    def reduce(value):
        return lax.psum_scatter(value, "fsdp", scatter_dimension=0, tiled=True)

    bits = replicas.bit_length() - 1

    def next_bit(j, step):
        return 1 << (bits - 1 - step if j % 2 else step)

    def next_halves(traded, j, step, cost=0):
        keep, got = traded
        left = keep.shape[0]
        place = jnp.arange(left, dtype=jnp.int32)
        here = left // 2 if j % 2 else 1
        mine = (me_r & next_bit(j, step)) != 0
        other = ((place & here) != 0) != mine
        spots = jnp.where(other, jnp.cumsum(other) - 1, left // 2 + jnp.cumsum(~other) - 1)
        return halve(jnp.zeros((left,), jnp.int32).at[spots].set(place), keep, got, cost)

    index_table = expert_index.astype(BF).reshape(w_query.shape[0], -1)
    sent = [columns(w_output, 0), router, index_table]
    sizes = [v.shape[1] for v in sent]
    sent.append(jnp.zeros((w_query.shape[0], -sum(sizes) % 128), BF))
    quarter = gather(jnp.concatenate(sent, axis=1))
    full_router = quarter[:, part : part + EXPERTS]
    full_index = quarter[:, part + EXPERTS : part + EXPERTS + sizes[2]].astype(jnp.int32)
    full_index = full_index.reshape(groups * length, -1)
    ids = jnp.arange(EXPERTS, dtype=jnp.int32)
    mask = jnp.any(full_index[:, :, None] == ids, axis=1).reshape(groups, length, EXPERTS)
    first = me_f * local_experts
    hot = lax.dynamic_slice_in_dim(mask, first, local_experts, 2)
    order = jnp.arange(length, dtype=jnp.int32)
    before = (order[:, None] < order[None, :]).astype(BF)
    rank = jnp.einsum("nsj,st->njt", hot.astype(BF), before, preferred_element_type=F32)
    rank = jnp.where(hot.transpose(0, 2, 1), rank.astype(jnp.int32), -1)
    slots = jnp.arange(CAP, dtype=jnp.int32)
    pick = (rank[:, :, None, :] == slots[:, None]).astype(BF)
    spots = (rank[:, :, :, None] == slots).astype(BF)
    lanes = 128
    mask_wide = jnp.pad(mask.astype(F32), ((0, 0), (0, 0), (0, lanes - EXPERTS)))
    router_wide = jnp.pad(full_router, ((0, 0), (0, lanes - EXPERTS)))
    tables = (pick, spots, mask_wide, router_wide)
    segments = spread(segment_ids)
    tokens_all = spread(after(tokens, *segments[1:]))
    segments = jnp.concatenate(segments, axis=0)
    normed = jnp.concatenate(
        [rms_norm(v.astype(F32), attn_gain).astype(BF) for v in tokens_all], axis=0
    )
    rounds = groups // 2
    where = jnp.stack([me_r, me_f // 2, core]).astype(jnp.int32)
    half = lax.dynamic_slice(quarter, (core * (width // 2), 0), (width // 2, part))
    near = spread(after(half, *tokens_all[1:]))
    near[1] = after(near[1], *tables, segments, normed)
    normed = after(normed, *near[1:])
    w_qkv = gather(jnp.concatenate([columns(w, 0) for w in (w_query, w_key, w_value)], axis=1))
    cot_all = gather(cotangent)
    cot_pair = (cotangent, cross(cotangent, 1))

    cosine, sine = rope_tables(length, HD)
    cosine = jnp.concatenate([cosine, cosine], axis=1)
    sine = jnp.concatenate([-sine, sine], axis=1)
    gains = jnp.stack([gain_query, gain_key])
    raw, ready, mixed_heads, totals, tops = attend(normed, w_qkv, segments, cosine, sine, gains, heads
    )
    near = jnp.stack([after(near[0], raw), *near[1:]])
    far = cross(near, 1)
    mixed_heads = mixed_heads.reshape(replicas, length, part)
    pieces = [mixed_heads[0]] + [swap(mixed_heads[k], k) for k in range(1, replicas)]
    inputs = tokens.astype(F32)
    hidden, normed_ffn, mixed = out_step(where, pieces, near, far, tokens, ffn_gain[None, :])
    mixed_all = spread(mixed)

    def first_bit(j):
        return 1 << (bits - 1 if j % 2 else 0)

    numbers = jnp.arange(replicas, dtype=jnp.int32)
    quarters = []
    for j in range(local_experts):
        other = ((numbers ^ me_r) & first_bit(j)) != 0
        place = jnp.where(other, jnp.cumsum(other) - 1, replicas // 2 + jnp.cumsum(~other) - 1)
        quarters.append(jnp.zeros((replicas,), jnp.int32).at[place].set(numbers))
    quarters = jnp.stack(quarters)
    kept = None
    shares = []
    added = []
    pending = []
    up, down = [normed_ffn], [normed_ffn]
    for k in range(rounds):
        chip = (me_f // 2) ^ k
        who = jnp.stack([2 * chip + core, 2 * chip + 1 - core, chip, core, first])
        if k + 1 < rounds:
            next_up, next_down = pass_on(up[-1], down[-1], k + 1)
        mine = choose(up, down, k) if k else normed_ffn
        nf = (mine, cross(mine, 1))
        kept, back_a, back_b = expert_block(k, rounds, who, nf, (cot_all,) if k else cot_pair, pick, spots, mask_wide, router_wide, expert_in, expert_out, kept, pending
        )
        if k + 1 < rounds:
            up.append(after(next_up, back_a))
            down.append(after(next_down, back_a))
        else:
            rows, grad_projected, cot_rows, scaled, moe = kept
            out_blocks = weight_grads(quarters, after(scaled, mixed_all[-1]), cot_rows, replicas, 0)
        if k == rounds - 1:
            back_b = after(back_b, *out_blocks, *shares[1:])
        share = (back_a.astype(F32) + cross(back_b, 1).astype(F32)).astype(BF)
        added.append(share)
        if k == rounds - 2:
            pending = added[1:]
        else:
            pending = mixed_all[1:-1] if k == rounds - 3 else []
        shares.append(share if k == 0 else cross(share, 2 * k))
    out_traded = [
        (out_blocks[2 * j + 1], swap(out_blocks[2 * j], first_bit(j))) for j in range(local_experts)
    ]
    in_blocks = weight_grads(quarters, after(rows, share), grad_projected, replicas, 10**11)
    shares[-1] = after(shares[-1], *in_blocks, *[v[1] for v in out_traded])
    moe_sum = reduce(after(moe, shares[-1]))
    output = (hidden + moe_sum.astype(F32)).astype(BF)

    my_mask = lax.dynamic_index_in_dim(mask_wide, me_f, 0, keepdims=False) > 0.0
    logits = jnp.where(my_mask, dot(normed_ffn, router_wide), -jnp.inf)
    powers = jnp.exp(logits - jnp.max(logits, axis=1, keepdims=True))
    my_gates = powers / jnp.sum(powers, axis=1, keepdims=True)
    grad_hidden, ffn_gain_grad, router_grad, pieces = back_step(
        where, shares, hidden, normed_ffn, cotangent, ffn_gain[None, :], my_gates, router_wide, near, far, EXPERTS
    )
    grad_mixed = jnp.concatenate(
        [pieces[0]] + [swap(pieces[k], k) for k in range(1, replicas)], axis=0
    )
    sends = [
        after(in_blocks[2 * j], grad_mixed, *[v[1] for v in out_traded]) for j in range(local_experts)
    ]
    in_traded = [
        (in_blocks[2 * j + 1], swap(v, first_bit(j))) for j, v in enumerate(sends)
    ]
    ready = after(ready, *sends)
    grad_qkv, gain_grads = attend_back(grad_mixed, raw, ready, totals, segments, cosine, sine, gains, heads
    )
    qkv_grad = product(normed, grad_qkv)
    part_normed = normed_grads(grad_qkv, w_qkv, replicas)
    received = [v[1] for v in in_traded]
    received[0] = after(received[0], *received[1:], moe_sum)
    in_traded = [(v[0], got) for v, got in zip(in_traded, received)]
    in_halves = [next_halves(v, j, 1, 10**11) for j, v in enumerate(in_traded)]
    in_sends = [v for v, _ in in_halves]
    in_done = [(keep, swap(v, next_bit(j, 1))) for j, (v, keep) in enumerate(in_halves)]
    mixed_rows = jnp.concatenate([mixed_all[0], after(mixed_all[1], *in_sends), *mixed_all[2:]], axis=0)
    output_grad = dot_tn(mixed_rows, grad_mixed[:, part:])
    o_grad = jnp.concatenate([output_grad.astype(BF), router_grad], axis=1)
    share_o = reduce(o_grad)
    out_halves = [next_halves((k, after(v, part_normed[0])), j, 1) for j, (k, v) in enumerate(out_traded)]
    pieces = [after(part_normed[0], *in_sends, o_grad, *[v for v, _ in out_halves])]
    pieces += [swap(part_normed[k], k) for k in range(1, replicas)]
    input_grad, small = input_step(
        where, pieces, tokens, attn_gain[None, :], grad_hidden, ffn_gain_grad, gain_grads, tops, heads
    )
    second = [v[1] for v in in_done]
    share_qkv = reduce(qkv_grad)
    blocks = spread(after(jnp.concatenate([share_qkv, share_o], axis=1), *second, input_grad))
    out_done = [
        (keep, swap(after(v, *second, moe_sum), next_bit(j, 1))) for j, (v, keep) in enumerate(out_halves)
    ]

    def settle(traded, cost):
        pairs = []
        for j, (keep, got) in enumerate(traded):
            for step in range(2, bits):
                send, keep = next_halves((keep, got), j, step)
                got = swap(send, next_bit(j, step))
            pairs.append((keep[0], got[0]))
        return join(pairs, cost)

    n_sums = 2 * width + 2 * HD
    small = merge(n_sums, small, cross(small, 1))
    small = merge(n_sums, small, *[cross(small, 2 * k) for k in range(1, rounds)])
    small = merge(n_sums, *spread(after(small, *second)))
    small = small[0]
    attn_gain_total = small[:width]
    ffn_gain_total = small[width : 2 * width]
    query_gain_total = small[2 * width : 2 * width + HD]
    key_gain_total = small[2 * width + HD : n_sums]
    head_max = small[n_sums : n_sums + replicas * heads]
    threshold = clip_threshold.astype(F32)
    factor = threshold / jnp.maximum(head_max, threshold)
    column_scale = jnp.repeat(jnp.sqrt(factor), HD)
    clipped_query = (w_query.astype(F32) * column_scale[None, :]).astype(BF)
    clipped_key = (w_key.astype(F32) * column_scale[None, :]).astype(BF)
    expert_in_grad = settle(
        [(keep, after(v, clipped_query, clipped_key, output)) for keep, v in in_done], 10**11
    )
    expert_out_grad = settle([(k, after(v, expert_in_grad)) for k, v in out_done], 0)

    blocks[1] = after(blocks[1], expert_in_grad)
    total_query, total_key, total_value, total_output, total_router = gather_step(where, blocks, 4)
    total_router = total_router[:, :EXPERTS]
    return (
        output,
        input_grad,
        attn_gain_total,
        total_query,
        total_key,
        total_value,
        total_output,
        query_gain_total,
        key_gain_total,
        ffn_gain_total,
        total_router,
        expert_in_grad,
        expert_out_grad,
        head_max,
        clipped_query,
        clipped_key,
    )


def solution(mesh):
    both = ("replica", "fsdp")
    return jax.shard_map(
        local,
        mesh=mesh,
        in_specs=(
            P(both, None),
            P(both, None),
            P(both, None),
            P(both, None),
            P(),
            P(),
            P("fsdp", None),
            P("fsdp", None),
            P("fsdp", None),
            P("fsdp", None),
            P(),
            P(),
            P(),
            P("fsdp", None),
            P("fsdp", None, None),
            P("fsdp", None, None),
        ),
        out_specs=(
            P(both, None),
            P(both, None),
            P(),
            P("fsdp", None),
            P("fsdp", None),
            P("fsdp", None),
            P("fsdp", None),
            P(),
            P(),
            P(),
            P("fsdp", None),
            P("fsdp", "replica", None),
            P("fsdp", "replica", None),
            P(),
            P("fsdp", None),
            P("fsdp", None),
        ),
        check_vma=False,
    )
```

```python
import functools

import jax
import jax.numpy as jnp
from jax import lax
from jax.experimental import pallas as pl
from jax.experimental.pallas import tpu as pltpu
from jax.sharding import PartitionSpec as P

HD = 128
EXPERTS = 16
CAP = 144

epsilon = 1e-06
rope_base = 10000.0
BF = jnp.bfloat16
F32 = jnp.float32


def rms_norm(values, gain):
    return values * lax.rsqrt(jnp.mean(values * values, axis=-1, keepdims=True) + epsilon) * gain


def rope_tables(length, width):
    places = jnp.arange(length, dtype=F32)
    rates = rope_base ** (-jnp.arange(width // 2, dtype=F32) * 2.0 / width)
    angle = places[:, None] * rates[None, :]
    return jnp.cos(angle), jnp.sin(angle)


def rotate(values, cosine, sine):
    half = values.shape[-1] // 2
    first = values[..., :half]
    second = values[..., half:]
    return jnp.concatenate(
        [first * cosine - second * sine, second * cosine + first * sine], axis=-1
    )


def dot(left, right):
    return jnp.dot(left, right, preferred_element_type=F32)


def dot_tn(left, right):
    return lax.dot_general(left, right, (((0,), (0,)), ((), ())), preferred_element_type=F32)


def dot_nt(left, right):
    return lax.dot_general(left, right, (((1,), (1,)), ((), ())), preferred_element_type=F32)


EXTRA = 16


def nothing(*refs):
    pass


def after(value, *others):
    held = pl.BlockSpec(memory_space=pl.ANY)
    return pl.pallas_call(
        nothing,
        in_specs=[held] * (1 + len(others)),
        out_specs=held,
        out_shape=jax.ShapeDtypeStruct(value.shape, value.dtype),
        input_output_aliases={0: 0},
        name="after",
    )(value, *others)


def expert_kernel(tile, wide, unread, who, *refs):
    (nf_a, nf_b, cot_a, cot_b, pick_a, pick_b, spread_a, spread_b) = refs[:8]
    (mask_a, mask_b, router, w_in, w_out) = refs[8:13]
    refs = refs[13 + unread :]
    rows, gp, cot_rows, scaled, moe, back_a, back_b, gates_hi, gates_lo = refs
    j = pl.program_id(0)
    cap = pick_a.shape[2]
    length = nf_a.shape[0]
    ff = w_out.shape[1]
    core, expert = who[3], who[4] + j

    @pl.when(j == 0)
    def _():
        for at, (nf, mask) in enumerate(((nf_a, mask_a), (nf_b, mask_b))):
            seen = mask[0] > 0.0
            logits = jnp.where(seen, dot(nf[...], router[...]), -1e30)
            powers = jnp.where(seen, jnp.exp(logits - jnp.max(logits, axis=1, keepdims=True)), 0.0)
            gates = powers / jnp.sum(powers, axis=1, keepdims=True)
            high = gates.astype(BF)
            gates_hi[at] = high
            gates_lo[at] = (gates - high.astype(F32)).astype(BF)

    pa, pb = pick_a[0, 0], pick_b[0, 0]
    lane = lax.broadcasted_iota(jnp.int32, (cap, router.shape[1]), 1)

    def slot_gates(p, at):
        every = dot(p, gates_hi[at]) + dot(p, gates_lo[at])
        return jnp.sum(jnp.where(lane == expert, every, 0.0), axis=1, keepdims=True)

    gate = jnp.concatenate([slot_gates(pa, 0), slot_gates(pb, 1)], axis=0)
    rows[0, :cap] = dot(pa, nf_a[...]).astype(BF)
    rows[0, cap:] = dot(pb, nf_b[...]).astype(BF)
    cot_rows[0, :cap] = dot(pa, cot_a[...]).astype(BF)
    cot_rows[0, cap:] = dot(pb, cot_b[...]).astype(BF)

    def forward(t, total):
        at = pl.multiple_of(t * tile, tile)
        g = dot(rows[0], w_in[0, :, pl.ds(at, tile)])
        u = dot(rows[0], w_in[0, :, pl.ds(ff + at, tile)])
        pulled = dot_nt(cot_rows[0], w_out[0, pl.ds(at, tile), :])
        sigma = jax.nn.sigmoid(g)
        silu = g * sigma
        active = silu * u
        scaled[0, :, pl.ds(at, tile)] = (active * gate).astype(BF)
        ga = pulled * gate
        gp[0, :, pl.ds(at, tile)] = (ga * u * sigma * (1.0 + g * (1.0 - sigma))).astype(BF)
        gp[0, :, pl.ds(ff + at, tile)] = (ga * silu).astype(BF)
        return total + jnp.sum(active * pulled, axis=1, keepdims=True)

    total = lax.fori_loop(0, ff // tile, forward, jnp.zeros((2 * cap, 1), F32))
    line = lax.broadcasted_iota(jnp.int32, (EXTRA, length), 0)
    place = 2 * (core * pl.num_programs(0) + j)
    for back, p, part in ((back_a, pa, total[:cap]), (back_b, pb, total[cap:])):
        by_token = jnp.sum(p.astype(F32) * part, axis=0, keepdims=True)
        high = by_token.astype(BF).astype(F32)
        new = jnp.where(line == place, high, jnp.where(line == place + 1, by_token - high, 0.0))

        @pl.when(j == 0)
        def _(back=back):
            back[length:, :] = jnp.zeros((EXTRA, back.shape[1]), BF)

        old = back[length:, :length].astype(F32)
        back[length:, :length] = (old + new).astype(BF)
    sa, sb = spread_a[0, 0], spread_b[0, 0]
    moe_a = pl.ds(pl.multiple_of(core * length, length), length)
    moe_b = pl.ds(pl.multiple_of((1 - core) * length, length), length)

    def backward(t, _):
        here = pl.ds(pl.multiple_of(t * wide, wide), wide)
        gr = dot_nt(gp[0], w_in[0, here, :]).astype(BF)
        res = dot(scaled[0], w_out[0, :, here]).astype(BF)
        for out, where, s, value in (
            (back_a, pl.ds(0, length), sa, gr[:cap]),
            (back_b, pl.ds(0, length), sb, gr[cap:]),
            (moe, moe_a, sa, res[:cap]),
            (moe, moe_b, sb, res[cap:]),
        ):
            old = jnp.where(j > 0, out[where, here].astype(F32), 0.0)
            out[where, here] = (dot(s, value) + old).astype(BF)
        return 0

    lax.fori_loop(0, w_in.shape[1] // wide, backward, 0)


def expert_block(k, rounds, who, nf, cot, pick, spread, mask, router, w_in, w_out, kept, first):
    length, width = nf[0].shape
    count, _, two_ff = w_in.shape
    groups = pick.shape[0]
    ff = two_ff // 2
    cap = pick.shape[2]
    lanes = router.shape[1]

    def whole(j, who):
        return (0, 0)

    def seq(i):
        return lambda j, who: (who[i], j, 0, 0)

    in_specs = [pl.BlockSpec((length, width), whole)] * 2
    if len(cot) == 2:
        in_specs += [pl.BlockSpec((length, width), whole)] * 2
    else:
        cot = [cot[0]] * 2
        in_specs += [
            pl.BlockSpec((length, width), lambda j, who, i=i: (who[i], 0)) for i in range(2)
        ]
    in_specs += [pl.BlockSpec((1, 1, cap, length), seq(i)) for i in range(2)]
    in_specs += [pl.BlockSpec((1, 1, length, cap), seq(i)) for i in range(2)]
    in_specs += [
        pl.BlockSpec((1, length, lanes), lambda j, who, i=i: (who[i], 0, 0)) for i in range(2)
    ]
    in_specs += [
        pl.BlockSpec((width, lanes), whole),
        pl.BlockSpec((1, width, two_ff), lambda j, who: (j, 0, 0)),
        pl.BlockSpec((1, ff, width), lambda j, who: (j, 0, 0)),
    ]
    args = [*nf, *cot, pick, pick, spread, spread, mask, mask, router, w_in, w_out]
    total = rounds * 2 * cap
    saved = [(count, total, n) for n in (width, two_ff, width, ff)]
    out_shape = [jax.ShapeDtypeStruct(s, BF) for s in saved]
    out_shape += [jax.ShapeDtypeStruct((groups * length, width), BF)]
    out_shape += [jax.ShapeDtypeStruct((length + EXTRA, width), BF)] * 2
    out_specs = [pl.BlockSpec((1, 2 * cap, s[2]), lambda j, who: (j, k, 0)) for s in saved]
    out_specs += [pl.BlockSpec((2 * length, width), lambda j, who: (who[2], 0))]
    out_specs += [pl.BlockSpec((length + EXTRA, width), whole)] * 2
    aliases = {}
    if kept is not None:
        aliases = {1 + len(args) + i: i for i in range(len(kept))}
        in_specs += [pl.BlockSpec(memory_space=pl.ANY)] * len(kept)
        args += list(kept)
    in_specs += [pl.BlockSpec(memory_space=pl.ANY)] * len(first)
    args += list(first)
    results = pl.pallas_call(
        functools.partial(expert_kernel, min(512, ff), min(1024, width), len(aliases) + len(first)),
        grid_spec=pltpu.PrefetchScalarGridSpec(
            num_scalar_prefetch=1,
            grid=(count,),
            in_specs=in_specs,
            out_specs=out_specs,
            scratch_shapes=[pltpu.VMEM((2, length, lanes), BF)] * 2,
        ),
        out_shape=out_shape,
        input_output_aliases=aliases,
        compiler_params=pltpu.CompilerParams(vmem_limit_bytes=60 * 2**20),
        cost_estimate=pl.CostEstimate(
            flops=count * 2 * cap * width * ff * 12 * 2,
            bytes_accessed=count * 3 * width * ff * 2 + 20 * length * width * 2,
            transcendentals=0,
        ),
        name="experts",
    )(who, *args)
    return results[:5], results[5], results[6]


def out_kernel(replicas, groups, who, *refs):
    pieces = refs[:replicas]
    near, far = refs[replicas : 2 * replicas], refs[2 * replicas : 3 * replicas]
    tokens, gain, hidden, normed, mixed = refs[3 * replicas :]
    part = pieces[0].shape[1]
    depth = near[0].shape[0] // (groups // 2)
    for q in range(replicas):
        mixed[:, pl.ds(pl.multiple_of((who[0] ^ q) * part, part), part)] = pieces[q][...]
    for q in range(replicas):
        total = jnp.zeros((tokens.shape[0], part), F32)
        for k in range(groups // 2):
            for flip, source in enumerate((near, far)):
                at = ((who[2] ^ flip) * (groups // 2) + k) * depth
                left = mixed[:, pl.ds(pl.multiple_of(at, depth), depth)]
                total += dot(left, source[q][k * depth : (k + 1) * depth])
        here = pl.ds(pl.multiple_of((who[0] ^ q) * part, part), part)
        hidden[:, here] = tokens[:, here].astype(F32) + total
    value = hidden[...]
    scale = lax.rsqrt(jnp.mean(value * value, axis=1, keepdims=True) + epsilon)
    normed[...] = (value * scale * gain[...]).astype(BF)


def out_step(who, pieces, near, far, tokens, gain):
    replicas = len(pieces)
    length, width = tokens.shape
    groups = lax.axis_size("fsdp")
    vmem = pl.BlockSpec(memory_space=pltpu.VMEM)
    return pl.pallas_call(
        functools.partial(out_kernel, replicas, groups),
        in_specs=[pl.BlockSpec(memory_space=pltpu.SMEM)] + [vmem] * (3 * replicas + 2),
        out_specs=[vmem] * 3,
        out_shape=[
            jax.ShapeDtypeStruct((length, width), F32),
            jax.ShapeDtypeStruct((length, width), BF),
            jax.ShapeDtypeStruct((length, width), BF),
        ],
        compiler_params=pltpu.CompilerParams(vmem_limit_bytes=60 * 2**20),
        name="attention_out",
    )(who, *pieces, *near, *far, tokens, gain)


def back_kernel(replicas, groups, experts, who, *refs):
    rounds = groups // 2
    shares = refs[:rounds]
    hidden, normed, cot, gain, gates, router = refs[rounds : rounds + 6]
    refs = refs[rounds + 6 :]
    near, far, refs = refs[:replicas], refs[replicas : 2 * replicas], refs[2 * replicas :]
    grad_hidden, gain_grad, router_grad = refs[:3]
    pieces = refs[3 : 3 + replicas]
    mixed = refs[3 + replicas]
    length, width = hidden.shape
    lanes = router.shape[1]
    part = width // replicas
    depth = width // groups
    per_chip = experts // rounds
    line = lax.broadcasted_iota(jnp.int32, (EXTRA, lanes), 0)
    lane = lax.broadcasted_iota(jnp.int32, (EXTRA, lanes), 1)
    summed = jnp.zeros((length, width), F32)
    grad_gates = jnp.zeros((length, lanes), F32)
    for k in range(rounds):
        summed += shares[k][:length].astype(F32)
        chip = who[1] ^ k
        place = (lane == chip * per_chip + line // 2) & (line < 2 * per_chip)
        grad_gates += dot_tn(shares[k][length:, :length], place.astype(BF))
    own = gates[...]
    centered = grad_gates - jnp.sum(own * grad_gates, axis=1, keepdims=True)
    grad_logits = (own * centered).astype(BF)
    router_grad[...] = dot_tn(normed[...], grad_logits).astype(BF)
    grad_normed = summed + dot_nt(grad_logits, router[...])
    value = hidden[...]
    scale = lax.rsqrt(jnp.mean(value * value, axis=1, keepdims=True) + epsilon)
    gain_grad[...] = jnp.sum(grad_normed * value * scale, axis=0, keepdims=True)
    pulled = grad_normed * gain[...]
    inner = jnp.mean(pulled * value, axis=1, keepdims=True)
    total = cot[...].astype(F32) + scale * pulled - value * (scale * scale * scale * inner)
    grad_hidden[...] = total
    for q in range(replicas):
        here = pl.ds(pl.multiple_of((who[0] ^ q) * part, part), part)
        pieces[q][:, part:] = grad_hidden[:, here].astype(BF)
    for k in range(rounds):
        for flip, source in enumerate((near, far)):
            block = jnp.zeros((length, depth), F32)
            for q in range(replicas):
                block += dot_nt(pieces[q][:, part:], source[q][k * depth : (k + 1) * depth])
            at = ((who[2] ^ flip) * (groups // 2) + k) * depth
            mixed[:, pl.ds(pl.multiple_of(at, depth), depth)] = block.astype(BF)
    for q in range(replicas):
        here = pl.ds(pl.multiple_of((who[0] ^ q) * part, part), part)
        pieces[q][:, :part] = mixed[:, here]


def back_step(who, shares, hidden, normed, cot, gain, gates, router, near, far, experts):
    replicas = len(near)
    length, width = hidden.shape
    groups = 2 * len(shares)
    vmem = pl.BlockSpec(memory_space=pltpu.VMEM)
    piece = jax.ShapeDtypeStruct((length, 2 * width // replicas), BF)
    results = pl.pallas_call(
        functools.partial(back_kernel, replicas, groups, experts),
        in_specs=[pl.BlockSpec(memory_space=pltpu.SMEM)] + [vmem] * (len(shares) + 6 + 2 * replicas),
        out_specs=[vmem] * (3 + replicas),
        scratch_shapes=[pltpu.VMEM((length, width), BF)],
        out_shape=[
            jax.ShapeDtypeStruct((length, width), F32),
            jax.ShapeDtypeStruct((1, width), F32),
            jax.ShapeDtypeStruct((width, router.shape[1]), BF),
            *[piece] * replicas,
        ],
        compiler_params=pltpu.CompilerParams(vmem_limit_bytes=60 * 2**20),
        cost_estimate=pl.CostEstimate(flops=10**11, bytes_accessed=0, transcendentals=0),
        name="attention_back",
    )(who, *shares, hidden, normed, cot, gain, gates, router, *near, *far)
    return results[0], results[1], results[2], results[3:]


def turn(value, cosine, sine):
    return value * cosine + pltpu.roll(value, value.shape[1] // 2, 1) * sine


def attend_kernel(heads, normed, weight, seg_row, seg_col, cosine, sine, gains, *outs):
    raw, ready, mixed, totals, tops = outs
    allowed = seg_col[0] == seg_row[0]
    lane = lax.broadcasted_iota(jnp.int32, totals.shape, 1)
    top_lane = lax.broadcasted_iota(jnp.int32, tops.shape[1:], 1)
    part = heads * HD
    totals[...] = jnp.zeros(totals.shape, F32)
    tops[0] = jnp.zeros(tops.shape[1:], F32)
    for i in range(2):
        raw[:, i * part : (i + 1) * part] = dot(normed[...], weight[:, i * part : (i + 1) * part])
    ready[:, 2 * part :] = dot(normed[...], weight[:, 2 * part : 3 * part]).astype(BF)
    for h in range(heads):
        rotated = []
        for i in range(2):
            at = slice(i * part + h * HD, i * part + (h + 1) * HD)
            head = raw[:, at]
            norm = lax.rsqrt(jnp.mean(head * head, axis=1, keepdims=True) + epsilon)
            rotated.append(turn(head * norm * gains[i : i + 1], cosine[...], sine[...]).astype(BF))
            ready[:, at] = rotated[i]
        scores = dot_nt(rotated[0], rotated[1]) * HD**-0.5
        scores = jnp.where(allowed, scores, -1e30)
        peak = jnp.max(scores, axis=1, keepdims=True)
        powers = jnp.exp(scores - peak)
        total = peak + jnp.log(jnp.sum(powers, axis=1, keepdims=True))
        weights = jnp.exp(scores - total).astype(BF)
        here = slice(h * HD, (h + 1) * HD)
        mixed[:, here] = dot(weights, ready[:, 2 * part + h * HD : 2 * part + (h + 1) * HD]).astype(BF)
        totals[...] = jnp.where(lane == h, total, totals[...])
        tops[0] = jnp.where(top_lane == h, jnp.max(peak, axis=0, keepdims=True), tops[0])


def attend(normed, weight, segments, cosine, sine, gains, heads):
    count, length = segments.shape
    rows, width = normed.shape
    part = heads * HD
    one = lambda n: (n, 0)
    fixed = lambda n: (0, 0)
    return pl.pallas_call(
        functools.partial(attend_kernel, heads),
        grid=(count,),
        in_specs=[
            pl.BlockSpec((length, width), one),
            pl.BlockSpec((width, 3 * part), fixed, pipeline_mode=pl.Buffered(1)),
            pl.BlockSpec((1, 1, length), lambda n: (n, 0, 0)),
            pl.BlockSpec((1, length, 1), lambda n: (n, 0, 0)),
            pl.BlockSpec((length, HD), fixed),
            pl.BlockSpec((length, HD), fixed),
            pl.BlockSpec((2, HD), fixed),
        ],
        out_specs=[
            pl.BlockSpec((length, 2 * part), one),
            pl.BlockSpec((length, 3 * part), one),
            pl.BlockSpec((length, part), one),
            pl.BlockSpec((length, 128), one),
            pl.BlockSpec((1, 1, 128), lambda n: (n, 0, 0)),
        ],
        out_shape=[
            jax.ShapeDtypeStruct((rows, 2 * part), F32),
            jax.ShapeDtypeStruct((rows, 3 * part), BF),
            jax.ShapeDtypeStruct((rows, part), BF),
            jax.ShapeDtypeStruct((rows, 128), F32),
            jax.ShapeDtypeStruct((count, 1, 128), F32),
        ],
        compiler_params=pltpu.CompilerParams(vmem_limit_bytes=60 * 2**20),
        cost_estimate=pl.CostEstimate(flops=0, bytes_accessed=0, transcendentals=0),
        name="attention",
    )(normed, weight, segments[:, None, :], segments[:, :, None], cosine, sine, gains)


def attend_back_kernel(heads, pull, raw, ready, totals, seg_row, seg_col, cosine, sine, gains, grad, gain_grads):
    allowed = seg_col[0] == seg_row[0]
    lane = lax.broadcasted_iota(jnp.int32, totals.shape, 1)
    part = heads * HD
    sums = [jnp.zeros((1, HD), F32)] * 2
    for h in range(heads):
        at = [slice(i * part + h * HD, i * part + (h + 1) * HD) for i in range(3)]
        query, key, value = (ready[:, a] for a in at)
        pulled = pull[:, h * HD : (h + 1) * HD]
        total = jnp.sum(jnp.where(lane == h, totals[...], 0.0), axis=1, keepdims=True)
        scores = dot_nt(query, key) * HD**-0.5
        probs = jnp.where(allowed, jnp.exp(jnp.where(allowed, scores - total, 0.0)), 0.0)
        grad_weights = dot_nt(pulled, value)
        grad[:, at[2]] = dot_tn(probs.astype(BF), pulled).astype(BF)
        inner = jnp.sum(probs * grad_weights, axis=1, keepdims=True)
        grad_scores = (probs * (grad_weights - inner)).astype(BF)
        both = (dot(grad_scores, key), dot_tn(grad_scores, query))
        for i, g in enumerate(both):
            g = g * HD**-0.5
            back = g * cosine[...] - pltpu.roll(g, HD // 2, 1) * sine[...]
            head = raw[:, at[i]]
            norm = lax.rsqrt(jnp.mean(head * head, axis=1, keepdims=True) + epsilon)
            sums[i] = sums[i] + jnp.sum(back * head * norm, axis=0, keepdims=True)
            scaled = back * gains[i : i + 1]
            mean = jnp.mean(scaled * head, axis=1, keepdims=True)
            grad[:, at[i]] = (norm * scaled - head * (norm * norm * norm * mean)).astype(BF)
    for i in range(2):
        gain_grads[0, i : i + 1] = sums[i]


def attend_back(pull, raw, ready, totals, segments, cosine, sine, gains, heads):
    count, length = segments.shape
    rows = raw.shape[0]
    part = heads * HD
    one = lambda n: (n, 0)
    fixed = lambda n: (0, 0)
    return pl.pallas_call(
        functools.partial(attend_back_kernel, heads),
        grid=(count,),
        in_specs=[
            pl.BlockSpec((length, part), one),
            pl.BlockSpec((length, 2 * part), one),
            pl.BlockSpec((length, 3 * part), one),
            pl.BlockSpec((length, 128), one),
            pl.BlockSpec((1, 1, length), lambda n: (n, 0, 0)),
            pl.BlockSpec((1, length, 1), lambda n: (n, 0, 0)),
            pl.BlockSpec((length, HD), fixed),
            pl.BlockSpec((length, HD), fixed),
            pl.BlockSpec((2, HD), fixed),
        ],
        out_specs=[
            pl.BlockSpec((length, 3 * part), one),
            pl.BlockSpec((1, 2, HD), lambda n: (n, 0, 0)),
        ],
        out_shape=[
            jax.ShapeDtypeStruct((rows, 3 * part), BF),
            jax.ShapeDtypeStruct((count, 2, HD), F32),
        ],
        compiler_params=pltpu.CompilerParams(vmem_limit_bytes=32 * 2**20),
        cost_estimate=pl.CostEstimate(
            flops=0, bytes_accessed=0, transcendentals=0
        ),
        name="attention_grad",
    )(pull, raw, ready, totals, segments[:, None, :], segments[:, :, None], cosine, sine, gains)


def weight_grad_kernel(half, quarters, left, right, *outs):
    j, i = pl.program_id(0), pl.program_id(1)
    block = dot_tn(left[0], right[0]).astype(BF)
    for at, out in enumerate(outs):

        @pl.when((j == at // 2) & ((i >= half) == (at % 2 == 1)))
        def _(out=out):
            out[0] = block


def weight_grads(quarters, left, right, parts, cost):
    count, rows, width = left.shape
    size, n = width // parts, right.shape[2]
    half = parts // 2

    def spot(at):
        def index(j, i, quarters):
            step = j * parts + i - (at // 2 * parts + at % 2 * half)
            return (jnp.clip(step, 0, half - 1), 0, 0)

        return index

    return pl.pallas_call(
        functools.partial(weight_grad_kernel, half),
        grid_spec=pltpu.PrefetchScalarGridSpec(
            num_scalar_prefetch=1,
            grid=(count, parts),
            in_specs=[
                pl.BlockSpec((1, rows, size), lambda j, i, quarters: (j, 0, quarters[j, i])),
                pl.BlockSpec((1, rows, n), lambda j, i, quarters: (j, 0, 0)),
            ],
            out_specs=[pl.BlockSpec((1, size, n), spot(at)) for at in range(2 * count)],
        ),
        out_shape=[jax.ShapeDtypeStruct((half, size, n), BF)] * (2 * count),
        compiler_params=pltpu.CompilerParams(vmem_limit_bytes=56 * 2**20),
        cost_estimate=pl.CostEstimate(flops=cost, bytes_accessed=0, transcendentals=0),
        name="weight_grads",
    )(quarters, left, right)


def product_kernel(left, right, out):
    out[...] = dot_tn(left[...], right[...]).astype(BF)


def product(left, right):
    rows, width = left.shape
    n = right.shape[1]
    size = min(width, 256)
    return pl.pallas_call(
        product_kernel,
        grid=(width // size,),
        in_specs=[
            pl.BlockSpec((rows, size), lambda i: (0, i)),
            pl.BlockSpec((rows, n), lambda i: (0, 0)),
        ],
        out_specs=pl.BlockSpec((size, n), lambda i: (i, 0)),
        out_shape=jax.ShapeDtypeStruct((width, n), BF),
        compiler_params=pltpu.CompilerParams(vmem_limit_bytes=32 * 2**20),
        cost_estimate=pl.CostEstimate(flops=0, bytes_accessed=0, transcendentals=0),
        name="product",
    )(left, right)


def spread_kernel(grad, weight, *outs):
    block = dot_nt(grad[...], weight[...]).astype(BF)
    for at, out in enumerate(outs):

        @pl.when(pl.program_id(0) == at)
        def _(out=out):
            out[...] = block


def normed_grads(grad, weight, count):
    rows, n = grad.shape
    width = weight.shape[0]
    length = rows // count
    return pl.pallas_call(
        spread_kernel,
        grid=(count,),
        in_specs=[
            pl.BlockSpec((length, n), lambda i: (i, 0)),
            pl.BlockSpec((width, n), lambda i: (0, 0), pipeline_mode=pl.Buffered(1)),
        ],
        out_specs=[pl.BlockSpec((length, width), lambda i: (0, 0))] * count,
        out_shape=[jax.ShapeDtypeStruct((length, width), BF)] * count,
        compiler_params=pltpu.CompilerParams(vmem_limit_bytes=48 * 2**20),
        cost_estimate=pl.CostEstimate(flops=0, bytes_accessed=0, transcendentals=0),
        name="normed_grads",
    )(grad, weight)


def halve_kernel(half, blocks, keep, got, send_out, keep_out):
    block = (keep[0].astype(F32) + got[0].astype(F32)).astype(BF)

    @pl.when(pl.program_id(0) < half)
    def _():
        send_out[0] = block

    @pl.when(pl.program_id(0) >= half)
    def _():
        keep_out[0] = block


def halve(blocks, keep, got, cost):
    count, size, n = keep.shape
    half = count // 2
    here = pl.BlockSpec((1, size, n), lambda i, blocks: (blocks[i], 0, 0))
    return pl.pallas_call(
        functools.partial(halve_kernel, half),
        grid_spec=pltpu.PrefetchScalarGridSpec(
            num_scalar_prefetch=1,
            grid=(count,),
            in_specs=[here, here],
            out_specs=[
                pl.BlockSpec((1, size, n), lambda i, blocks: (jnp.minimum(i, half - 1), 0, 0)),
                pl.BlockSpec((1, size, n), lambda i, blocks: (jnp.maximum(i - half, 0), 0, 0)),
            ],
        ),
        out_shape=[jax.ShapeDtypeStruct((half, size, n), BF)] * 2,
        compiler_params=pltpu.CompilerParams(vmem_limit_bytes=32 * 2**20),
        cost_estimate=pl.CostEstimate(flops=cost, bytes_accessed=0, transcendentals=0),
        name="halve",
    )(blocks, keep, got)


def join_kernel(*refs):
    out = refs[-1]
    for j in range((len(refs) - 1) // 2):

        @pl.when(pl.program_id(0) == j)
        def _(j=j):
            out[0] = refs[2 * j][...].astype(F32) + refs[2 * j + 1][...].astype(F32)


def join(pairs, cost):
    size, n = pairs[0][0].shape
    step = min(size, 256)
    count = len(pairs)

    def spot(at):
        def index(j, i):
            k = j * (size // step) + i - at * (size // step)
            return (jnp.clip(k, 0, size // step - 1), 0)

        return index

    return pl.pallas_call(
        join_kernel,
        grid=(count, size // step),
        in_specs=[pl.BlockSpec((step, n), spot(at // 2)) for at in range(2 * count)],
        out_specs=pl.BlockSpec((1, step, n), lambda j, i: (j, i, 0)),
        out_shape=jax.ShapeDtypeStruct((count, size, n), F32),
        compiler_params=pltpu.CompilerParams(vmem_limit_bytes=60 * 2**20),
        cost_estimate=pl.CostEstimate(flops=cost, bytes_accessed=0, transcendentals=0),
        name="join",
    )(*[v for pair in pairs for v in pair])


def input_kernel(count, heads, who, *refs):
    pieces = refs[:count]
    tokens, gain, grad_hidden, ffn, gains, tops, grad, small = refs[count:]
    width = tokens.shape[1]
    pulled = pieces[0][...].astype(F32)
    for piece in pieces[1:]:
        pulled = pulled + piece[...].astype(F32)
    value = tokens[...].astype(F32)
    scale = lax.rsqrt(jnp.mean(value * value, axis=1, keepdims=True) + epsilon)
    small[:, :width] = jnp.sum(pulled * value * scale, axis=0, keepdims=True)
    small[:, width : 2 * width] = ffn[...]
    for i in range(2):
        at = 2 * width + i * HD
        small[:, at : at + HD] = jnp.sum(gains[:, i], axis=0, keepdims=True)
    top = jnp.max(tops[:, 0], axis=0, keepdims=True)
    lane = lax.broadcasted_iota(jnp.int32, top.shape, 1)
    top = jnp.where(lane < heads, top, -3e38)
    small[:, 2 * width + 2 * HD :] = pltpu.roll(top, who[0] * heads, 1)
    pulled = pulled * gain[...]
    inner = jnp.mean(pulled * value, axis=1, keepdims=True)
    back = scale * pulled - value * (scale * scale * scale * inner)
    grad[...] = (grad_hidden[...] + back).astype(BF)


def input_step(who, pieces, tokens, gain, grad_hidden, ffn, gains, tops, heads):
    length, width = tokens.shape
    vmem = pl.BlockSpec(memory_space=pltpu.VMEM)
    return pl.pallas_call(
        functools.partial(input_kernel, len(pieces), heads),
        in_specs=[pl.BlockSpec(memory_space=pltpu.SMEM)] + [vmem] * (len(pieces) + 6),
        out_specs=[vmem] * 2,
        out_shape=[
            jax.ShapeDtypeStruct((length, width), BF),
            jax.ShapeDtypeStruct((1, 2 * width + 2 * HD + 128), F32),
        ],
        compiler_params=pltpu.CompilerParams(vmem_limit_bytes=60 * 2**20),
        cost_estimate=pl.CostEstimate(flops=10**11, bytes_accessed=0, transcendentals=0),
        name="input_grad",
    )(who, *pieces, tokens, gain, grad_hidden, ffn, gains, tops)


def gather_kernel(count, arrays, who, *refs):
    blocks, outs = refs[:count], refs[count:]
    part = outs[0].shape[1] // count
    total = 0.0
    for k, block in enumerate(blocks):
        here = pl.ds(pl.multiple_of((who[0] ^ k) * part, part), part)
        for i in range(arrays):
            outs[i][:, here] = block[:, i * part : (i + 1) * part].astype(F32)
        if len(outs) > arrays:
            total += block[:, arrays * part :].astype(F32)
    if len(outs) > arrays:
        outs[-1][...] = total


def gather_step(who, blocks, arrays):
    rows, wide = blocks[0].shape
    lanes = 128 if wide % (arrays * 256) else 0
    part = (wide - lanes) // arrays
    count = len(blocks)
    vmem = pl.BlockSpec(memory_space=pltpu.VMEM)
    return pl.pallas_call(
        functools.partial(gather_kernel, count, arrays),
        in_specs=[pl.BlockSpec(memory_space=pltpu.SMEM)] + [vmem] * count,
        out_specs=[vmem] * (arrays + (lanes > 0)),
        out_shape=[jax.ShapeDtypeStruct((rows, part * count), F32)] * arrays
        + [jax.ShapeDtypeStruct((rows, lanes), F32)] * (lanes > 0),
        compiler_params=pltpu.CompilerParams(vmem_limit_bytes=48 * 2**20),
        cost_estimate=pl.CostEstimate(flops=0, bytes_accessed=0, transcendentals=0),
        name="gather_columns",
    )(who, *blocks)


def merge_kernel(sums, *refs):
    out = refs[-1]
    total = refs[0][...]
    lane = lax.broadcasted_iota(jnp.int32, total.shape, 1)
    for ref in refs[1:-1]:
        other = ref[...]
        total = jnp.where(lane < sums, total + other, jnp.maximum(total, other))
    out[...] = total


def merge(sums, *values):
    vmem = pl.BlockSpec(memory_space=pltpu.VMEM)
    return pl.pallas_call(
        functools.partial(merge_kernel, sums),
        in_specs=[vmem] * len(values),
        out_specs=vmem,
        out_shape=jax.ShapeDtypeStruct(values[0].shape, F32),
        cost_estimate=pl.CostEstimate(flops=0, bytes_accessed=0, transcendentals=0),
        name="merge",
    )(*values)


def norm_kernel(count, gain, *refs):
    out = refs[-1]
    for k in range(count):

        @pl.when(pl.program_id(0) == k)
        def _(k=k):
            value = refs[k][...].astype(F32)
            scale = lax.rsqrt(jnp.mean(value * value, axis=1, keepdims=True) + epsilon)
            out[...] = (value * scale * gain[...]).astype(BF)


def norm_rows(values, gain):
    count = len(values)
    length, width = values[0].shape
    return pl.pallas_call(
        functools.partial(norm_kernel, count),
        grid=(count,),
        in_specs=[pl.BlockSpec((1, width), lambda n: (0, 0))]
        + [pl.BlockSpec((length, width), lambda n: (0, 0))] * count,
        out_specs=pl.BlockSpec((length, width), lambda n: (n, 0)),
        out_shape=jax.ShapeDtypeStruct((count * length, width), BF),
        compiler_params=pltpu.CompilerParams(vmem_limit_bytes=32 * 2**20),
        cost_estimate=pl.CostEstimate(flops=10**11, bytes_accessed=0, transcendentals=0),
        name="norm_rows",
    )(gain, *values)


def local(
    tokens,
    cotangent,
    segment_ids,
    expert_index,
    clip_threshold,
    attn_norm_gain,
    w_query,
    w_key,
    w_value,
    w_output,
    query_gain,
    key_gain,
    ffn_norm_gain,
    router,
    expert_in,
    expert_out,
):
    replicas = lax.axis_size("replica")
    groups = lax.axis_size("fsdp")
    me_r = lax.axis_index("replica")
    me_f = lax.axis_index("fsdp")
    core = me_f % 2
    length, width = tokens.shape
    part = width // replicas
    heads = part // HD
    ff = expert_out.shape[1]
    local_experts = expert_in.shape[0]
    scale = HD ** (-0.5)
    attn_gain = attn_norm_gain.astype(F32)
    ffn_gain = ffn_norm_gain.astype(F32)
    gain_query = query_gain.astype(F32)
    gain_key = key_gain.astype(F32)

    def swap(value, k):
        return lax.ppermute(value, "replica", [(r, r ^ k) for r in range(replicas)])

    def columns(value, k, axis=1):
        return lax.dynamic_slice_in_dim(value, (me_r ^ k) * part, part, axis)

    def spread(value):
        return [value] + [swap(value, k) for k in range(1, replicas)]

    def trade_columns(value):
        return [columns(value, 0)] + [swap(columns(value, k), k) for k in range(1, replicas)]

    def join_columns(blocks):
        out = jnp.zeros((blocks[0].shape[0], part * replicas), blocks[0].dtype)
        for k, block in enumerate(blocks):
            out = lax.dynamic_update_slice_in_dim(out, block, (me_r ^ k) * part, 1)
        return out

    def cross(value, k):
        return lax.ppermute(value, "fsdp", [(f, f ^ k) for f in range(groups)])

    def pass_on(up, down, hop):
        chips = groups // 2
        pairs = [(2 * a + i, 2 * a + 2 + i) for a in range(hop - 1, chips - 1) for i in (0, 1)]
        back = [(2 * a + 2 + i, 2 * a + i) for a in range(chips - hop) for i in (0, 1)]
        return lax.ppermute(up, "fsdp", pairs), lax.ppermute(down, "fsdp", back)

    def choose(up, down, k):
        chips = groups // 2
        found = {}
        for a in range(chips):
            b = a ^ k
            found.setdefault((b > a, abs(b - a)), []).append(a)
        picked = None
        for (above, hop), at in found.items():
            source = down[hop] if above else up[hop]
            if picked is None:
                picked = source
            else:
                here = functools.reduce(jnp.logical_or, [me_f // 2 == a for a in at])
                picked = jnp.where(here, source, picked)
        return picked

    def gather(value):
        return lax.all_gather(value, "fsdp", axis=0, tiled=True)

    def reduce(value):
        return lax.psum_scatter(value, "fsdp", scatter_dimension=0, tiled=True)

    bits = replicas.bit_length() - 1

    def next_bit(j, step):
        return 1 << (bits - 1 - step if j % 2 else step)

    def next_halves(traded, j, step, cost=0):
        keep, got = traded
        left = keep.shape[0]
        place = jnp.arange(left, dtype=jnp.int32)
        here = left // 2 if j % 2 else 1
        mine = (me_r & next_bit(j, step)) != 0
        other = ((place & here) != 0) != mine
        spots = jnp.where(other, jnp.cumsum(other) - 1, left // 2 + jnp.cumsum(~other) - 1)
        return halve(jnp.zeros((left,), jnp.int32).at[spots].set(place), keep, got, cost)

    index_table = expert_index.astype(BF).reshape(w_query.shape[0], -1)
    sent = [columns(w_output, 0), router, index_table]
    sizes = [v.shape[1] for v in sent]
    sent.append(jnp.zeros((w_query.shape[0], -sum(sizes) % 128), BF))
    quarter = gather(jnp.concatenate(sent, axis=1))
    full_router = quarter[:, part : part + EXPERTS]
    full_index = quarter[:, part + EXPERTS : part + EXPERTS + sizes[2]].astype(jnp.int32)
    full_index = full_index.reshape(groups * length, -1)
    ids = jnp.arange(EXPERTS, dtype=jnp.int32)
    mask = jnp.any(full_index[:, :, None] == ids, axis=1).reshape(groups, length, EXPERTS)
    first = me_f * local_experts
    hot = lax.dynamic_slice_in_dim(mask, first, local_experts, 2)
    order = jnp.arange(length, dtype=jnp.int32)
    before = (order[:, None] < order[None, :]).astype(BF)
    rank = jnp.einsum("nsj,st->njt", hot.astype(BF), before, preferred_element_type=F32)
    rank = jnp.where(hot.transpose(0, 2, 1), rank.astype(jnp.int32), -1)
    slots = jnp.arange(CAP, dtype=jnp.int32)
    pick = (rank[:, :, None, :] == slots[:, None]).astype(BF)
    spots = (rank[:, :, :, None] == slots).astype(BF)
    lanes = 128
    mask_wide = jnp.pad(mask.astype(F32), ((0, 0), (0, 0), (0, lanes - EXPERTS)))
    router_wide = jnp.pad(full_router, ((0, 0), (0, lanes - EXPERTS)))
    tables = (pick, spots, mask_wide, router_wide)
    tokens_all = spread(tokens)
    segments = jnp.concatenate(spread(after(segment_ids, *tokens_all[1:])), axis=0)
    normed = norm_rows(tokens_all, attn_gain[None, :])
    rounds = groups // 2
    where = jnp.stack([me_r, me_f // 2, core]).astype(jnp.int32)
    half = lax.dynamic_slice(quarter, (core * (width // 2), 0), (width // 2, part))
    near = spread(after(half, *tokens_all[1:]))
    near[1] = after(near[1], *tables, segments, normed)
    normed = after(normed, *near[1:])
    far = [cross(v, 1) for v in near]
    w_qkv = gather(jnp.concatenate([columns(w, 0) for w in (w_query, w_key, w_value)], axis=1))
    cot_all = gather(cotangent)
    cot_pair = (cotangent, cross(cotangent, 1))

    cosine, sine = rope_tables(length, HD)
    cosine = jnp.concatenate([cosine, cosine], axis=1)
    sine = jnp.concatenate([-sine, sine], axis=1)
    gains = jnp.stack([gain_query, gain_key])
    raw, ready, mixed_heads, totals, tops = attend(normed, w_qkv, segments, cosine, sine, gains, heads
    )
    mixed_heads = mixed_heads.reshape(replicas, length, part)
    pieces = [mixed_heads[0]] + [swap(mixed_heads[k], k) for k in range(1, replicas)]
    inputs = tokens.astype(F32)
    hidden, normed_ffn, mixed = out_step(where, pieces, near, far, tokens, ffn_gain[None, :])
    mixed_all = spread(mixed)

    def first_bit(j):
        return 1 << (bits - 1 if j % 2 else 0)

    numbers = jnp.arange(replicas, dtype=jnp.int32)
    quarters = []
    for j in range(local_experts):
        other = ((numbers ^ me_r) & first_bit(j)) != 0
        place = jnp.where(other, jnp.cumsum(other) - 1, replicas // 2 + jnp.cumsum(~other) - 1)
        quarters.append(jnp.zeros((replicas,), jnp.int32).at[place].set(numbers))
    quarters = jnp.stack(quarters)
    kept = None
    shares = []
    added = []
    pending = []
    up, down = [normed_ffn], [normed_ffn]
    for k in range(rounds):
        chip = (me_f // 2) ^ k
        who = jnp.stack([2 * chip + core, 2 * chip + 1 - core, chip, core, first])
        if k + 1 < rounds:
            next_up, next_down = pass_on(up[-1], down[-1], k + 1)
        mine = choose(up, down, k) if k else normed_ffn
        nf = (mine, cross(mine, 1))
        kept, back_a, back_b = expert_block(k, rounds, who, nf, (cot_all,) if k else cot_pair, pick, spots, mask_wide, router_wide, expert_in, expert_out, kept, pending
        )
        if k + 1 < rounds:
            up.append(after(next_up, back_a))
            down.append(after(next_down, back_a))
        else:
            rows, grad_projected, cot_rows, scaled, moe = kept
            out_blocks = weight_grads(quarters, after(scaled, mixed_all[-1]), cot_rows, replicas, 0)
        if k == rounds - 1:
            back_b = after(back_b, *out_blocks, *shares[1:])
        share = (back_a.astype(F32) + cross(back_b, 1).astype(F32)).astype(BF)
        added.append(share)
        if k == rounds - 2:
            pending = added[1:]
        else:
            pending = mixed_all[1:-1] if k == rounds - 3 else []
        shares.append(share if k == 0 else cross(share, 2 * k))
    out_traded = [
        (out_blocks[2 * j + 1], swap(out_blocks[2 * j], first_bit(j))) for j in range(local_experts)
    ]
    in_blocks = weight_grads(quarters, after(rows, share), grad_projected, replicas, 10**11)
    shares[-1] = after(shares[-1], *in_blocks, *[v[1] for v in out_traded])
    moe_sum = reduce(after(moe, shares[-1]))
    output = (hidden + moe_sum.astype(F32)).astype(BF)

    my_mask = lax.dynamic_index_in_dim(mask_wide, me_f, 0, keepdims=False) > 0.0
    logits = jnp.where(my_mask, dot(normed_ffn, router_wide), -jnp.inf)
    powers = jnp.exp(logits - jnp.max(logits, axis=1, keepdims=True))
    my_gates = powers / jnp.sum(powers, axis=1, keepdims=True)
    grad_hidden, ffn_gain_grad, router_grad, pieces = back_step(
        where, shares, hidden, normed_ffn, cotangent, ffn_gain[None, :], my_gates, router_wide, near, far, EXPERTS
    )
    grad_mixed = jnp.concatenate(
        [pieces[0]] + [swap(pieces[k], k) for k in range(1, replicas)], axis=0
    )
    sends = [
        after(in_blocks[2 * j], grad_mixed, *[v[1] for v in out_traded]) for j in range(local_experts)
    ]
    in_traded = [
        (in_blocks[2 * j + 1], swap(v, first_bit(j))) for j, v in enumerate(sends)
    ]
    ready = after(ready, *sends)
    grad_qkv, gain_grads = attend_back(grad_mixed, raw, ready, totals, segments, cosine, sine, gains, heads
    )
    qkv_grad = product(normed, grad_qkv)
    part_normed = normed_grads(grad_qkv, w_qkv, replicas)
    received = [v[1] for v in in_traded]
    received[0] = after(received[0], *received[1:], moe_sum)
    in_traded = [(v[0], got) for v, got in zip(in_traded, received)]
    in_halves = [next_halves(v, j, 1, 10**11) for j, v in enumerate(in_traded)]
    in_sends = [v for v, _ in in_halves]
    in_done = [(keep, swap(v, next_bit(j, 1))) for j, (v, keep) in enumerate(in_halves)]
    mixed_rows = jnp.concatenate([mixed_all[0], after(mixed_all[1], *in_sends), *mixed_all[2:]], axis=0)
    output_grad = dot_tn(mixed_rows, grad_mixed[:, part:])
    o_grad = jnp.concatenate([output_grad.astype(BF), router_grad], axis=1)
    share_o = reduce(o_grad)
    out_halves = [next_halves((k, after(v, part_normed[0])), j, 1) for j, (k, v) in enumerate(out_traded)]
    pieces = [after(part_normed[0], *in_sends, o_grad, *[v for v, _ in out_halves])]
    pieces += [swap(part_normed[k], k) for k in range(1, replicas)]
    input_grad, small = input_step(
        where, pieces, tokens, attn_gain[None, :], grad_hidden, ffn_gain_grad, gain_grads, tops, heads
    )
    second = [v[1] for v in in_done]
    share_qkv = reduce(qkv_grad)
    blocks = spread(after(jnp.concatenate([share_qkv, share_o], axis=1), *second, input_grad))
    out_done = [
        (keep, swap(after(v, *second, moe_sum), next_bit(j, 1))) for j, (v, keep) in enumerate(out_halves)
    ]

    def settle(traded, cost):
        pairs = []
        for j, (keep, got) in enumerate(traded):
            for step in range(2, bits):
                send, keep = next_halves((keep, got), j, step)
                got = swap(send, next_bit(j, step))
            pairs.append((keep[0], got[0]))
        return join(pairs, cost)

    n_sums = 2 * width + 2 * HD
    small = merge(n_sums, small, cross(small, 1))
    small = merge(n_sums, small, *[cross(small, 2 * k) for k in range(1, rounds)])
    small = merge(n_sums, *spread(after(small, *second)))
    small = small[0]
    attn_gain_total = small[:width]
    ffn_gain_total = small[width : 2 * width]
    query_gain_total = small[2 * width : 2 * width + HD]
    key_gain_total = small[2 * width + HD : n_sums]
    head_max = small[n_sums : n_sums + replicas * heads]
    threshold = clip_threshold.astype(F32)
    factor = threshold / jnp.maximum(head_max, threshold)
    column_scale = jnp.repeat(jnp.sqrt(factor), HD)
    clipped_query = (w_query.astype(F32) * column_scale[None, :]).astype(BF)
    clipped_key = (w_key.astype(F32) * column_scale[None, :]).astype(BF)
    expert_in_grad = settle(
        [(keep, after(v, clipped_query, clipped_key, output)) for keep, v in in_done], 10**11
    )
    expert_out_grad = settle([(k, after(v, expert_in_grad)) for k, v in out_done], 0)

    blocks[1] = after(blocks[1], expert_in_grad)
    total_query, total_key, total_value, total_output, total_router = gather_step(where, blocks, 4)
    total_router = total_router[:, :EXPERTS]
    return (
        output,
        input_grad,
        attn_gain_total,
        total_query,
        total_key,
        total_value,
        total_output,
        query_gain_total,
        key_gain_total,
        ffn_gain_total,
        total_router,
        expert_in_grad,
        expert_out_grad,
        head_max,
        clipped_query,
        clipped_key,
    )


def solution(mesh):
    both = ("replica", "fsdp")
    return jax.shard_map(
        local,
        mesh=mesh,
        in_specs=(
            P(both, None),
            P(both, None),
            P(both, None),
            P(both, None),
            P(),
            P(),
            P("fsdp", None),
            P("fsdp", None),
            P("fsdp", None),
            P("fsdp", None),
            P(),
            P(),
            P(),
            P("fsdp", None),
            P("fsdp", None, None),
            P("fsdp", None, None),
        ),
        out_specs=(
            P(both, None),
            P(both, None),
            P(),
            P("fsdp", None),
            P("fsdp", None),
            P("fsdp", None),
            P("fsdp", None),
            P(),
            P(),
            P(),
            P("fsdp", None),
            P("fsdp", "replica", None),
            P("fsdp", "replica", None),
            P(),
            P("fsdp", None),
            P("fsdp", None),
        ),
        check_vma=False,
    )
```

```python
import functools

import jax
import jax.numpy as jnp
from jax import lax
from jax.experimental import pallas as pl
from jax.experimental.pallas import tpu as pltpu
from jax.sharding import PartitionSpec as P

HD = 128
EXPERTS = 16
CAP = 144

epsilon = 1e-06
rope_base = 10000.0
BF = jnp.bfloat16
F32 = jnp.float32


def rms_norm(values, gain):
    return values * lax.rsqrt(jnp.mean(values * values, axis=-1, keepdims=True) + epsilon) * gain


def rope_tables(length, width):
    places = jnp.arange(length, dtype=F32)
    rates = rope_base ** (-jnp.arange(width // 2, dtype=F32) * 2.0 / width)
    angle = places[:, None] * rates[None, :]
    return jnp.cos(angle), jnp.sin(angle)


def rotate(values, cosine, sine):
    half = values.shape[-1] // 2
    first = values[..., :half]
    second = values[..., half:]
    return jnp.concatenate(
        [first * cosine - second * sine, second * cosine + first * sine], axis=-1
    )


def dot(left, right):
    return jnp.dot(left, right, preferred_element_type=F32)


def dot_tn(left, right):
    return lax.dot_general(left, right, (((0,), (0,)), ((), ())), preferred_element_type=F32)


def dot_nt(left, right):
    return lax.dot_general(left, right, (((1,), (1,)), ((), ())), preferred_element_type=F32)


EXTRA = 16


def nothing(*refs):
    pass


def after(value, *others):
    held = pl.BlockSpec(memory_space=pl.ANY)
    return pl.pallas_call(
        nothing,
        in_specs=[held] * (1 + len(others)),
        out_specs=held,
        out_shape=jax.ShapeDtypeStruct(value.shape, value.dtype),
        input_output_aliases={0: 0},
        name="after",
    )(value, *others)


def expert_kernel(tile, wide, unread, who, *refs):
    (nf_a, nf_b, cot_a, cot_b, pick_a, pick_b, spread_a, spread_b) = refs[:8]
    (mask_a, mask_b, router, w_in, w_out) = refs[8:13]
    refs = refs[13 + unread :]
    rows, gp, cot_rows, scaled, moe, back_a, back_b, gates_hi, gates_lo = refs
    j = pl.program_id(0)
    cap = pick_a.shape[2]
    length = nf_a.shape[0]
    ff = w_out.shape[1]
    core, expert = who[3], who[4] + j

    @pl.when(j == 0)
    def _():
        for at, (nf, mask) in enumerate(((nf_a, mask_a), (nf_b, mask_b))):
            seen = mask[0] > 0.0
            logits = jnp.where(seen, dot(nf[...], router[...]), -1e30)
            powers = jnp.where(seen, jnp.exp(logits - jnp.max(logits, axis=1, keepdims=True)), 0.0)
            gates = powers / jnp.sum(powers, axis=1, keepdims=True)
            high = gates.astype(BF)
            gates_hi[at] = high
            gates_lo[at] = (gates - high.astype(F32)).astype(BF)

    pa, pb = pick_a[0, 0], pick_b[0, 0]
    lane = lax.broadcasted_iota(jnp.int32, (cap, router.shape[1]), 1)

    def slot_gates(p, at):
        every = dot(p, gates_hi[at]) + dot(p, gates_lo[at])
        return jnp.sum(jnp.where(lane == expert, every, 0.0), axis=1, keepdims=True)

    gate = jnp.concatenate([slot_gates(pa, 0), slot_gates(pb, 1)], axis=0)
    rows[0, :cap] = dot(pa, nf_a[...]).astype(BF)
    rows[0, cap:] = dot(pb, nf_b[...]).astype(BF)
    cot_rows[0, :cap] = dot(pa, cot_a[...]).astype(BF)
    cot_rows[0, cap:] = dot(pb, cot_b[...]).astype(BF)

    def forward(t, total):
        at = pl.multiple_of(t * tile, tile)
        g = dot(rows[0], w_in[0, :, pl.ds(at, tile)])
        u = dot(rows[0], w_in[0, :, pl.ds(ff + at, tile)])
        pulled = dot_nt(cot_rows[0], w_out[0, pl.ds(at, tile), :])
        sigma = jax.nn.sigmoid(g)
        silu = g * sigma
        active = silu * u
        scaled[0, :, pl.ds(at, tile)] = (active * gate).astype(BF)
        ga = pulled * gate
        gp[0, :, pl.ds(at, tile)] = (ga * u * sigma * (1.0 + g * (1.0 - sigma))).astype(BF)
        gp[0, :, pl.ds(ff + at, tile)] = (ga * silu).astype(BF)
        return total + jnp.sum(active * pulled, axis=1, keepdims=True)

    total = lax.fori_loop(0, ff // tile, forward, jnp.zeros((2 * cap, 1), F32))
    line = lax.broadcasted_iota(jnp.int32, (EXTRA, length), 0)
    place = 2 * (core * pl.num_programs(0) + j)
    for back, p, part in ((back_a, pa, total[:cap]), (back_b, pb, total[cap:])):
        by_token = jnp.sum(p.astype(F32) * part, axis=0, keepdims=True)
        high = by_token.astype(BF).astype(F32)
        new = jnp.where(line == place, high, jnp.where(line == place + 1, by_token - high, 0.0))

        @pl.when(j == 0)
        def _(back=back):
            back[length:, :] = jnp.zeros((EXTRA, back.shape[1]), BF)

        old = back[length:, :length].astype(F32)
        back[length:, :length] = (old + new).astype(BF)
    sa, sb = spread_a[0, 0], spread_b[0, 0]
    moe_a = pl.ds(pl.multiple_of(core * length, length), length)
    moe_b = pl.ds(pl.multiple_of((1 - core) * length, length), length)

    def backward(t, _):
        here = pl.ds(pl.multiple_of(t * wide, wide), wide)
        gr = dot_nt(gp[0], w_in[0, here, :]).astype(BF)
        res = dot(scaled[0], w_out[0, :, here]).astype(BF)
        for out, where, s, value in (
            (back_a, pl.ds(0, length), sa, gr[:cap]),
            (back_b, pl.ds(0, length), sb, gr[cap:]),
            (moe, moe_a, sa, res[:cap]),
            (moe, moe_b, sb, res[cap:]),
        ):
            old = jnp.where(j > 0, out[where, here].astype(F32), 0.0)
            out[where, here] = (dot(s, value) + old).astype(BF)
        return 0

    lax.fori_loop(0, w_in.shape[1] // wide, backward, 0)


def expert_block(k, rounds, who, nf, cot, pick, spread, mask, router, w_in, w_out, kept, first):
    length, width = nf[0].shape
    count, _, two_ff = w_in.shape
    groups = pick.shape[0]
    ff = two_ff // 2
    cap = pick.shape[2]
    lanes = router.shape[1]

    def whole(j, who):
        return (0, 0)

    def seq(i):
        return lambda j, who: (who[i], j, 0, 0)

    in_specs = [pl.BlockSpec((length, width), whole)] * 2
    if len(cot) == 2:
        in_specs += [pl.BlockSpec((length, width), whole)] * 2
    else:
        cot = [cot[0]] * 2
        in_specs += [
            pl.BlockSpec((length, width), lambda j, who, i=i: (who[i], 0)) for i in range(2)
        ]
    in_specs += [pl.BlockSpec((1, 1, cap, length), seq(i)) for i in range(2)]
    in_specs += [pl.BlockSpec((1, 1, length, cap), seq(i)) for i in range(2)]
    in_specs += [
        pl.BlockSpec((1, length, lanes), lambda j, who, i=i: (who[i], 0, 0)) for i in range(2)
    ]
    in_specs += [
        pl.BlockSpec((width, lanes), whole),
        pl.BlockSpec((1, width, two_ff), lambda j, who: (j, 0, 0)),
        pl.BlockSpec((1, ff, width), lambda j, who: (j, 0, 0)),
    ]
    args = [*nf, *cot, pick, pick, spread, spread, mask, mask, router, w_in, w_out]
    total = rounds * 2 * cap
    saved = [(count, total, n) for n in (width, two_ff, width, ff)]
    out_shape = [jax.ShapeDtypeStruct(s, BF) for s in saved]
    out_shape += [jax.ShapeDtypeStruct((groups * length, width), BF)]
    out_shape += [jax.ShapeDtypeStruct((length + EXTRA, width), BF)] * 2
    out_specs = [pl.BlockSpec((1, 2 * cap, s[2]), lambda j, who: (j, k, 0)) for s in saved]
    out_specs += [pl.BlockSpec((2 * length, width), lambda j, who: (who[2], 0))]
    out_specs += [pl.BlockSpec((length + EXTRA, width), whole)] * 2
    aliases = {}
    if kept is not None:
        aliases = {1 + len(args) + i: i for i in range(len(kept))}
        in_specs += [pl.BlockSpec(memory_space=pl.ANY)] * len(kept)
        args += list(kept)
    in_specs += [pl.BlockSpec(memory_space=pl.ANY)] * len(first)
    args += list(first)
    results = pl.pallas_call(
        functools.partial(expert_kernel, min(512, ff), min(1024, width), len(aliases) + len(first)),
        grid_spec=pltpu.PrefetchScalarGridSpec(
            num_scalar_prefetch=1,
            grid=(count,),
            in_specs=in_specs,
            out_specs=out_specs,
            scratch_shapes=[pltpu.VMEM((2, length, lanes), BF)] * 2,
        ),
        out_shape=out_shape,
        input_output_aliases=aliases,
        compiler_params=pltpu.CompilerParams(vmem_limit_bytes=60 * 2**20),
        cost_estimate=pl.CostEstimate(
            flops=count * 2 * cap * width * ff * 12 * 2,
            bytes_accessed=count * 3 * width * ff * 2 + 20 * length * width * 2,
            transcendentals=0,
        ),
        name="experts",
    )(who, *args)
    return results[:5], results[5], results[6]


def out_kernel(replicas, groups, who, *refs):
    pieces = refs[:replicas]
    near, far, tokens, gain = refs[replicas : replicas + 4]
    hidden, normed, mixed = refs[replicas + 4 :]
    part = pieces[0].shape[1]
    depth = near.shape[1] // (groups // 2)
    for q in range(replicas):
        mixed[:, pl.ds(pl.multiple_of((who[0] ^ q) * part, part), part)] = pieces[q][...]
    for q in range(replicas):
        total = jnp.zeros((tokens.shape[0], part), F32)
        for k in range(groups // 2):
            for flip, source in enumerate((near, far)):
                at = ((who[2] ^ flip) * (groups // 2) + k) * depth
                left = mixed[:, pl.ds(pl.multiple_of(at, depth), depth)]
                total += dot(left, source[q, k * depth : (k + 1) * depth])
        here = pl.ds(pl.multiple_of((who[0] ^ q) * part, part), part)
        hidden[:, here] = tokens[:, here].astype(F32) + total
    value = hidden[...]
    scale = lax.rsqrt(jnp.mean(value * value, axis=1, keepdims=True) + epsilon)
    normed[...] = (value * scale * gain[...]).astype(BF)


def out_step(who, pieces, near, far, tokens, gain):
    replicas = len(pieces)
    length, width = tokens.shape
    groups = lax.axis_size("fsdp")
    vmem = pl.BlockSpec(memory_space=pltpu.VMEM)
    return pl.pallas_call(
        functools.partial(out_kernel, replicas, groups),
        in_specs=[pl.BlockSpec(memory_space=pltpu.SMEM)] + [vmem] * (replicas + 4),
        out_specs=[vmem] * 3,
        out_shape=[
            jax.ShapeDtypeStruct((length, width), F32),
            jax.ShapeDtypeStruct((length, width), BF),
            jax.ShapeDtypeStruct((length, width), BF),
        ],
        compiler_params=pltpu.CompilerParams(vmem_limit_bytes=60 * 2**20),
        name="attention_out",
    )(who, *pieces, near, far, tokens, gain)


def back_kernel(replicas, groups, experts, who, *refs):
    rounds = groups // 2
    shares = refs[:rounds]
    hidden, normed, cot, gain, gates, router, near, far = refs[rounds : rounds + 8]
    grad_hidden, gain_grad, router_grad = refs[rounds + 8 : rounds + 11]
    pieces = refs[rounds + 11 : rounds + 11 + replicas]
    mixed = refs[rounds + 11 + replicas]
    length, width = hidden.shape
    lanes = router.shape[1]
    part = width // replicas
    depth = width // groups
    per_chip = experts // rounds
    line = lax.broadcasted_iota(jnp.int32, (EXTRA, lanes), 0)
    lane = lax.broadcasted_iota(jnp.int32, (EXTRA, lanes), 1)
    summed = jnp.zeros((length, width), F32)
    grad_gates = jnp.zeros((length, lanes), F32)
    for k in range(rounds):
        summed += shares[k][:length].astype(F32)
        chip = who[1] ^ k
        place = (lane == chip * per_chip + line // 2) & (line < 2 * per_chip)
        grad_gates += dot_tn(shares[k][length:, :length], place.astype(BF))
    own = gates[...]
    centered = grad_gates - jnp.sum(own * grad_gates, axis=1, keepdims=True)
    grad_logits = (own * centered).astype(BF)
    router_grad[...] = dot_tn(normed[...], grad_logits).astype(BF)
    grad_normed = summed + dot_nt(grad_logits, router[...])
    value = hidden[...]
    scale = lax.rsqrt(jnp.mean(value * value, axis=1, keepdims=True) + epsilon)
    gain_grad[...] = jnp.sum(grad_normed * value * scale, axis=0, keepdims=True)
    pulled = grad_normed * gain[...]
    inner = jnp.mean(pulled * value, axis=1, keepdims=True)
    total = cot[...].astype(F32) + scale * pulled - value * (scale * scale * scale * inner)
    grad_hidden[...] = total
    for q in range(replicas):
        here = pl.ds(pl.multiple_of((who[0] ^ q) * part, part), part)
        pieces[q][:, part:] = grad_hidden[:, here].astype(BF)
    for k in range(rounds):
        for flip, source in enumerate((near, far)):
            block = jnp.zeros((length, depth), F32)
            for q in range(replicas):
                block += dot_nt(pieces[q][:, part:], source[q, k * depth : (k + 1) * depth])
            at = ((who[2] ^ flip) * (groups // 2) + k) * depth
            mixed[:, pl.ds(pl.multiple_of(at, depth), depth)] = block.astype(BF)
    for q in range(replicas):
        here = pl.ds(pl.multiple_of((who[0] ^ q) * part, part), part)
        pieces[q][:, :part] = mixed[:, here]


def back_step(who, shares, hidden, normed, cot, gain, gates, router, near, far, experts):
    replicas = near.shape[0]
    length, width = hidden.shape
    groups = 2 * len(shares)
    vmem = pl.BlockSpec(memory_space=pltpu.VMEM)
    piece = jax.ShapeDtypeStruct((length, 2 * width // replicas), BF)
    results = pl.pallas_call(
        functools.partial(back_kernel, replicas, groups, experts),
        in_specs=[pl.BlockSpec(memory_space=pltpu.SMEM)] + [vmem] * (len(shares) + 8),
        out_specs=[vmem] * (3 + replicas),
        scratch_shapes=[pltpu.VMEM((length, width), BF)],
        out_shape=[
            jax.ShapeDtypeStruct((length, width), F32),
            jax.ShapeDtypeStruct((1, width), F32),
            jax.ShapeDtypeStruct((width, router.shape[1]), BF),
            *[piece] * replicas,
        ],
        compiler_params=pltpu.CompilerParams(vmem_limit_bytes=60 * 2**20),
        cost_estimate=pl.CostEstimate(flops=10**11, bytes_accessed=0, transcendentals=0),
        name="attention_back",
    )(who, *shares, hidden, normed, cot, gain, gates, router, near, far)
    return results[0], results[1], results[2], results[3:]


def turn(value, cosine, sine):
    return value * cosine + pltpu.roll(value, value.shape[1] // 2, 1) * sine


def attend_kernel(heads, normed, weight, seg_row, seg_col, cosine, sine, gains, *outs):
    raw, ready, mixed, totals, tops = outs
    allowed = seg_col[0] == seg_row[0]
    lane = lax.broadcasted_iota(jnp.int32, totals.shape, 1)
    top_lane = lax.broadcasted_iota(jnp.int32, tops.shape[1:], 1)
    part = heads * HD
    totals[...] = jnp.zeros(totals.shape, F32)
    tops[0] = jnp.zeros(tops.shape[1:], F32)
    for i in range(2):
        raw[:, i * part : (i + 1) * part] = dot(normed[...], weight[:, i * part : (i + 1) * part])
    ready[:, 2 * part :] = dot(normed[...], weight[:, 2 * part : 3 * part]).astype(BF)
    for h in range(heads):
        rotated = []
        for i in range(2):
            at = slice(i * part + h * HD, i * part + (h + 1) * HD)
            head = raw[:, at]
            norm = lax.rsqrt(jnp.mean(head * head, axis=1, keepdims=True) + epsilon)
            rotated.append(turn(head * norm * gains[i : i + 1], cosine[...], sine[...]).astype(BF))
            ready[:, at] = rotated[i]
        scores = dot_nt(rotated[0], rotated[1]) * HD**-0.5
        scores = jnp.where(allowed, scores, -1e30)
        peak = jnp.max(scores, axis=1, keepdims=True)
        powers = jnp.exp(scores - peak)
        total = peak + jnp.log(jnp.sum(powers, axis=1, keepdims=True))
        weights = jnp.exp(scores - total).astype(BF)
        here = slice(h * HD, (h + 1) * HD)
        mixed[:, here] = dot(weights, ready[:, 2 * part + h * HD : 2 * part + (h + 1) * HD]).astype(BF)
        totals[...] = jnp.where(lane == h, total, totals[...])
        tops[0] = jnp.where(top_lane == h, jnp.max(peak, axis=0, keepdims=True), tops[0])


def attend(normed, weight, segments, cosine, sine, gains, heads):
    count, length = segments.shape
    rows, width = normed.shape
    part = heads * HD
    one = lambda n: (n, 0)
    fixed = lambda n: (0, 0)
    return pl.pallas_call(
        functools.partial(attend_kernel, heads),
        grid=(count,),
        in_specs=[
            pl.BlockSpec((length, width), one),
            pl.BlockSpec((width, 3 * part), fixed, pipeline_mode=pl.Buffered(1)),
            pl.BlockSpec((1, 1, length), lambda n: (n, 0, 0)),
            pl.BlockSpec((1, length, 1), lambda n: (n, 0, 0)),
            pl.BlockSpec((length, HD), fixed),
            pl.BlockSpec((length, HD), fixed),
            pl.BlockSpec((2, HD), fixed),
        ],
        out_specs=[
            pl.BlockSpec((length, 2 * part), one),
            pl.BlockSpec((length, 3 * part), one),
            pl.BlockSpec((length, part), one),
            pl.BlockSpec((length, 128), one),
            pl.BlockSpec((1, 1, 128), lambda n: (n, 0, 0)),
        ],
        out_shape=[
            jax.ShapeDtypeStruct((rows, 2 * part), F32),
            jax.ShapeDtypeStruct((rows, 3 * part), BF),
            jax.ShapeDtypeStruct((rows, part), BF),
            jax.ShapeDtypeStruct((rows, 128), F32),
            jax.ShapeDtypeStruct((count, 1, 128), F32),
        ],
        compiler_params=pltpu.CompilerParams(vmem_limit_bytes=60 * 2**20),
        cost_estimate=pl.CostEstimate(flops=0, bytes_accessed=0, transcendentals=0),
        name="attention",
    )(normed, weight, segments[:, None, :], segments[:, :, None], cosine, sine, gains)


def attend_back_kernel(heads, pull, raw, ready, totals, seg_row, seg_col, cosine, sine, gains, grad, gain_grads):
    allowed = seg_col[0] == seg_row[0]
    lane = lax.broadcasted_iota(jnp.int32, totals.shape, 1)
    part = heads * HD
    sums = [jnp.zeros((1, HD), F32)] * 2
    for h in range(heads):
        at = [slice(i * part + h * HD, i * part + (h + 1) * HD) for i in range(3)]
        query, key, value = (ready[:, a] for a in at)
        pulled = pull[:, h * HD : (h + 1) * HD]
        total = jnp.sum(jnp.where(lane == h, totals[...], 0.0), axis=1, keepdims=True)
        scores = dot_nt(query, key) * HD**-0.5
        probs = jnp.where(allowed, jnp.exp(jnp.where(allowed, scores - total, 0.0)), 0.0)
        grad_weights = dot_nt(pulled, value)
        grad[:, at[2]] = dot_tn(probs.astype(BF), pulled).astype(BF)
        inner = jnp.sum(probs * grad_weights, axis=1, keepdims=True)
        grad_scores = (probs * (grad_weights - inner)).astype(BF)
        both = (dot(grad_scores, key), dot_tn(grad_scores, query))
        for i, g in enumerate(both):
            g = g * HD**-0.5
            back = g * cosine[...] - pltpu.roll(g, HD // 2, 1) * sine[...]
            head = raw[:, at[i]]
            norm = lax.rsqrt(jnp.mean(head * head, axis=1, keepdims=True) + epsilon)
            sums[i] = sums[i] + jnp.sum(back * head * norm, axis=0, keepdims=True)
            scaled = back * gains[i : i + 1]
            mean = jnp.mean(scaled * head, axis=1, keepdims=True)
            grad[:, at[i]] = (norm * scaled - head * (norm * norm * norm * mean)).astype(BF)
    for i in range(2):
        gain_grads[0, i : i + 1] = sums[i]


def attend_back(pull, raw, ready, totals, segments, cosine, sine, gains, heads):
    count, length = segments.shape
    rows = raw.shape[0]
    part = heads * HD
    one = lambda n: (n, 0)
    fixed = lambda n: (0, 0)
    return pl.pallas_call(
        functools.partial(attend_back_kernel, heads),
        grid=(count,),
        in_specs=[
            pl.BlockSpec((length, part), one),
            pl.BlockSpec((length, 2 * part), one),
            pl.BlockSpec((length, 3 * part), one),
            pl.BlockSpec((length, 128), one),
            pl.BlockSpec((1, 1, length), lambda n: (n, 0, 0)),
            pl.BlockSpec((1, length, 1), lambda n: (n, 0, 0)),
            pl.BlockSpec((length, HD), fixed),
            pl.BlockSpec((length, HD), fixed),
            pl.BlockSpec((2, HD), fixed),
        ],
        out_specs=[
            pl.BlockSpec((length, 3 * part), one),
            pl.BlockSpec((1, 2, HD), lambda n: (n, 0, 0)),
        ],
        out_shape=[
            jax.ShapeDtypeStruct((rows, 3 * part), BF),
            jax.ShapeDtypeStruct((count, 2, HD), F32),
        ],
        compiler_params=pltpu.CompilerParams(vmem_limit_bytes=32 * 2**20),
        cost_estimate=pl.CostEstimate(
            flops=0, bytes_accessed=0, transcendentals=0
        ),
        name="attention_grad",
    )(pull, raw, ready, totals, segments[:, None, :], segments[:, :, None], cosine, sine, gains)


def weight_grad_kernel(half, quarters, left, right, *outs):
    j, i = pl.program_id(0), pl.program_id(1)
    block = dot_tn(left[0], right[0]).astype(BF)
    for at, out in enumerate(outs):

        @pl.when((j == at // 2) & ((i >= half) == (at % 2 == 1)))
        def _(out=out):
            out[0] = block


def weight_grads(quarters, left, right, parts, cost):
    count, rows, width = left.shape
    size, n = width // parts, right.shape[2]
    half = parts // 2

    def spot(at):
        def index(j, i, quarters):
            step = j * parts + i - (at // 2 * parts + at % 2 * half)
            return (jnp.clip(step, 0, half - 1), 0, 0)

        return index

    return pl.pallas_call(
        functools.partial(weight_grad_kernel, half),
        grid_spec=pltpu.PrefetchScalarGridSpec(
            num_scalar_prefetch=1,
            grid=(count, parts),
            in_specs=[
                pl.BlockSpec((1, rows, size), lambda j, i, quarters: (j, 0, quarters[j, i])),
                pl.BlockSpec((1, rows, n), lambda j, i, quarters: (j, 0, 0)),
            ],
            out_specs=[pl.BlockSpec((1, size, n), spot(at)) for at in range(2 * count)],
        ),
        out_shape=[jax.ShapeDtypeStruct((half, size, n), BF)] * (2 * count),
        compiler_params=pltpu.CompilerParams(vmem_limit_bytes=56 * 2**20),
        cost_estimate=pl.CostEstimate(flops=cost, bytes_accessed=0, transcendentals=0),
        name="weight_grads",
    )(quarters, left, right)


def product_kernel(left, right, out):
    out[...] = dot_tn(left[...], right[...]).astype(BF)


def product(left, right):
    rows, width = left.shape
    n = right.shape[1]
    size = min(width, 256)
    return pl.pallas_call(
        product_kernel,
        grid=(width // size,),
        in_specs=[
            pl.BlockSpec((rows, size), lambda i: (0, i)),
            pl.BlockSpec((rows, n), lambda i: (0, 0)),
        ],
        out_specs=pl.BlockSpec((size, n), lambda i: (i, 0)),
        out_shape=jax.ShapeDtypeStruct((width, n), BF),
        compiler_params=pltpu.CompilerParams(vmem_limit_bytes=32 * 2**20),
        cost_estimate=pl.CostEstimate(flops=0, bytes_accessed=0, transcendentals=0),
        name="product",
    )(left, right)


def spread_kernel(grad, weight, *outs):
    block = dot_nt(grad[...], weight[...]).astype(BF)
    for at, out in enumerate(outs):

        @pl.when(pl.program_id(0) == at)
        def _(out=out):
            out[...] = block


def normed_grads(grad, weight, count):
    rows, n = grad.shape
    width = weight.shape[0]
    length = rows // count
    return pl.pallas_call(
        spread_kernel,
        grid=(count,),
        in_specs=[
            pl.BlockSpec((length, n), lambda i: (i, 0)),
            pl.BlockSpec((width, n), lambda i: (0, 0), pipeline_mode=pl.Buffered(1)),
        ],
        out_specs=[pl.BlockSpec((length, width), lambda i: (0, 0))] * count,
        out_shape=[jax.ShapeDtypeStruct((length, width), BF)] * count,
        compiler_params=pltpu.CompilerParams(vmem_limit_bytes=48 * 2**20),
        cost_estimate=pl.CostEstimate(flops=0, bytes_accessed=0, transcendentals=0),
        name="normed_grads",
    )(grad, weight)


def halve_kernel(half, blocks, keep, got, send_out, keep_out):
    block = (keep[0].astype(F32) + got[0].astype(F32)).astype(BF)

    @pl.when(pl.program_id(0) < half)
    def _():
        send_out[0] = block

    @pl.when(pl.program_id(0) >= half)
    def _():
        keep_out[0] = block


def halve(blocks, keep, got, cost):
    count, size, n = keep.shape
    half = count // 2
    here = pl.BlockSpec((1, size, n), lambda i, blocks: (blocks[i], 0, 0))
    return pl.pallas_call(
        functools.partial(halve_kernel, half),
        grid_spec=pltpu.PrefetchScalarGridSpec(
            num_scalar_prefetch=1,
            grid=(count,),
            in_specs=[here, here],
            out_specs=[
                pl.BlockSpec((1, size, n), lambda i, blocks: (jnp.minimum(i, half - 1), 0, 0)),
                pl.BlockSpec((1, size, n), lambda i, blocks: (jnp.maximum(i - half, 0), 0, 0)),
            ],
        ),
        out_shape=[jax.ShapeDtypeStruct((half, size, n), BF)] * 2,
        compiler_params=pltpu.CompilerParams(vmem_limit_bytes=32 * 2**20),
        cost_estimate=pl.CostEstimate(flops=cost, bytes_accessed=0, transcendentals=0),
        name="halve",
    )(blocks, keep, got)


def join_kernel(*refs):
    out = refs[-1]
    for j in range((len(refs) - 1) // 2):

        @pl.when(pl.program_id(0) == j)
        def _(j=j):
            out[0] = refs[2 * j][...].astype(F32) + refs[2 * j + 1][...].astype(F32)


def join(pairs, cost):
    size, n = pairs[0][0].shape
    step = min(size, 256)
    count = len(pairs)

    def spot(at):
        def index(j, i):
            k = j * (size // step) + i - at * (size // step)
            return (jnp.clip(k, 0, size // step - 1), 0)

        return index

    return pl.pallas_call(
        join_kernel,
        grid=(count, size // step),
        in_specs=[pl.BlockSpec((step, n), spot(at // 2)) for at in range(2 * count)],
        out_specs=pl.BlockSpec((1, step, n), lambda j, i: (j, i, 0)),
        out_shape=jax.ShapeDtypeStruct((count, size, n), F32),
        compiler_params=pltpu.CompilerParams(vmem_limit_bytes=60 * 2**20),
        cost_estimate=pl.CostEstimate(flops=cost, bytes_accessed=0, transcendentals=0),
        name="join",
    )(*[v for pair in pairs for v in pair])


def input_kernel(count, heads, who, *refs):
    pieces = refs[:count]
    tokens, gain, grad_hidden, ffn, gains, tops, grad, small = refs[count:]
    width = tokens.shape[1]
    pulled = pieces[0][...].astype(F32)
    for piece in pieces[1:]:
        pulled = pulled + piece[...].astype(F32)
    value = tokens[...].astype(F32)
    scale = lax.rsqrt(jnp.mean(value * value, axis=1, keepdims=True) + epsilon)
    small[:, :width] = jnp.sum(pulled * value * scale, axis=0, keepdims=True)
    small[:, width : 2 * width] = ffn[...]
    for i in range(2):
        at = 2 * width + i * HD
        small[:, at : at + HD] = jnp.sum(gains[:, i], axis=0, keepdims=True)
    top = jnp.max(tops[:, 0], axis=0, keepdims=True)
    lane = lax.broadcasted_iota(jnp.int32, top.shape, 1)
    top = jnp.where(lane < heads, top, -3e38)
    small[:, 2 * width + 2 * HD :] = pltpu.roll(top, who[0] * heads, 1)
    pulled = pulled * gain[...]
    inner = jnp.mean(pulled * value, axis=1, keepdims=True)
    back = scale * pulled - value * (scale * scale * scale * inner)
    grad[...] = (grad_hidden[...] + back).astype(BF)


def input_step(who, pieces, tokens, gain, grad_hidden, ffn, gains, tops, heads):
    length, width = tokens.shape
    vmem = pl.BlockSpec(memory_space=pltpu.VMEM)
    return pl.pallas_call(
        functools.partial(input_kernel, len(pieces), heads),
        in_specs=[pl.BlockSpec(memory_space=pltpu.SMEM)] + [vmem] * (len(pieces) + 6),
        out_specs=[vmem] * 2,
        out_shape=[
            jax.ShapeDtypeStruct((length, width), BF),
            jax.ShapeDtypeStruct((1, 2 * width + 2 * HD + 128), F32),
        ],
        compiler_params=pltpu.CompilerParams(vmem_limit_bytes=60 * 2**20),
        cost_estimate=pl.CostEstimate(flops=10**11, bytes_accessed=0, transcendentals=0),
        name="input_grad",
    )(who, *pieces, tokens, gain, grad_hidden, ffn, gains, tops)


def gather_kernel(count, arrays, who, *refs):
    blocks, outs = refs[:count], refs[count:]
    part = outs[0].shape[1] // count
    total = 0.0
    for k, block in enumerate(blocks):
        here = pl.ds(pl.multiple_of((who[0] ^ k) * part, part), part)
        for i in range(arrays):
            outs[i][:, here] = block[:, i * part : (i + 1) * part].astype(F32)
        if len(outs) > arrays:
            total += block[:, arrays * part :].astype(F32)
    if len(outs) > arrays:
        outs[-1][...] = total


def gather_step(who, blocks, arrays):
    rows, wide = blocks[0].shape
    lanes = 128 if wide % (arrays * 256) else 0
    part = (wide - lanes) // arrays
    count = len(blocks)
    vmem = pl.BlockSpec(memory_space=pltpu.VMEM)
    return pl.pallas_call(
        functools.partial(gather_kernel, count, arrays),
        in_specs=[pl.BlockSpec(memory_space=pltpu.SMEM)] + [vmem] * count,
        out_specs=[vmem] * (arrays + (lanes > 0)),
        out_shape=[jax.ShapeDtypeStruct((rows, part * count), F32)] * arrays
        + [jax.ShapeDtypeStruct((rows, lanes), F32)] * (lanes > 0),
        compiler_params=pltpu.CompilerParams(vmem_limit_bytes=48 * 2**20),
        cost_estimate=pl.CostEstimate(flops=0, bytes_accessed=0, transcendentals=0),
        name="gather_columns",
    )(who, *blocks)


def merge_kernel(sums, *refs):
    out = refs[-1]
    total = refs[0][...]
    lane = lax.broadcasted_iota(jnp.int32, total.shape, 1)
    for ref in refs[1:-1]:
        other = ref[...]
        total = jnp.where(lane < sums, total + other, jnp.maximum(total, other))
    out[...] = total


def merge(sums, *values):
    vmem = pl.BlockSpec(memory_space=pltpu.VMEM)
    return pl.pallas_call(
        functools.partial(merge_kernel, sums),
        in_specs=[vmem] * len(values),
        out_specs=vmem,
        out_shape=jax.ShapeDtypeStruct(values[0].shape, F32),
        cost_estimate=pl.CostEstimate(flops=0, bytes_accessed=0, transcendentals=0),
        name="merge",
    )(*values)


def local(
    tokens,
    cotangent,
    segment_ids,
    expert_index,
    clip_threshold,
    attn_norm_gain,
    w_query,
    w_key,
    w_value,
    w_output,
    query_gain,
    key_gain,
    ffn_norm_gain,
    router,
    expert_in,
    expert_out,
):
    replicas = lax.axis_size("replica")
    groups = lax.axis_size("fsdp")
    me_r = lax.axis_index("replica")
    me_f = lax.axis_index("fsdp")
    core = me_f % 2
    length, width = tokens.shape
    part = width // replicas
    heads = part // HD
    ff = expert_out.shape[1]
    local_experts = expert_in.shape[0]
    scale = HD ** (-0.5)
    attn_gain = attn_norm_gain.astype(F32)
    ffn_gain = ffn_norm_gain.astype(F32)
    gain_query = query_gain.astype(F32)
    gain_key = key_gain.astype(F32)

    def swap(value, k):
        return lax.ppermute(value, "replica", [(r, r ^ k) for r in range(replicas)])

    def columns(value, k, axis=1):
        return lax.dynamic_slice_in_dim(value, (me_r ^ k) * part, part, axis)

    def spread(value):
        return [value] + [swap(value, k) for k in range(1, replicas)]

    def trade_columns(value):
        return [columns(value, 0)] + [swap(columns(value, k), k) for k in range(1, replicas)]

    def join_columns(blocks):
        out = jnp.zeros((blocks[0].shape[0], part * replicas), blocks[0].dtype)
        for k, block in enumerate(blocks):
            out = lax.dynamic_update_slice_in_dim(out, block, (me_r ^ k) * part, 1)
        return out

    def cross(value, k):
        return lax.ppermute(value, "fsdp", [(f, f ^ k) for f in range(groups)])

    def pass_on(up, down, hop):
        chips = groups // 2
        pairs = [(2 * a + i, 2 * a + 2 + i) for a in range(hop - 1, chips - 1) for i in (0, 1)]
        back = [(2 * a + 2 + i, 2 * a + i) for a in range(chips - hop) for i in (0, 1)]
        return lax.ppermute(up, "fsdp", pairs), lax.ppermute(down, "fsdp", back)

    def choose(up, down, k):
        chips = groups // 2
        found = {}
        for a in range(chips):
            b = a ^ k
            found.setdefault((b > a, abs(b - a)), []).append(a)
        picked = None
        for (above, hop), at in found.items():
            source = down[hop] if above else up[hop]
            if picked is None:
                picked = source
            else:
                here = functools.reduce(jnp.logical_or, [me_f // 2 == a for a in at])
                picked = jnp.where(here, source, picked)
        return picked

    def gather(value):
        return lax.all_gather(value, "fsdp", axis=0, tiled=True)

    def reduce(value):
        return lax.psum_scatter(value, "fsdp", scatter_dimension=0, tiled=True)

    bits = replicas.bit_length() - 1

    def next_bit(j, step):
        return 1 << (bits - 1 - step if j % 2 else step)

    def next_halves(traded, j, step, cost=0):
        keep, got = traded
        left = keep.shape[0]
        place = jnp.arange(left, dtype=jnp.int32)
        here = left // 2 if j % 2 else 1
        mine = (me_r & next_bit(j, step)) != 0
        other = ((place & here) != 0) != mine
        spots = jnp.where(other, jnp.cumsum(other) - 1, left // 2 + jnp.cumsum(~other) - 1)
        return halve(jnp.zeros((left,), jnp.int32).at[spots].set(place), keep, got, cost)

    index_table = expert_index.astype(BF).reshape(w_query.shape[0], -1)
    sent = [columns(w_output, 0), router, index_table]
    sizes = [v.shape[1] for v in sent]
    sent.append(jnp.zeros((w_query.shape[0], -sum(sizes) % 128), BF))
    quarter = gather(jnp.concatenate(sent, axis=1))
    full_router = quarter[:, part : part + EXPERTS]
    full_index = quarter[:, part + EXPERTS : part + EXPERTS + sizes[2]].astype(jnp.int32)
    full_index = full_index.reshape(groups * length, -1)
    ids = jnp.arange(EXPERTS, dtype=jnp.int32)
    mask = jnp.any(full_index[:, :, None] == ids, axis=1).reshape(groups, length, EXPERTS)
    first = me_f * local_experts
    hot = lax.dynamic_slice_in_dim(mask, first, local_experts, 2)
    order = jnp.arange(length, dtype=jnp.int32)
    before = (order[:, None] < order[None, :]).astype(BF)
    rank = jnp.einsum("nsj,st->njt", hot.astype(BF), before, preferred_element_type=F32)
    rank = jnp.where(hot.transpose(0, 2, 1), rank.astype(jnp.int32), -1)
    slots = jnp.arange(CAP, dtype=jnp.int32)
    pick = (rank[:, :, None, :] == slots[:, None]).astype(BF)
    spots = (rank[:, :, :, None] == slots).astype(BF)
    lanes = 128
    mask_wide = jnp.pad(mask.astype(F32), ((0, 0), (0, 0), (0, lanes - EXPERTS)))
    router_wide = jnp.pad(full_router, ((0, 0), (0, lanes - EXPERTS)))
    tables = (pick, spots, mask_wide, router_wide)
    segments = spread(segment_ids)
    tokens_all = spread(after(tokens, *segments[1:]))
    segments = jnp.concatenate(segments, axis=0)
    normed = jnp.concatenate(
        [rms_norm(v.astype(F32), attn_gain).astype(BF) for v in tokens_all], axis=0
    )
    rounds = groups // 2
    where = jnp.stack([me_r, me_f // 2, core]).astype(jnp.int32)
    half = lax.dynamic_slice(quarter, (core * (width // 2), 0), (width // 2, part))
    near = spread(after(half, *tokens_all[1:]))
    near[1] = after(near[1], *tables, segments, normed)
    normed = after(normed, *near[1:])
    w_qkv = gather(jnp.concatenate([columns(w, 0) for w in (w_query, w_key, w_value)], axis=1))
    cot_all = gather(cotangent)
    cot_pair = (cotangent, cross(cotangent, 1))

    cosine, sine = rope_tables(length, HD)
    cosine = jnp.concatenate([cosine, cosine], axis=1)
    sine = jnp.concatenate([-sine, sine], axis=1)
    gains = jnp.stack([gain_query, gain_key])
    raw, ready, mixed_heads, totals, tops = attend(normed, w_qkv, segments, cosine, sine, gains, heads
    )
    near = jnp.stack([after(near[0], raw), *near[1:]])
    far = cross(near, 1)
    mixed_heads = mixed_heads.reshape(replicas, length, part)
    pieces = [mixed_heads[0]] + [swap(mixed_heads[k], k) for k in range(1, replicas)]
    inputs = tokens.astype(F32)
    hidden, normed_ffn, mixed = out_step(where, pieces, near, far, tokens, ffn_gain[None, :])
    mixed_all = spread(mixed)

    def first_bit(j):
        return 1 << (bits - 1 if j % 2 else 0)

    numbers = jnp.arange(replicas, dtype=jnp.int32)
    quarters = []
    for j in range(local_experts):
        other = ((numbers ^ me_r) & first_bit(j)) != 0
        place = jnp.where(other, jnp.cumsum(other) - 1, replicas // 2 + jnp.cumsum(~other) - 1)
        quarters.append(jnp.zeros((replicas,), jnp.int32).at[place].set(numbers))
    quarters = jnp.stack(quarters)
    kept = None
    shares = []
    added = []
    pending = []
    up, down = [normed_ffn], [normed_ffn]
    for k in range(rounds):
        chip = (me_f // 2) ^ k
        who = jnp.stack([2 * chip + core, 2 * chip + 1 - core, chip, core, first])
        if k + 1 < rounds:
            next_up, next_down = pass_on(up[-1], down[-1], k + 1)
        mine = choose(up, down, k) if k else normed_ffn
        nf = (mine, cross(mine, 1))
        kept, back_a, back_b = expert_block(k, rounds, who, nf, (cot_all,) if k else cot_pair, pick, spots, mask_wide, router_wide, expert_in, expert_out, kept, pending
        )
        if k + 1 < rounds:
            up.append(after(next_up, back_a))
            down.append(after(next_down, back_a))
        else:
            rows, grad_projected, cot_rows, scaled, moe = kept
            out_blocks = weight_grads(quarters, after(scaled, mixed_all[-1]), cot_rows, replicas, 0)
        if k == rounds - 1:
            back_b = after(back_b, *out_blocks, *shares[1:])
        share = (back_a.astype(F32) + cross(back_b, 1).astype(F32)).astype(BF)
        added.append(share)
        if k == rounds - 2:
            pending = added[1:]
        else:
            pending = mixed_all[1:-1] if k == rounds - 3 else []
        shares.append(share if k == 0 else cross(share, 2 * k))
    out_traded = [
        (out_blocks[2 * j + 1], swap(out_blocks[2 * j], first_bit(j))) for j in range(local_experts)
    ]
    in_blocks = weight_grads(quarters, after(rows, share), grad_projected, replicas, 10**11)
    shares[-1] = after(shares[-1], *in_blocks, *[v[1] for v in out_traded])
    moe_sum = reduce(after(moe, shares[-1]))
    output = (hidden + moe_sum.astype(F32)).astype(BF)

    my_mask = lax.dynamic_index_in_dim(mask_wide, me_f, 0, keepdims=False) > 0.0
    logits = jnp.where(my_mask, dot(normed_ffn, router_wide), -jnp.inf)
    powers = jnp.exp(logits - jnp.max(logits, axis=1, keepdims=True))
    my_gates = powers / jnp.sum(powers, axis=1, keepdims=True)
    grad_hidden, ffn_gain_grad, router_grad, pieces = back_step(
        where, shares, hidden, normed_ffn, cotangent, ffn_gain[None, :], my_gates, router_wide, near, far, EXPERTS
    )
    grad_mixed = jnp.concatenate(
        [pieces[0]] + [swap(pieces[k], k) for k in range(1, replicas)], axis=0
    )
    sends = [
        after(in_blocks[2 * j], grad_mixed, *[v[1] for v in out_traded]) for j in range(local_experts)
    ]
    in_traded = [
        (in_blocks[2 * j + 1], swap(v, first_bit(j))) for j, v in enumerate(sends)
    ]
    ready = after(ready, *sends)
    grad_qkv, gain_grads = attend_back(grad_mixed, raw, ready, totals, segments, cosine, sine, gains, heads
    )
    qkv_grad = product(normed, grad_qkv)
    part_normed = normed_grads(grad_qkv, w_qkv, replicas)
    received = [v[1] for v in in_traded]
    received[0] = after(received[0], *received[1:], moe_sum)
    in_traded = [(v[0], got) for v, got in zip(in_traded, received)]
    in_halves = [next_halves(v, j, 1, 10**11) for j, v in enumerate(in_traded)]
    in_sends = [v for v, _ in in_halves]
    in_done = [(keep, swap(v, next_bit(j, 1))) for j, (v, keep) in enumerate(in_halves)]
    mixed_rows = jnp.concatenate([mixed_all[0], after(mixed_all[1], *in_sends), *mixed_all[2:]], axis=0)
    output_grad = dot_tn(mixed_rows, grad_mixed[:, part:])
    o_grad = jnp.concatenate([output_grad.astype(BF), router_grad], axis=1)
    share_o = reduce(o_grad)
    out_halves = [next_halves((k, after(v, part_normed[0])), j, 1) for j, (k, v) in enumerate(out_traded)]
    pieces = [after(part_normed[0], *in_sends, o_grad, *[v for v, _ in out_halves])]
    pieces += [swap(part_normed[k], k) for k in range(1, replicas)]
    input_grad, small = input_step(
        where, pieces, tokens, attn_gain[None, :], grad_hidden, ffn_gain_grad, gain_grads, tops, heads
    )
    second = [v[1] for v in in_done]
    share_qkv = reduce(qkv_grad)
    payload = after(jnp.concatenate([share_qkv, share_o], axis=1), *second, input_grad)
    if replicas == 4:
        across, along = swap(payload, 1), swap(payload, 2)
        cut_at = payload.shape[0] // 2
        upper = swap(across[:cut_at], 2)
        lower = swap(along[cut_at:], 1)
        blocks = [payload, across, along, jnp.concatenate([upper, lower], axis=0)]
    else:
        blocks = spread(payload)
    out_done = [
        (keep, swap(after(v, *second, moe_sum), next_bit(j, 1))) for j, (v, keep) in enumerate(out_halves)
    ]

    def settle(traded, cost):
        pairs = []
        for j, (keep, got) in enumerate(traded):
            for step in range(2, bits):
                send, keep = next_halves((keep, got), j, step)
                got = swap(send, next_bit(j, step))
            pairs.append((keep[0], got[0]))
        return join(pairs, cost)

    n_sums = 2 * width + 2 * HD
    small = merge(n_sums, small, cross(small, 1))
    small = merge(n_sums, small, *[cross(small, 2 * k) for k in range(1, rounds)])
    small = merge(n_sums, *spread(after(small, *second)))
    small = small[0]
    attn_gain_total = small[:width]
    ffn_gain_total = small[width : 2 * width]
    query_gain_total = small[2 * width : 2 * width + HD]
    key_gain_total = small[2 * width + HD : n_sums]
    head_max = small[n_sums : n_sums + replicas * heads]
    threshold = clip_threshold.astype(F32)
    factor = threshold / jnp.maximum(head_max, threshold)
    column_scale = jnp.repeat(jnp.sqrt(factor), HD)
    clipped_query = (w_query.astype(F32) * column_scale[None, :]).astype(BF)
    clipped_key = (w_key.astype(F32) * column_scale[None, :]).astype(BF)
    expert_in_grad = settle(
        [(keep, after(v, clipped_query, clipped_key, output)) for keep, v in in_done], 10**11
    )
    expert_out_grad = settle([(k, after(v, expert_in_grad)) for k, v in out_done], 0)

    blocks[1] = after(blocks[1], expert_in_grad)
    total_query, total_key, total_value, total_output, total_router = gather_step(where, blocks, 4)
    total_router = total_router[:, :EXPERTS]
    return (
        output,
        input_grad,
        attn_gain_total,
        total_query,
        total_key,
        total_value,
        total_output,
        query_gain_total,
        key_gain_total,
        ffn_gain_total,
        total_router,
        expert_in_grad,
        expert_out_grad,
        head_max,
        clipped_query,
        clipped_key,
    )


def solution(mesh):
    both = ("replica", "fsdp")
    return jax.shard_map(
        local,
        mesh=mesh,
        in_specs=(
            P(both, None),
            P(both, None),
            P(both, None),
            P(both, None),
            P(),
            P(),
            P("fsdp", None),
            P("fsdp", None),
            P("fsdp", None),
            P("fsdp", None),
            P(),
            P(),
            P(),
            P("fsdp", None),
            P("fsdp", None, None),
            P("fsdp", None, None),
        ),
        out_specs=(
            P(both, None),
            P(both, None),
            P(),
            P("fsdp", None),
            P("fsdp", None),
            P("fsdp", None),
            P("fsdp", None),
            P(),
            P(),
            P(),
            P("fsdp", None),
            P("fsdp", "replica", None),
            P("fsdp", "replica", None),
            P(),
            P("fsdp", None),
            P("fsdp", None),
        ),
        check_vma=False,
    )
```

```python
import functools

import jax
import jax.numpy as jnp
from jax import lax
from jax.experimental import pallas as pl
from jax.experimental.pallas import tpu as pltpu
from jax.sharding import PartitionSpec as P

HD = 128
EXPERTS = 16
CAP = 144

epsilon = 1e-06
rope_base = 10000.0
BF = jnp.bfloat16
F32 = jnp.float32


def rms_norm(values, gain):
    return values * lax.rsqrt(jnp.mean(values * values, axis=-1, keepdims=True) + epsilon) * gain


def rope_tables(length, width):
    places = jnp.arange(length, dtype=F32)
    rates = rope_base ** (-jnp.arange(width // 2, dtype=F32) * 2.0 / width)
    angle = places[:, None] * rates[None, :]
    return jnp.cos(angle), jnp.sin(angle)


def rotate(values, cosine, sine):
    half = values.shape[-1] // 2
    first = values[..., :half]
    second = values[..., half:]
    return jnp.concatenate(
        [first * cosine - second * sine, second * cosine + first * sine], axis=-1
    )


def dot(left, right):
    return jnp.dot(left, right, preferred_element_type=F32)


def dot_tn(left, right):
    return lax.dot_general(left, right, (((0,), (0,)), ((), ())), preferred_element_type=F32)


def dot_nt(left, right):
    return lax.dot_general(left, right, (((1,), (1,)), ((), ())), preferred_element_type=F32)


EXTRA = 16


def nothing(*refs):
    pass


def after(value, *others):
    held = pl.BlockSpec(memory_space=pl.ANY)
    return pl.pallas_call(
        nothing,
        in_specs=[held] * (1 + len(others)),
        out_specs=held,
        out_shape=jax.ShapeDtypeStruct(value.shape, value.dtype),
        input_output_aliases={0: 0},
        name="after",
    )(value, *others)


def expert_kernel(tile, wide, unread, who, *refs):
    (nf_a, nf_b, cot_a, cot_b, pick_a, pick_b, spread_a, spread_b) = refs[:8]
    (mask_a, mask_b, router, w_in, w_out) = refs[8:13]
    refs = refs[13 + unread :]
    rows, gp, cot_rows, scaled, moe, back_a, back_b, gates_hi, gates_lo = refs
    j = pl.program_id(0)
    cap = pick_a.shape[2]
    length = nf_a.shape[0]
    ff = w_out.shape[1]
    core, expert = who[3], who[4] + j

    @pl.when(j == 0)
    def _():
        for at, (nf, mask) in enumerate(((nf_a, mask_a), (nf_b, mask_b))):
            seen = mask[0] > 0.0
            logits = jnp.where(seen, dot(nf[...], router[...]), -1e30)
            powers = jnp.where(seen, jnp.exp(logits - jnp.max(logits, axis=1, keepdims=True)), 0.0)
            gates = powers / jnp.sum(powers, axis=1, keepdims=True)
            high = gates.astype(BF)
            gates_hi[at] = high
            gates_lo[at] = (gates - high.astype(F32)).astype(BF)

    pa, pb = pick_a[0, 0], pick_b[0, 0]
    lane = lax.broadcasted_iota(jnp.int32, (cap, router.shape[1]), 1)

    def slot_gates(p, at):
        every = dot(p, gates_hi[at]) + dot(p, gates_lo[at])
        return jnp.sum(jnp.where(lane == expert, every, 0.0), axis=1, keepdims=True)

    gate = jnp.concatenate([slot_gates(pa, 0), slot_gates(pb, 1)], axis=0)
    rows[0, :cap] = dot(pa, nf_a[...]).astype(BF)
    rows[0, cap:] = dot(pb, nf_b[...]).astype(BF)
    cot_rows[0, :cap] = dot(pa, cot_a[...]).astype(BF)
    cot_rows[0, cap:] = dot(pb, cot_b[...]).astype(BF)

    def forward(t, total):
        at = pl.multiple_of(t * tile, tile)
        g = dot(rows[0], w_in[0, :, pl.ds(at, tile)])
        u = dot(rows[0], w_in[0, :, pl.ds(ff + at, tile)])
        pulled = dot_nt(cot_rows[0], w_out[0, pl.ds(at, tile), :])
        sigma = jax.nn.sigmoid(g)
        silu = g * sigma
        active = silu * u
        scaled[0, :, pl.ds(at, tile)] = (active * gate).astype(BF)
        ga = pulled * gate
        gp[0, :, pl.ds(at, tile)] = (ga * u * sigma * (1.0 + g * (1.0 - sigma))).astype(BF)
        gp[0, :, pl.ds(ff + at, tile)] = (ga * silu).astype(BF)
        return total + jnp.sum(active * pulled, axis=1, keepdims=True)

    total = lax.fori_loop(0, ff // tile, forward, jnp.zeros((2 * cap, 1), F32))
    line = lax.broadcasted_iota(jnp.int32, (EXTRA, length), 0)
    place = 2 * (core * pl.num_programs(0) + j)
    for back, p, part in ((back_a, pa, total[:cap]), (back_b, pb, total[cap:])):
        by_token = jnp.sum(p.astype(F32) * part, axis=0, keepdims=True)
        high = by_token.astype(BF).astype(F32)
        new = jnp.where(line == place, high, jnp.where(line == place + 1, by_token - high, 0.0))

        @pl.when(j == 0)
        def _(back=back):
            back[length:, :] = jnp.zeros((EXTRA, back.shape[1]), BF)

        old = back[length:, :length].astype(F32)
        back[length:, :length] = (old + new).astype(BF)
    sa, sb = spread_a[0, 0], spread_b[0, 0]
    moe_a = pl.ds(pl.multiple_of(core * length, length), length)
    moe_b = pl.ds(pl.multiple_of((1 - core) * length, length), length)

    def backward(t, _):
        here = pl.ds(pl.multiple_of(t * wide, wide), wide)
        gr = dot_nt(gp[0], w_in[0, here, :]).astype(BF)
        res = dot(scaled[0], w_out[0, :, here]).astype(BF)
        for out, where, s, value in (
            (back_a, pl.ds(0, length), sa, gr[:cap]),
            (back_b, pl.ds(0, length), sb, gr[cap:]),
            (moe, moe_a, sa, res[:cap]),
            (moe, moe_b, sb, res[cap:]),
        ):
            old = jnp.where(j > 0, out[where, here].astype(F32), 0.0)
            out[where, here] = (dot(s, value) + old).astype(BF)
        return 0

    lax.fori_loop(0, w_in.shape[1] // wide, backward, 0)


def expert_block(k, rounds, who, nf, cot, pick, spread, mask, router, w_in, w_out, kept, first):
    length, width = nf[0].shape
    count, _, two_ff = w_in.shape
    groups = pick.shape[0]
    ff = two_ff // 2
    cap = pick.shape[2]
    lanes = router.shape[1]

    def whole(j, who):
        return (0, 0)

    def seq(i):
        return lambda j, who: (who[i], j, 0, 0)

    in_specs = [pl.BlockSpec((length, width), whole)] * 2
    if len(cot) == 2:
        in_specs += [pl.BlockSpec((length, width), whole)] * 2
    else:
        cot = [cot[0]] * 2
        in_specs += [
            pl.BlockSpec((length, width), lambda j, who, i=i: (who[i], 0)) for i in range(2)
        ]
    in_specs += [pl.BlockSpec((1, 1, cap, length), seq(i)) for i in range(2)]
    in_specs += [pl.BlockSpec((1, 1, length, cap), seq(i)) for i in range(2)]
    in_specs += [
        pl.BlockSpec((1, length, lanes), lambda j, who, i=i: (who[i], 0, 0)) for i in range(2)
    ]
    in_specs += [
        pl.BlockSpec((width, lanes), whole),
        pl.BlockSpec((1, width, two_ff), lambda j, who: (j, 0, 0)),
        pl.BlockSpec((1, ff, width), lambda j, who: (j, 0, 0)),
    ]
    args = [*nf, *cot, pick, pick, spread, spread, mask, mask, router, w_in, w_out]
    total = rounds * 2 * cap
    saved = [(count, total, n) for n in (width, two_ff, width, ff)]
    out_shape = [jax.ShapeDtypeStruct(s, BF) for s in saved]
    out_shape += [jax.ShapeDtypeStruct((groups * length, width), BF)]
    out_shape += [jax.ShapeDtypeStruct((length + EXTRA, width), BF)] * 2
    out_specs = [pl.BlockSpec((1, 2 * cap, s[2]), lambda j, who: (j, k, 0)) for s in saved]
    out_specs += [pl.BlockSpec((2 * length, width), lambda j, who: (who[2], 0))]
    out_specs += [pl.BlockSpec((length + EXTRA, width), whole)] * 2
    aliases = {}
    if kept is not None:
        aliases = {1 + len(args) + i: i for i in range(len(kept))}
        in_specs += [pl.BlockSpec(memory_space=pl.ANY)] * len(kept)
        args += list(kept)
    in_specs += [pl.BlockSpec(memory_space=pl.ANY)] * len(first)
    args += list(first)
    results = pl.pallas_call(
        functools.partial(expert_kernel, min(512, ff), min(1024, width), len(aliases) + len(first)),
        grid_spec=pltpu.PrefetchScalarGridSpec(
            num_scalar_prefetch=1,
            grid=(count,),
            in_specs=in_specs,
            out_specs=out_specs,
            scratch_shapes=[pltpu.VMEM((2, length, lanes), BF)] * 2,
        ),
        out_shape=out_shape,
        input_output_aliases=aliases,
        compiler_params=pltpu.CompilerParams(vmem_limit_bytes=60 * 2**20),
        cost_estimate=pl.CostEstimate(
            flops=count * 2 * cap * width * ff * 12 * 2,
            bytes_accessed=count * 3 * width * ff * 2 + 20 * length * width * 2,
            transcendentals=0,
        ),
        name="experts",
    )(who, *args)
    return results[:5], results[5], results[6]


def out_kernel(replicas, groups, who, *refs):
    pieces = refs[:replicas]
    near, far, tokens, gain = refs[replicas : replicas + 4]
    hidden, normed, mixed = refs[replicas + 4 :]
    part = pieces[0].shape[1]
    depth = near.shape[1] // (groups // 2)
    for q in range(replicas):
        mixed[:, pl.ds(pl.multiple_of((who[0] ^ q) * part, part), part)] = pieces[q][...]
    for q in range(replicas):
        total = jnp.zeros((tokens.shape[0], part), F32)
        for k in range(groups // 2):
            for flip, source in enumerate((near, far)):
                at = ((who[2] ^ flip) * (groups // 2) + k) * depth
                left = mixed[:, pl.ds(pl.multiple_of(at, depth), depth)]
                total += dot(left, source[q, k * depth : (k + 1) * depth])
        here = pl.ds(pl.multiple_of((who[0] ^ q) * part, part), part)
        hidden[:, here] = tokens[:, here].astype(F32) + total
    value = hidden[...]
    scale = lax.rsqrt(jnp.mean(value * value, axis=1, keepdims=True) + epsilon)
    normed[...] = (value * scale * gain[...]).astype(BF)


def out_step(who, pieces, near, far, tokens, gain):
    replicas = len(pieces)
    length, width = tokens.shape
    groups = lax.axis_size("fsdp")
    vmem = pl.BlockSpec(memory_space=pltpu.VMEM)
    return pl.pallas_call(
        functools.partial(out_kernel, replicas, groups),
        in_specs=[pl.BlockSpec(memory_space=pltpu.SMEM)] + [vmem] * (replicas + 4),
        out_specs=[vmem] * 3,
        out_shape=[
            jax.ShapeDtypeStruct((length, width), F32),
            jax.ShapeDtypeStruct((length, width), BF),
            jax.ShapeDtypeStruct((length, width), BF),
        ],
        compiler_params=pltpu.CompilerParams(vmem_limit_bytes=48 * 2**20),
        name="attention_out",
    )(who, *pieces, near, far, tokens, gain)


def back_kernel(replicas, groups, experts, who, *refs):
    rounds = groups // 2
    shares = refs[:rounds]
    hidden, normed, cot, gain, gates, router, near, far = refs[rounds : rounds + 8]
    grad_hidden, gain_grad, router_grad = refs[rounds + 8 : rounds + 11]
    pieces = refs[rounds + 11 : rounds + 11 + replicas]
    mixed = refs[rounds + 11 + replicas]
    length, width = hidden.shape
    lanes = router.shape[1]
    part = width // replicas
    depth = width // groups
    per_chip = experts // rounds
    line = lax.broadcasted_iota(jnp.int32, (EXTRA, lanes), 0)
    lane = lax.broadcasted_iota(jnp.int32, (EXTRA, lanes), 1)
    summed = jnp.zeros((length, width), F32)
    grad_gates = jnp.zeros((length, lanes), F32)
    for k in range(rounds):
        summed += shares[k][:length].astype(F32)
        chip = who[1] ^ k
        place = (lane == chip * per_chip + line // 2) & (line < 2 * per_chip)
        grad_gates += dot_tn(shares[k][length:, :length], place.astype(BF))
    own = gates[...]
    centered = grad_gates - jnp.sum(own * grad_gates, axis=1, keepdims=True)
    grad_logits = (own * centered).astype(BF)
    router_grad[...] = dot_tn(normed[...], grad_logits).astype(BF)
    grad_normed = summed + dot_nt(grad_logits, router[...])
    value = hidden[...]
    scale = lax.rsqrt(jnp.mean(value * value, axis=1, keepdims=True) + epsilon)
    gain_grad[...] = jnp.sum(grad_normed * value * scale, axis=0, keepdims=True)
    pulled = grad_normed * gain[...]
    inner = jnp.mean(pulled * value, axis=1, keepdims=True)
    total = cot[...].astype(F32) + scale * pulled - value * (scale * scale * scale * inner)
    grad_hidden[...] = total
    for q in range(replicas):
        here = pl.ds(pl.multiple_of((who[0] ^ q) * part, part), part)
        pieces[q][:, part:] = grad_hidden[:, here].astype(BF)
    for k in range(rounds):
        for flip, source in enumerate((near, far)):
            block = jnp.zeros((length, depth), F32)
            for q in range(replicas):
                block += dot_nt(pieces[q][:, part:], source[q, k * depth : (k + 1) * depth])
            at = ((who[2] ^ flip) * (groups // 2) + k) * depth
            mixed[:, pl.ds(pl.multiple_of(at, depth), depth)] = block.astype(BF)
    for q in range(replicas):
        here = pl.ds(pl.multiple_of((who[0] ^ q) * part, part), part)
        pieces[q][:, :part] = mixed[:, here]


def back_step(who, shares, hidden, normed, cot, gain, gates, router, near, far, experts):
    replicas = near.shape[0]
    length, width = hidden.shape
    groups = 2 * len(shares)
    vmem = pl.BlockSpec(memory_space=pltpu.VMEM)
    piece = jax.ShapeDtypeStruct((length, 2 * width // replicas), BF)
    results = pl.pallas_call(
        functools.partial(back_kernel, replicas, groups, experts),
        in_specs=[pl.BlockSpec(memory_space=pltpu.SMEM)] + [vmem] * (len(shares) + 8),
        out_specs=[vmem] * (3 + replicas),
        scratch_shapes=[pltpu.VMEM((length, width), BF)],
        out_shape=[
            jax.ShapeDtypeStruct((length, width), F32),
            jax.ShapeDtypeStruct((1, width), F32),
            jax.ShapeDtypeStruct((width, router.shape[1]), BF),
            *[piece] * replicas,
        ],
        compiler_params=pltpu.CompilerParams(vmem_limit_bytes=48 * 2**20),
        cost_estimate=pl.CostEstimate(flops=10**11, bytes_accessed=0, transcendentals=0),
        name="attention_back",
    )(who, *shares, hidden, normed, cot, gain, gates, router, near, far)
    return results[0], results[1], results[2], results[3:]


def turn(value, cosine, sine):
    return value * cosine + pltpu.roll(value, value.shape[1] // 2, 1) * sine


def attend_kernel(heads, normed, weight, seg_row, seg_col, cosine, sine, gains, *outs):
    raw, ready, mixed, totals, tops = outs
    allowed = seg_col[0] == seg_row[0]
    lane = lax.broadcasted_iota(jnp.int32, totals.shape, 1)
    top_lane = lax.broadcasted_iota(jnp.int32, tops.shape[1:], 1)
    part = heads * HD
    totals[...] = jnp.zeros(totals.shape, F32)
    tops[0] = jnp.zeros(tops.shape[1:], F32)
    for i in range(2):
        raw[:, i * part : (i + 1) * part] = dot(normed[...], weight[:, i * part : (i + 1) * part])
    ready[:, 2 * part :] = dot(normed[...], weight[:, 2 * part : 3 * part]).astype(BF)
    for h in range(heads):
        rotated = []
        for i in range(2):
            at = slice(i * part + h * HD, i * part + (h + 1) * HD)
            head = raw[:, at]
            norm = lax.rsqrt(jnp.mean(head * head, axis=1, keepdims=True) + epsilon)
            rotated.append(turn(head * norm * gains[i : i + 1], cosine[...], sine[...]).astype(BF))
            ready[:, at] = rotated[i]
        scores = dot_nt(rotated[0], rotated[1]) * HD**-0.5
        scores = jnp.where(allowed, scores, -1e30)
        peak = jnp.max(scores, axis=1, keepdims=True)
        powers = jnp.exp(scores - peak)
        total = peak + jnp.log(jnp.sum(powers, axis=1, keepdims=True))
        weights = jnp.exp(scores - total).astype(BF)
        here = slice(h * HD, (h + 1) * HD)
        mixed[:, here] = dot(weights, ready[:, 2 * part + h * HD : 2 * part + (h + 1) * HD]).astype(BF)
        totals[...] = jnp.where(lane == h, total, totals[...])
        tops[0] = jnp.where(top_lane == h, jnp.max(peak, axis=0, keepdims=True), tops[0])


def attend(normed, weight, segments, cosine, sine, gains, heads):
    count, length = segments.shape
    rows, width = normed.shape
    part = heads * HD
    one = lambda n: (n, 0)
    fixed = lambda n: (0, 0)
    return pl.pallas_call(
        functools.partial(attend_kernel, heads),
        grid=(count,),
        in_specs=[
            pl.BlockSpec((length, width), one),
            pl.BlockSpec((width, 3 * part), fixed, pipeline_mode=pl.Buffered(1)),
            pl.BlockSpec((1, 1, length), lambda n: (n, 0, 0)),
            pl.BlockSpec((1, length, 1), lambda n: (n, 0, 0)),
            pl.BlockSpec((length, HD), fixed),
            pl.BlockSpec((length, HD), fixed),
            pl.BlockSpec((2, HD), fixed),
        ],
        out_specs=[
            pl.BlockSpec((length, 2 * part), one),
            pl.BlockSpec((length, 3 * part), one),
            pl.BlockSpec((length, part), one),
            pl.BlockSpec((length, 128), one),
            pl.BlockSpec((1, 1, 128), lambda n: (n, 0, 0)),
        ],
        out_shape=[
            jax.ShapeDtypeStruct((rows, 2 * part), F32),
            jax.ShapeDtypeStruct((rows, 3 * part), BF),
            jax.ShapeDtypeStruct((rows, part), BF),
            jax.ShapeDtypeStruct((rows, 128), F32),
            jax.ShapeDtypeStruct((count, 1, 128), F32),
        ],
        compiler_params=pltpu.CompilerParams(vmem_limit_bytes=60 * 2**20),
        cost_estimate=pl.CostEstimate(flops=0, bytes_accessed=0, transcendentals=0),
        name="attention",
    )(normed, weight, segments[:, None, :], segments[:, :, None], cosine, sine, gains)


def attend_back_kernel(heads, pull, raw, ready, totals, seg_row, seg_col, cosine, sine, gains, grad, gain_grads):
    allowed = seg_col[0] == seg_row[0]
    lane = lax.broadcasted_iota(jnp.int32, totals.shape, 1)
    part = heads * HD
    sums = [jnp.zeros((1, HD), F32)] * 2
    for h in range(heads):
        at = [slice(i * part + h * HD, i * part + (h + 1) * HD) for i in range(3)]
        query, key, value = (ready[:, a] for a in at)
        pulled = pull[:, h * HD : (h + 1) * HD]
        total = jnp.sum(jnp.where(lane == h, totals[...], 0.0), axis=1, keepdims=True)
        scores = dot_nt(query, key) * HD**-0.5
        probs = jnp.where(allowed, jnp.exp(jnp.where(allowed, scores - total, 0.0)), 0.0)
        grad_weights = dot_nt(pulled, value)
        grad[:, at[2]] = dot_tn(probs.astype(BF), pulled).astype(BF)
        inner = jnp.sum(probs * grad_weights, axis=1, keepdims=True)
        grad_scores = (probs * (grad_weights - inner)).astype(BF)
        both = (dot(grad_scores, key), dot_tn(grad_scores, query))
        for i, g in enumerate(both):
            g = g * HD**-0.5
            back = g * cosine[...] - pltpu.roll(g, HD // 2, 1) * sine[...]
            head = raw[:, at[i]]
            norm = lax.rsqrt(jnp.mean(head * head, axis=1, keepdims=True) + epsilon)
            sums[i] = sums[i] + jnp.sum(back * head * norm, axis=0, keepdims=True)
            scaled = back * gains[i : i + 1]
            mean = jnp.mean(scaled * head, axis=1, keepdims=True)
            grad[:, at[i]] = (norm * scaled - head * (norm * norm * norm * mean)).astype(BF)
    for i in range(2):
        gain_grads[0, i : i + 1] = sums[i]


def attend_back(pull, raw, ready, totals, segments, cosine, sine, gains, heads):
    count, length = segments.shape
    rows = raw.shape[0]
    part = heads * HD
    one = lambda n: (n, 0)
    fixed = lambda n: (0, 0)
    return pl.pallas_call(
        functools.partial(attend_back_kernel, heads),
        grid=(count,),
        in_specs=[
            pl.BlockSpec((length, part), one),
            pl.BlockSpec((length, 2 * part), one),
            pl.BlockSpec((length, 3 * part), one),
            pl.BlockSpec((length, 128), one),
            pl.BlockSpec((1, 1, length), lambda n: (n, 0, 0)),
            pl.BlockSpec((1, length, 1), lambda n: (n, 0, 0)),
            pl.BlockSpec((length, HD), fixed),
            pl.BlockSpec((length, HD), fixed),
            pl.BlockSpec((2, HD), fixed),
        ],
        out_specs=[
            pl.BlockSpec((length, 3 * part), one),
            pl.BlockSpec((1, 2, HD), lambda n: (n, 0, 0)),
        ],
        out_shape=[
            jax.ShapeDtypeStruct((rows, 3 * part), BF),
            jax.ShapeDtypeStruct((count, 2, HD), F32),
        ],
        compiler_params=pltpu.CompilerParams(vmem_limit_bytes=32 * 2**20),
        cost_estimate=pl.CostEstimate(
            flops=0, bytes_accessed=0, transcendentals=0
        ),
        name="attention_grad",
    )(pull, raw, ready, totals, segments[:, None, :], segments[:, :, None], cosine, sine, gains)


def weight_grad_kernel(half, quarters, left, right, *outs):
    j, i = pl.program_id(0), pl.program_id(1)
    block = dot_tn(left[0], right[0]).astype(BF)
    for at, out in enumerate(outs):

        @pl.when((j == at // 2) & ((i >= half) == (at % 2 == 1)))
        def _(out=out):
            out[0] = block


def weight_grads(quarters, left, right, parts, cost):
    count, rows, width = left.shape
    size, n = width // parts, right.shape[2]
    half = parts // 2

    def spot(at):
        def index(j, i, quarters):
            step = j * parts + i - (at // 2 * parts + at % 2 * half)
            return (jnp.clip(step, 0, half - 1), 0, 0)

        return index

    return pl.pallas_call(
        functools.partial(weight_grad_kernel, half),
        grid_spec=pltpu.PrefetchScalarGridSpec(
            num_scalar_prefetch=1,
            grid=(count, parts),
            in_specs=[
                pl.BlockSpec((1, rows, size), lambda j, i, quarters: (j, 0, quarters[j, i])),
                pl.BlockSpec((1, rows, n), lambda j, i, quarters: (j, 0, 0)),
            ],
            out_specs=[pl.BlockSpec((1, size, n), spot(at)) for at in range(2 * count)],
        ),
        out_shape=[jax.ShapeDtypeStruct((half, size, n), BF)] * (2 * count),
        compiler_params=pltpu.CompilerParams(vmem_limit_bytes=56 * 2**20),
        cost_estimate=pl.CostEstimate(flops=cost, bytes_accessed=0, transcendentals=0),
        name="weight_grads",
    )(quarters, left, right)


def product_kernel(left, right, out):
    out[...] = dot_tn(left[...], right[...]).astype(BF)


def product(left, right):
    rows, width = left.shape
    n = right.shape[1]
    size = min(width, 256)
    return pl.pallas_call(
        product_kernel,
        grid=(width // size,),
        in_specs=[
            pl.BlockSpec((rows, size), lambda i: (0, i)),
            pl.BlockSpec((rows, n), lambda i: (0, 0)),
        ],
        out_specs=pl.BlockSpec((size, n), lambda i: (i, 0)),
        out_shape=jax.ShapeDtypeStruct((width, n), BF),
        compiler_params=pltpu.CompilerParams(vmem_limit_bytes=32 * 2**20),
        cost_estimate=pl.CostEstimate(flops=0, bytes_accessed=0, transcendentals=0),
        name="product",
    )(left, right)


def spread_kernel(grad, weight, *outs):
    block = dot_nt(grad[...], weight[...]).astype(BF)
    for at, out in enumerate(outs):

        @pl.when(pl.program_id(0) == at)
        def _(out=out):
            out[...] = block


def normed_grads(grad, weight, count):
    rows, n = grad.shape
    width = weight.shape[0]
    length = rows // count
    return pl.pallas_call(
        spread_kernel,
        grid=(count,),
        in_specs=[
            pl.BlockSpec((length, n), lambda i: (i, 0)),
            pl.BlockSpec((width, n), lambda i: (0, 0), pipeline_mode=pl.Buffered(1)),
        ],
        out_specs=[pl.BlockSpec((length, width), lambda i: (0, 0))] * count,
        out_shape=[jax.ShapeDtypeStruct((length, width), BF)] * count,
        compiler_params=pltpu.CompilerParams(vmem_limit_bytes=48 * 2**20),
        cost_estimate=pl.CostEstimate(flops=0, bytes_accessed=0, transcendentals=0),
        name="normed_grads",
    )(grad, weight)


def halve_kernel(half, blocks, keep, got, send_out, keep_out):
    block = (keep[0].astype(F32) + got[0].astype(F32)).astype(BF)

    @pl.when(pl.program_id(0) < half)
    def _():
        send_out[0] = block

    @pl.when(pl.program_id(0) >= half)
    def _():
        keep_out[0] = block


def halve(blocks, keep, got, cost):
    count, size, n = keep.shape
    half = count // 2
    here = pl.BlockSpec((1, size, n), lambda i, blocks: (blocks[i], 0, 0))
    return pl.pallas_call(
        functools.partial(halve_kernel, half),
        grid_spec=pltpu.PrefetchScalarGridSpec(
            num_scalar_prefetch=1,
            grid=(count,),
            in_specs=[here, here],
            out_specs=[
                pl.BlockSpec((1, size, n), lambda i, blocks: (jnp.minimum(i, half - 1), 0, 0)),
                pl.BlockSpec((1, size, n), lambda i, blocks: (jnp.maximum(i - half, 0), 0, 0)),
            ],
        ),
        out_shape=[jax.ShapeDtypeStruct((half, size, n), BF)] * 2,
        compiler_params=pltpu.CompilerParams(vmem_limit_bytes=32 * 2**20),
        cost_estimate=pl.CostEstimate(flops=cost, bytes_accessed=0, transcendentals=0),
        name="halve",
    )(blocks, keep, got)


def join_kernel(*refs):
    out = refs[-1]
    for j in range((len(refs) - 1) // 2):

        @pl.when(pl.program_id(0) == j)
        def _(j=j):
            out[0] = refs[2 * j][...].astype(F32) + refs[2 * j + 1][...].astype(F32)


def join(pairs, cost):
    size, n = pairs[0][0].shape
    step = min(size, 256)
    count = len(pairs)

    def spot(at):
        def index(j, i):
            k = j * (size // step) + i - at * (size // step)
            return (jnp.clip(k, 0, size // step - 1), 0)

        return index

    return pl.pallas_call(
        join_kernel,
        grid=(count, size // step),
        in_specs=[pl.BlockSpec((step, n), spot(at // 2)) for at in range(2 * count)],
        out_specs=pl.BlockSpec((1, step, n), lambda j, i: (j, i, 0)),
        out_shape=jax.ShapeDtypeStruct((count, size, n), F32),
        compiler_params=pltpu.CompilerParams(vmem_limit_bytes=60 * 2**20),
        cost_estimate=pl.CostEstimate(flops=cost, bytes_accessed=0, transcendentals=0),
        name="join",
    )(*[v for pair in pairs for v in pair])


def input_kernel(count, heads, who, *refs):
    pieces = refs[:count]
    tokens, gain, grad_hidden, ffn, gains, tops, grad, small = refs[count:]
    width = tokens.shape[1]
    pulled = pieces[0][...].astype(F32)
    for piece in pieces[1:]:
        pulled = pulled + piece[...].astype(F32)
    value = tokens[...].astype(F32)
    scale = lax.rsqrt(jnp.mean(value * value, axis=1, keepdims=True) + epsilon)
    small[:, :width] = jnp.sum(pulled * value * scale, axis=0, keepdims=True)
    small[:, width : 2 * width] = ffn[...]
    for i in range(2):
        at = 2 * width + i * HD
        small[:, at : at + HD] = jnp.sum(gains[:, i], axis=0, keepdims=True)
    top = jnp.max(tops[:, 0], axis=0, keepdims=True)
    lane = lax.broadcasted_iota(jnp.int32, top.shape, 1)
    top = jnp.where(lane < heads, top, -3e38)
    small[:, 2 * width + 2 * HD :] = pltpu.roll(top, who[0] * heads, 1)
    pulled = pulled * gain[...]
    inner = jnp.mean(pulled * value, axis=1, keepdims=True)
    back = scale * pulled - value * (scale * scale * scale * inner)
    grad[...] = (grad_hidden[...] + back).astype(BF)


def input_step(who, pieces, tokens, gain, grad_hidden, ffn, gains, tops, heads):
    length, width = tokens.shape
    vmem = pl.BlockSpec(memory_space=pltpu.VMEM)
    return pl.pallas_call(
        functools.partial(input_kernel, len(pieces), heads),
        in_specs=[pl.BlockSpec(memory_space=pltpu.SMEM)] + [vmem] * (len(pieces) + 6),
        out_specs=[vmem] * 2,
        out_shape=[
            jax.ShapeDtypeStruct((length, width), BF),
            jax.ShapeDtypeStruct((1, 2 * width + 2 * HD + 128), F32),
        ],
        compiler_params=pltpu.CompilerParams(vmem_limit_bytes=60 * 2**20),
        cost_estimate=pl.CostEstimate(flops=10**11, bytes_accessed=0, transcendentals=0),
        name="input_grad",
    )(who, *pieces, tokens, gain, grad_hidden, ffn, gains, tops)


def gather_kernel(count, arrays, who, *refs):
    blocks, outs = refs[:count], refs[count:]
    part = outs[0].shape[1] // count
    total = 0.0
    for k, block in enumerate(blocks):
        here = pl.ds(pl.multiple_of((who[0] ^ k) * part, part), part)
        for i in range(arrays):
            outs[i][:, here] = block[:, i * part : (i + 1) * part].astype(F32)
        if len(outs) > arrays:
            total += block[:, arrays * part :].astype(F32)
    if len(outs) > arrays:
        outs[-1][...] = total


def gather_step(who, blocks, arrays):
    rows, wide = blocks[0].shape
    lanes = 128 if wide % (arrays * 256) else 0
    part = (wide - lanes) // arrays
    count = len(blocks)
    step = rows // 4

    def spec(n):
        return pl.BlockSpec((step, n), lambda i: (i, 0))

    return pl.pallas_call(
        functools.partial(gather_kernel, count, arrays),
        grid=(rows // step,),
        in_specs=[pl.BlockSpec(memory_space=pltpu.SMEM)] + [spec(wide)] * count,
        out_specs=[spec(part * count)] * arrays + [spec(lanes)] * (lanes > 0),
        out_shape=[jax.ShapeDtypeStruct((rows, part * count), F32)] * arrays
        + [jax.ShapeDtypeStruct((rows, lanes), F32)] * (lanes > 0),
        compiler_params=pltpu.CompilerParams(vmem_limit_bytes=48 * 2**20),
        cost_estimate=pl.CostEstimate(flops=0, bytes_accessed=0, transcendentals=0),
        name="gather_columns",
    )(who, *blocks)


def merge_kernel(sums, *refs):
    out = refs[-1]
    total = refs[0][...]
    lane = lax.broadcasted_iota(jnp.int32, total.shape, 1)
    for ref in refs[1:-1]:
        other = ref[...]
        total = jnp.where(lane < sums, total + other, jnp.maximum(total, other))
    out[...] = total


def merge(sums, *values):
    vmem = pl.BlockSpec(memory_space=pltpu.VMEM)
    return pl.pallas_call(
        functools.partial(merge_kernel, sums),
        in_specs=[vmem] * len(values),
        out_specs=vmem,
        out_shape=jax.ShapeDtypeStruct(values[0].shape, F32),
        cost_estimate=pl.CostEstimate(flops=0, bytes_accessed=0, transcendentals=0),
        name="merge",
    )(*values)


def local(
    tokens,
    cotangent,
    segment_ids,
    expert_index,
    clip_threshold,
    attn_norm_gain,
    w_query,
    w_key,
    w_value,
    w_output,
    query_gain,
    key_gain,
    ffn_norm_gain,
    router,
    expert_in,
    expert_out,
):
    replicas = lax.axis_size("replica")
    groups = lax.axis_size("fsdp")
    me_r = lax.axis_index("replica")
    me_f = lax.axis_index("fsdp")
    core = me_f % 2
    length, width = tokens.shape
    part = width // replicas
    heads = part // HD
    ff = expert_out.shape[1]
    local_experts = expert_in.shape[0]
    scale = HD ** (-0.5)
    attn_gain = attn_norm_gain.astype(F32)
    ffn_gain = ffn_norm_gain.astype(F32)
    gain_query = query_gain.astype(F32)
    gain_key = key_gain.astype(F32)

    def swap(value, k):
        return lax.ppermute(value, "replica", [(r, r ^ k) for r in range(replicas)])

    def columns(value, k, axis=1):
        return lax.dynamic_slice_in_dim(value, (me_r ^ k) * part, part, axis)

    def spread(value):
        return [value] + [swap(value, k) for k in range(1, replicas)]

    def trade_columns(value):
        return [columns(value, 0)] + [swap(columns(value, k), k) for k in range(1, replicas)]

    def join_columns(blocks):
        out = jnp.zeros((blocks[0].shape[0], part * replicas), blocks[0].dtype)
        for k, block in enumerate(blocks):
            out = lax.dynamic_update_slice_in_dim(out, block, (me_r ^ k) * part, 1)
        return out

    def cross(value, k):
        return lax.ppermute(value, "fsdp", [(f, f ^ k) for f in range(groups)])

    def pass_on(up, down, hop):
        chips = groups // 2
        pairs = [(2 * a + i, 2 * a + 2 + i) for a in range(hop - 1, chips - 1) for i in (0, 1)]
        back = [(2 * a + 2 + i, 2 * a + i) for a in range(chips - hop) for i in (0, 1)]
        return lax.ppermute(up, "fsdp", pairs), lax.ppermute(down, "fsdp", back)

    def choose(up, down, k):
        chips = groups // 2
        found = {}
        for a in range(chips):
            b = a ^ k
            found.setdefault((b > a, abs(b - a)), []).append(a)
        picked = None
        for (above, hop), at in found.items():
            source = down[hop] if above else up[hop]
            if picked is None:
                picked = source
            else:
                here = functools.reduce(jnp.logical_or, [me_f // 2 == a for a in at])
                picked = jnp.where(here, source, picked)
        return picked

    def gather(value):
        return lax.all_gather(value, "fsdp", axis=0, tiled=True)

    def reduce(value):
        return lax.psum_scatter(value, "fsdp", scatter_dimension=0, tiled=True)

    bits = replicas.bit_length() - 1

    def next_bit(j, step):
        return 1 << (bits - 1 - step if j % 2 else step)

    def next_halves(traded, j, step, cost=0):
        keep, got = traded
        left = keep.shape[0]
        place = jnp.arange(left, dtype=jnp.int32)
        here = left // 2 if j % 2 else 1
        mine = (me_r & next_bit(j, step)) != 0
        other = ((place & here) != 0) != mine
        spots = jnp.where(other, jnp.cumsum(other) - 1, left // 2 + jnp.cumsum(~other) - 1)
        return halve(jnp.zeros((left,), jnp.int32).at[spots].set(place), keep, got, cost)

    index_table = expert_index.astype(BF).reshape(w_query.shape[0], -1)
    sent = [columns(w_output, 0), router, index_table]
    sizes = [v.shape[1] for v in sent]
    sent.append(jnp.zeros((w_query.shape[0], -sum(sizes) % 128), BF))
    quarter = gather(jnp.concatenate(sent, axis=1))
    full_router = quarter[:, part : part + EXPERTS]
    full_index = quarter[:, part + EXPERTS : part + EXPERTS + sizes[2]].astype(jnp.int32)
    full_index = full_index.reshape(groups * length, -1)
    ids = jnp.arange(EXPERTS, dtype=jnp.int32)
    mask = jnp.any(full_index[:, :, None] == ids, axis=1).reshape(groups, length, EXPERTS)
    first = me_f * local_experts
    hot = lax.dynamic_slice_in_dim(mask, first, local_experts, 2)
    order = jnp.arange(length, dtype=jnp.int32)
    before = (order[:, None] < order[None, :]).astype(BF)
    rank = jnp.einsum("nsj,st->njt", hot.astype(BF), before, preferred_element_type=F32)
    rank = jnp.where(hot.transpose(0, 2, 1), rank.astype(jnp.int32), -1)
    slots = jnp.arange(CAP, dtype=jnp.int32)
    pick = (rank[:, :, None, :] == slots[:, None]).astype(BF)
    spots = (rank[:, :, :, None] == slots).astype(BF)
    lanes = 128
    mask_wide = jnp.pad(mask.astype(F32), ((0, 0), (0, 0), (0, lanes - EXPERTS)))
    router_wide = jnp.pad(full_router, ((0, 0), (0, lanes - EXPERTS)))
    tables = (pick, spots, mask_wide, router_wide)
    segments = spread(segment_ids)
    tokens_all = spread(after(tokens, *segments[1:]))
    segments = jnp.concatenate(segments, axis=0)
    normed = jnp.concatenate(
        [rms_norm(v.astype(F32), attn_gain).astype(BF) for v in tokens_all], axis=0
    )
    rounds = groups // 2
    where = jnp.stack([me_r, me_f // 2, core]).astype(jnp.int32)
    half = lax.dynamic_slice(quarter, (core * (width // 2), 0), (width // 2, part))
    near = spread(after(half, *tokens_all[1:]))
    near[1] = after(near[1], *tables, segments, normed)
    normed = after(normed, *near[1:])
    w_qkv = gather(jnp.concatenate([columns(w, 0) for w in (w_query, w_key, w_value)], axis=1))
    cot_all = gather(cotangent)
    cot_pair = (cotangent, cross(cotangent, 1))

    cosine, sine = rope_tables(length, HD)
    cosine = jnp.concatenate([cosine, cosine], axis=1)
    sine = jnp.concatenate([-sine, sine], axis=1)
    gains = jnp.stack([gain_query, gain_key])
    raw, ready, mixed_heads, totals, tops = attend(normed, w_qkv, segments, cosine, sine, gains, heads
    )
    near = jnp.stack([after(near[0], raw), *near[1:]])
    far = cross(near, 1)
    mixed_heads = mixed_heads.reshape(replicas, length, part)
    pieces = [mixed_heads[0]] + [swap(mixed_heads[k], k) for k in range(1, replicas)]
    inputs = tokens.astype(F32)
    hidden, normed_ffn, mixed = out_step(where, pieces, near, far, tokens, ffn_gain[None, :])
    mixed_all = spread(mixed)

    def first_bit(j):
        return 1 << (bits - 1 if j % 2 else 0)

    numbers = jnp.arange(replicas, dtype=jnp.int32)
    quarters = []
    for j in range(local_experts):
        other = ((numbers ^ me_r) & first_bit(j)) != 0
        place = jnp.where(other, jnp.cumsum(other) - 1, replicas // 2 + jnp.cumsum(~other) - 1)
        quarters.append(jnp.zeros((replicas,), jnp.int32).at[place].set(numbers))
    quarters = jnp.stack(quarters)
    kept = None
    shares = []
    added = []
    pending = []
    up, down = [normed_ffn], [normed_ffn]
    for k in range(rounds):
        chip = (me_f // 2) ^ k
        who = jnp.stack([2 * chip + core, 2 * chip + 1 - core, chip, core, first])
        if k + 1 < rounds:
            next_up, next_down = pass_on(up[-1], down[-1], k + 1)
        mine = choose(up, down, k) if k else normed_ffn
        nf = (mine, cross(mine, 1))
        kept, back_a, back_b = expert_block(k, rounds, who, nf, (cot_all,) if k else cot_pair, pick, spots, mask_wide, router_wide, expert_in, expert_out, kept, pending
        )
        if k + 1 < rounds:
            up.append(after(next_up, back_a))
            down.append(after(next_down, back_a))
        else:
            rows, grad_projected, cot_rows, scaled, moe = kept
            out_blocks = weight_grads(quarters, after(scaled, mixed_all[-1]), cot_rows, replicas, 0)
        if k == rounds - 1:
            back_b = after(back_b, *out_blocks, *shares[1:])
        share = (back_a.astype(F32) + cross(back_b, 1).astype(F32)).astype(BF)
        added.append(share)
        if k == rounds - 2:
            pending = added[1:]
        else:
            pending = mixed_all[1:-1] if k == rounds - 3 else []
        shares.append(share if k == 0 else cross(share, 2 * k))
    out_traded = [
        (out_blocks[2 * j + 1], swap(out_blocks[2 * j], first_bit(j))) for j in range(local_experts)
    ]
    in_blocks = weight_grads(quarters, after(rows, share), grad_projected, replicas, 10**11)
    shares[-1] = after(shares[-1], *in_blocks, *[v[1] for v in out_traded])
    moe_sum = reduce(after(moe, shares[-1]))
    output = (hidden + moe_sum.astype(F32)).astype(BF)

    my_mask = lax.dynamic_index_in_dim(mask_wide, me_f, 0, keepdims=False) > 0.0
    logits = jnp.where(my_mask, dot(normed_ffn, router_wide), -jnp.inf)
    powers = jnp.exp(logits - jnp.max(logits, axis=1, keepdims=True))
    my_gates = powers / jnp.sum(powers, axis=1, keepdims=True)
    grad_hidden, ffn_gain_grad, router_grad, pieces = back_step(
        where, shares, hidden, normed_ffn, cotangent, ffn_gain[None, :], my_gates, router_wide, near, far, EXPERTS
    )
    grad_mixed = jnp.concatenate(
        [pieces[0]] + [swap(pieces[k], k) for k in range(1, replicas)], axis=0
    )
    sends = [
        after(in_blocks[2 * j], grad_mixed, *[v[1] for v in out_traded]) for j in range(local_experts)
    ]
    in_traded = [
        (in_blocks[2 * j + 1], swap(v, first_bit(j))) for j, v in enumerate(sends)
    ]
    ready = after(ready, *sends)
    grad_qkv, gain_grads = attend_back(grad_mixed, raw, ready, totals, segments, cosine, sine, gains, heads
    )
    qkv_grad = product(normed, grad_qkv)
    part_normed = normed_grads(grad_qkv, w_qkv, replicas)
    received = [v[1] for v in in_traded]
    received[0] = after(received[0], *received[1:], moe_sum)
    in_traded = [(v[0], got) for v, got in zip(in_traded, received)]
    in_halves = [next_halves(v, j, 1, 10**11) for j, v in enumerate(in_traded)]
    in_sends = [v for v, _ in in_halves]
    in_done = [(keep, swap(v, next_bit(j, 1))) for j, (v, keep) in enumerate(in_halves)]
    mixed_rows = jnp.concatenate([mixed_all[0], after(mixed_all[1], *in_sends), *mixed_all[2:]], axis=0)
    output_grad = dot_tn(mixed_rows, grad_mixed[:, part:])
    o_grad = jnp.concatenate([output_grad.astype(BF), router_grad], axis=1)
    share_o = reduce(o_grad)
    out_halves = [next_halves((k, after(v, part_normed[0])), j, 1) for j, (k, v) in enumerate(out_traded)]
    pieces = [after(part_normed[0], *in_sends, o_grad, *[v for v, _ in out_halves])]
    pieces += [swap(part_normed[k], k) for k in range(1, replicas)]
    input_grad, small = input_step(
        where, pieces, tokens, attn_gain[None, :], grad_hidden, ffn_gain_grad, gain_grads, tops, heads
    )
    second = [v[1] for v in in_done]
    share_qkv = reduce(qkv_grad)
    payload = after(jnp.concatenate([share_qkv, share_o], axis=1), *second, input_grad)
    if replicas == 4:
        across, along = swap(payload, 1), swap(payload, 2)
        cut_at = payload.shape[0] // 2
        upper = swap(across[:cut_at], 2)
        lower = swap(along[cut_at:], 1)
        blocks = [payload, across, along, jnp.concatenate([upper, lower], axis=0)]
    else:
        blocks = spread(payload)
    out_done = [
        (keep, swap(after(v, *second, moe_sum), next_bit(j, 1))) for j, (v, keep) in enumerate(out_halves)
    ]

    def settle(traded, cost):
        pairs = []
        for j, (keep, got) in enumerate(traded):
            for step in range(2, bits):
                send, keep = next_halves((keep, got), j, step)
                got = swap(send, next_bit(j, step))
            pairs.append((keep[0], got[0]))
        return join(pairs, cost)

    n_sums = 2 * width + 2 * HD
    small = merge(n_sums, small, cross(small, 1))
    small = merge(n_sums, small, *[cross(small, 2 * k) for k in range(1, rounds)])
    small = merge(n_sums, *spread(after(small, *second)))
    small = small[0]
    attn_gain_total = small[:width]
    ffn_gain_total = small[width : 2 * width]
    query_gain_total = small[2 * width : 2 * width + HD]
    key_gain_total = small[2 * width + HD : n_sums]
    head_max = small[n_sums : n_sums + replicas * heads]
    threshold = clip_threshold.astype(F32)
    factor = threshold / jnp.maximum(head_max, threshold)
    column_scale = jnp.repeat(jnp.sqrt(factor), HD)
    clipped_query = (w_query.astype(F32) * column_scale[None, :]).astype(BF)
    clipped_key = (w_key.astype(F32) * column_scale[None, :]).astype(BF)
    expert_in_grad = settle(
        [(keep, after(v, clipped_query, clipped_key, output)) for keep, v in in_done], 10**11
    )
    expert_out_grad = settle([(k, after(v, expert_in_grad)) for k, v in out_done], 0)

    blocks[1] = after(blocks[1], expert_in_grad)
    total_query, total_key, total_value, total_output, total_router = gather_step(where, blocks, 4)
    total_router = total_router[:, :EXPERTS]
    return (
        output,
        input_grad,
        attn_gain_total,
        total_query,
        total_key,
        total_value,
        total_output,
        query_gain_total,
        key_gain_total,
        ffn_gain_total,
        total_router,
        expert_in_grad,
        expert_out_grad,
        head_max,
        clipped_query,
        clipped_key,
    )


def solution(mesh):
    both = ("replica", "fsdp")
    return jax.shard_map(
        local,
        mesh=mesh,
        in_specs=(
            P(both, None),
            P(both, None),
            P(both, None),
            P(both, None),
            P(),
            P(),
            P("fsdp", None),
            P("fsdp", None),
            P("fsdp", None),
            P("fsdp", None),
            P(),
            P(),
            P(),
            P("fsdp", None),
            P("fsdp", None, None),
            P("fsdp", None, None),
        ),
        out_specs=(
            P(both, None),
            P(both, None),
            P(),
            P("fsdp", None),
            P("fsdp", None),
            P("fsdp", None),
            P("fsdp", None),
            P(),
            P(),
            P(),
            P("fsdp", None),
            P("fsdp", "replica", None),
            P("fsdp", "replica", None),
            P(),
            P("fsdp", None),
            P("fsdp", None),
        ),
        check_vma=False,
    )
```
